512 devices in a mesh: clip: 2 (over core), seq: 16 (over z_hi, x), mp: 16 (over z_lo, y).
Axes of the slice: x: 4, y: 8, z: 8 (z_hi: 4, z_lo: 2; z = z_hi * 2 + z_lo), core: 2. Of those that a mesh axis runs over, the one named last changes fastest.
Arguments:
- frames_in: bfloat16 [32, 256, 2048], P(('clip', 'seq'), None, 'mp'), parts along dimension 0, may hold values from -6 to 6
- norm_gain: bfloat16 [2048], replicated, may hold values from 0.5 to 1.5
- w_qkv: bfloat16 [2048, 6144], P(None, 'mp'), may hold values from -4 to 4
- w_out: bfloat16 [2048, 2048], P('mp'), may hold values from -0.125 to 0.125
- cotangent: bfloat16 [32, 256, 2048], P(('clip', 'seq'), None, 'mp'), parts along dimension 0, may hold values from -6 to 6
Outputs:
- layer_out: bfloat16 [32, 256, 2048], P(('clip', 'seq'), None, 'mp'), parts along dimension 0
- input_grad: bfloat16 [32, 256, 2048], P(('clip', 'seq'), None, 'mp'), parts along dimension 0
- qkv_weight_grad: bfloat16 [4096, 6144], P('clip', 'mp'), parts along dimension 0
- out_weight_grad: bfloat16 [4096, 2048], P(('clip', 'mp'), 'seq'), parts along dimension 0
The draws below stay inside these ranges and needn't reach their ends.
There are 2 independent parts, one for each index of `clip`. The reference program is written for one: setup_inputs(seed, part) draws one part's arguments, and reference() takes and returns one part's arrays. A program takes and returns all parts, laid end to end along the dimension named above; an argument that names none is the same for every part. Nothing has to cross between parts.
All inputs are finite; a program needn't handle non-finite values.
Results may differ from the reference program's by a relative error of at most 0.028.
The reference program's roundings to bfloat16 on the way (of `normed`, `projected`, `probs`, `attended`, `grad_heads` and `grad_qkv`) count: a program that leaves them out, or rounds other values in their place, can miss the bound.
Values may be sent and summed in bfloat16 or wider, within the bound.
A program may use at most 64 MiB of HBM per device.

```python
import jax
import jax.numpy as jnp
from jax import lax

D = 2048
HEADS = 16
HEAD = 128
P_SIZE = 256
FRAMES = 16
HEADS_DEV = 1
N_MP = 16


def draw_w_qkv(key, part):
    key = jax.random.fold_in(key, 11)
    shape = (D, 3 * D)
    base = jax.random.truncated_normal(key, -3.0, 3.0, shape, jnp.float32)
    return (base * D ** (-0.5)).astype(jnp.bfloat16)


def level_of(own_key, extent, cuts, low, top_value):
    level, own = 1.0, jax.random.fold_in(own_key, 6)
    for axis_at, blocks in cuts:
        heights = jnp.exp(jax.random.uniform(jax.random.fold_in(own, axis_at), (blocks,), jnp.float32, low / len(cuts), top_value / len(cuts)))
        level = level * jnp.repeat(heights, extent[axis_at] // blocks).reshape([-1 if axis == axis_at else 1 for axis in range(len(extent))])
    return level


def scatter_about(rng, extent, width, limit, cuts=(), dtype=jnp.bfloat16):
    array = jax.random.normal(rng, extent, jnp.float32) * width
    if len(cuts) > 0:
        array = level_of(rng, extent, cuts, -0.22, 0.18) * array
    return jnp.clip(array, min=-limit, max=limit).astype(dtype)


def setup_inputs(seed: int = 0, part: int = 0) -> dict:
    splits = jax.random.split(jax.random.key(seed), 6)
    part_splits = jax.random.split(jax.random.fold_in(splits[5], part), 6)
    return {
        "frames_in": scatter_about(part_splits[0], (FRAMES, P_SIZE, D), 1.0, 6.0, ((0, 16), (2, 16))),
        "norm_gain": jnp.clip(1.0 + 0.1 * jax.random.normal(splits[1], (D,), jnp.float32), 0.5, 1.5).astype(jnp.bfloat16),
        "w_qkv": draw_w_qkv(jax.random.fold_in(splits[5], 71), part),
        "w_out": scatter_about(splits[3], (D, D), D ** -0.5, 0.125, ((0, 16),)),
        "cotangent": scatter_about(part_splits[4], (FRAMES, P_SIZE, D), 1.0, 6.0, ((0, 16), (2, 16))),
    }


EPS = 1e-05

def attend(queries, keys, values):
    scale = queries.shape[-1] ** (-0.5)
    scores = jnp.einsum('fphe,gphe->phfg', queries, keys, preferred_element_type=jnp.float32) * scale
    count = queries.shape[0]
    causal = jnp.arange(count)[:, None] >= jnp.arange(count)[None, :]
    scores = jnp.where(causal, scores, -1e+30)
    peak = lax.optimization_barrier(jnp.max(scores, axis=-1, keepdims=True))
    expo = jnp.exp(scores - peak)
    probs = (expo / lax.optimization_barrier(jnp.sum(expo, axis=-1, keepdims=True))).astype(jnp.bfloat16)
    return jnp.einsum('phfg,gphe->fphe', probs, values, preferred_element_type=jnp.float32)

def group_sum(left, right, group_width):
    total = jnp.zeros((left.shape[0], right.shape[1]), jnp.float32)
    for group in range(N_MP):
        lower = group * group_width
        term = jnp.dot(left[:, lower:lower + group_width], right[lower:lower + group_width], preferred_element_type=jnp.float32)
        term = lax.optimization_barrier(term.astype(jnp.bfloat16)).astype(jnp.float32)
        total = total + term
    return total

def reference(frames_in, norm_gain, w_qkv, w_out, cotangent):
    tokens = FRAMES * P_SIZE
    inputs = frames_in.astype(jnp.float32).reshape(tokens, D)
    gain = norm_gain.astype(jnp.float32)
    inv_rms = lax.rsqrt(lax.optimization_barrier(jnp.mean(inputs * inputs, axis=-1, keepdims=True)) + EPS)
    normed = (inputs * inv_rms * gain).astype(jnp.bfloat16)
    projected = jnp.dot(normed, w_qkv, preferred_element_type=jnp.float32).astype(jnp.bfloat16)
    split = projected.reshape(FRAMES, P_SIZE, HEADS, 3, HEAD)
    queries = split[:, :, :, 0]
    keys = split[:, :, :, 1]
    values = split[:, :, :, 2]
    attended = attend(queries, keys, values).astype(jnp.bfloat16).reshape(tokens, D)
    summed = group_sum(attended, w_out, HEADS_DEV * HEAD)
    layer_out = (inputs + summed).astype(jnp.bfloat16).reshape(FRAMES, P_SIZE, D)
    grad_rows = cotangent.reshape(tokens, D)
    out_weight_grad = jnp.dot(attended.T, grad_rows, preferred_element_type=jnp.float32).astype(jnp.bfloat16)
    grad_heads = jnp.dot(grad_rows, w_out.T, preferred_element_type=jnp.float32).astype(jnp.bfloat16)
    _, pull = jax.vjp(attend, queries, keys, values)
    grad_q, grad_k, grad_v = pull(grad_heads.reshape(FRAMES, P_SIZE, HEADS, HEAD).astype(jnp.float32))
    grad_qkv = jnp.stack([grad_q, grad_k, grad_v], axis=3).reshape(tokens, 3 * D)
    qkv_weight_grad = jnp.dot(normed.T, grad_qkv, preferred_element_type=jnp.float32).astype(jnp.bfloat16)
    normed_grad = group_sum(grad_qkv, w_qkv.T, HEADS_DEV * 3 * HEAD)
    row = lax.optimization_barrier(jnp.sum(gain * normed_grad * inputs, axis=-1, keepdims=True))
    input_grad = grad_rows.astype(jnp.float32) + inv_rms * gain * normed_grad - inputs * inv_rms ** 3 * row / D
    input_grad = input_grad.astype(jnp.bfloat16).reshape(FRAMES, P_SIZE, D)
    return (layer_out, input_grad, qkv_weight_grad, out_weight_grad)
```

```python
import jax
import jax.numpy as jnp
from jax import lax
from jax.experimental import pallas as pl
from jax.experimental.pallas import tpu as pltpu
from jax.sharding import PartitionSpec as P

HEAD = 128
EPS = 1e-05
BF = jnp.bfloat16
F32 = jnp.float32
MESH = pl.DeviceIdType.MESH
COPIES = 200
NT = (((1,), (1,)), ((), ()))


def mm(a, b):
    return jnp.dot(a, b, preferred_element_type=F32)


def mm_nt(a, b):
    return lax.dot_general(a, b, NT, preferred_element_type=F32)


def flat(block):
    return block.reshape(256, HEAD)


def kernel(
    x_hbm, gain_hbm, wqkv_hbm, wout_hbm, g_hbm,
    lo_hbm, ig_hbm, dwqkv_hbm, dwo_hbm,
    x_ref, g_ref, gain_ref, a1x, a1g, xb, gb, wqkv, wout, gain, inv, norm, norm_t, qkv, att, att_t,
    probs, probs_t, gheads, dqkv, term1, term2, rb1, rb2, zs1, zb1, zs2, zb2, rowb,
    wg, tx, px, mx, sx, rz, res, dwo, los, igs, b1l, b1i, lod, igd,
    ssem, rsem, lsem,
):
    clip, seq, mp = lax.axis_index("clip"), lax.axis_index("seq"), lax.axis_index("mp")
    zh, x = lax.div(seq, 4), lax.rem(seq, 4)
    zl, y = lax.div(mp, 8), lax.rem(mp, 8)
    e = 1 - 2 * clip
    zp = 1 - zl

    def x_at(step):
        return lax.rem(x + step + 4, 4)

    def z_at(step):
        return lax.rem(zh + step + 4, 4)

    def y_at(step):
        return lax.rem(y + step + 8, 8)

    def dev_x(to):
        return (clip, zh * 4 + to, mp)

    def dev_z(to):
        return (clip, to * 4 + x, mp)

    def dev_y(to):
        return (clip, seq, zl * 8 + to)

    dev_pair = (clip, seq, zp * 8 + y)

    loads = [
        pltpu.make_async_copy(src, dst, lsem.at[at])
        for at, (src, dst) in enumerate(
            [(x_hbm, x_ref), (g_hbm, g_ref), (gain_hbm, gain_ref), (wqkv_hbm, wqkv), (wout_hbm, wout)]
        )
    ]
    for load in loads:
        load.start()

    barrier = pltpu.get_barrier_semaphore()
    peers = [dev_x(x_at(s)) for s in (1, 2, 3)] + [dev_z(z_at(s)) for s in (1, 2, 3)]
    peers += [dev_y(y_at(1)), dev_y(y_at(-1)), dev_pair]
    for peer in peers:
        pl.semaphore_signal(barrier, inc=1, device_id=peer, device_id_type=MESH)
    pl.semaphore_wait(barrier, len(peers))

    started = []

    def send(src, dst, device):
        at = len(started)
        copy = pltpu.make_async_remote_copy(
            src_ref=src,
            dst_ref=dst,
            send_sem=ssem.at[at],
            recv_sem=rsem.at[at],
            device_id=device,
            device_id_type=MESH,
        )
        copy.start()
        started.append(copy)
        return copy

    stores = []

    def store(src, dst):
        stores.append(pltpu.make_async_copy(src, dst, lsem.at[len(loads) + len(stores)]))
        stores[-1].start()

    def frames_to_patches(src, mid, dst):
        sent = [send(src.at[:, x_at(s)], mid.at[x], dev_x(x_at(s))) for s in (1, 3, 2)]
        mid[x] = src[:, x]
        yield 2.0
        for copy in sent:
            copy.wait_recv()
        sent = [send(mid.at[:, z_at(s)], dst.at[mp, zh], dev_z(z_at(s))) for s in (1, 3, 2)]
        dst[mp, zh] = mid[:, zh]
        yield 2.0
        for copy in sent:
            copy.wait_recv()

    def patches_to_frames(src, mid, dst):
        sent = [send(src.at[z_at(s)], mid.at[zh], dev_z(z_at(s))) for s in (1, 3, 2)]
        mid[zh] = src[zh]
        yield 2.0
        for copy in sent:
            copy.wait_recv()
        sent = [send(mid.at[:, x_at(s)], dst.at[:, x], dev_x(x_at(s))) for s in (1, 3, 2)]
        dst[:, x] = mid[:, x]
        yield 2.0
        for copy in sent:
            copy.wait_recv()

    def gather(buf):
        def pass_on(block, device):
            return send(buf.at[block], buf.at[block], device)

        ahead, back = dev_y(y_at(e)), dev_y(y_at(-e))

        def own(step):
            return zl * 8 + y_at(step)

        def other(step):
            return zp * 8 + y_at(step)

        a = pass_on(mp, ahead)
        b = pass_on(mp, back)
        pair = [pass_on(mp, dev_pair)]
        yield 2.0
        a.wait_recv()
        a = pass_on(own(-e), ahead)
        yield 0.1
        b.wait_recv()
        b = pass_on(own(e), back)
        yield 0.5
        pair[0].wait_recv()
        c = pass_on(other(0), ahead)
        d = pass_on(other(0), back)
        yield 1.0
        a.wait_recv()
        a = pass_on(own(-2 * e), ahead)
        yield 0.1
        b.wait_recv()
        b = pass_on(own(2 * e), back)
        pair.append(pass_on(own(2 * e), dev_pair))
        yield 1.0
        c.wait_recv()
        c = pass_on(other(-e), ahead)
        yield 0.1
        d.wait_recv()
        yield 1.0
        a.wait_recv()
        a = pass_on(own(-3 * e), ahead)
        pair.append(pass_on(own(-3 * e), dev_pair))
        yield 0.1
        b.wait_recv()
        pair.append(pass_on(own(3 * e), dev_pair))
        yield 0.5
        c.wait_recv()
        yield 1.0
        a.wait_recv()
        pair.append(pass_on(own(-4 * e), dev_pair))
        for copy in pair[1:]:
            yield 0.5
            copy.wait_recv()

    def scatter_sum(term, rb, zs, zb):
        def slot(i, j, k):
            return i * 7 + j * 4 + k - 1

        planes = (zp, zl)
        ways = ((e, 4), (-e, 3))
        order = [(i, j) for i in (0, 1) for j in (0, 1)]
        sent = {}
        for i, j in order:
            way, steps = ways[j]
            dest = planes[i] * 8 + y_at(steps * way)
            sent[i, j] = send(term.at[dest], rb.at[slot(i, j, 1)], dev_y(y_at(way)))
        last = None
        for k in (1, 2, 3, 4):
            for i, j in order:
                way, steps = ways[j]
                if k > steps:
                    continue
                yield 2.2 if (i, j) == (0, 0) else 0.5
                sent[i, j].wait_recv()
                if k < steps:
                    dest = planes[i] * 8 + y_at((steps - k) * way)
                    here = rb.at[slot(i, j, k)]
                    here[...] = (here[...].astype(F32) + term[dest].astype(F32)).astype(BF)
                    sent[i, j] = send(here, rb.at[slot(i, j, k + 1)], dev_y(y_at(way)))
                elif k == 4 and i == 0:
                    zs[...] = (
                        term[zp * 8 + y].astype(F32)
                        + rb[slot(0, 0, 4)].astype(F32)
                        + rb[slot(0, 1, 3)].astype(F32)
                    ).astype(BF)
                    last = send(zs, zb, dev_pair)
        yield 2.0
        last.wait_recv()

    def summed(term, rb, zb):
        return (
            term[mp].astype(F32)
            + rb[7 + 3].astype(F32)
            + rb[7 + 4 + 2].astype(F32)
            + zb[...].astype(F32)
        )

    def weight_sum(c, gathered):
        xp, xm = x_at(e), x_at(-e)
        ahead, back = dev_x(xp), dev_x(xm)
        order = (2, 1, 3, 0)
        far = {}
        for r in order:
            far[r] = send(wg.at[c, z_at(r), x_at(2)], tx.at[c, z_at(r)], ahead)
        plain = send(wg.at[c, :, xm], px.at[c], back)
        near = {}
        for r in order:
            yield 3.0 if r == 2 else 0.7
            q = z_at(r)
            far[r].wait_recv()
            tx[c, q] = (tx[c, q].astype(F32) + wg[c, q, xp].astype(F32)).astype(BF)
            near[r] = send(tx.at[c, q], mx.at[c, q], ahead)
        across = []
        yield 1.0
        plain.wait_recv()
        for r in order[:3]:
            yield 0.7
            q = z_at(r)
            near[r].wait_recv()
            sx[c, q] = (
                wg[c, q, x].astype(F32) + px[c, q].astype(F32) + mx[c, q].astype(F32)
            ).astype(BF)
            across.append(send(sx.at[c, q], rz.at[c, r - 1], dev_z(q)))
        yield 0.7
        near[0].wait_recv()
        total = wg[c, zh, x].astype(F32) + px[c, zh].astype(F32) + mx[c, zh].astype(F32)
        yield 2.0
        for copy in across:
            copy.wait_recv()
        for r in range(3):
            total += rz[c, r].astype(F32)
        if not gathered:
            dwo[...] = total.astype(BF)
            store(dwo, dwo_hbm)
            return
        res[c, zh, x] = total.astype(BF)

        def pass_on(q, column, device):
            return send(res.at[c, q, column], res.at[c, q, column], device)

        zm = z_at(-e)
        up = pass_on(zh, x, dev_z(z_at(e)))
        down = pass_on(zh, x, dev_z(zm))
        first, second = [pass_on(zh, x, ahead)], [pass_on(zh, x, back)]
        third = []
        yield 2.5
        up.wait_recv()
        up = pass_on(zm, x, dev_z(z_at(e)))
        first.append(pass_on(zm, x, ahead))
        second.append(pass_on(zm, x, back))
        yield 0.2
        down.wait_recv()
        first.append(pass_on(z_at(e), x, ahead))
        second.append(pass_on(z_at(e), x, back))
        yield 0.3
        first[0].wait_recv()
        third.append(pass_on(zh, xm, ahead))
        yield 2.0
        up.wait_recv()
        first.append(pass_on(z_at(2), x, ahead))
        second.append(pass_on(z_at(2), x, back))
        for at, q in ((1, zm), (2, z_at(e)), (3, z_at(2))):
            yield 0.7
            first[at].wait_recv()
            third.append(pass_on(q, xm, ahead))
        yield 2.5
        for copy in second + third:
            copy.wait_recv()
        store(res.at[c], dwqkv_hbm.at[:, :, :, pl.ds(c * 128, 128)])

    flows = []
    clock = [0.0]

    def start(flow):
        flows.append([clock[0] + next(flow), flow])
        return flow

    def step(item):
        clock[0] = max(clock[0], item[0])
        wait = next(item[1], None)
        if wait is None:
            flows.remove(item)
        else:
            item[0] = clock[0] + wait

    def finish(flow):
        while any(item[1] is flow for item in flows):
            step(min(flows, key=lambda item: item[0]))

    def passed(time):
        target = clock[0] + time
        while flows and min(item[0] for item in flows) <= target:
            step(min(flows, key=lambda item: item[0]))
        clock[0] = target

    loads[0].wait()
    flow_x = start(frames_to_patches(x_ref, a1x, xb))
    loads[1].wait()
    flow_g = start(frames_to_patches(g_ref, a1g, gb))
    loads[2].wait()
    gain[...] = gain_ref[...].astype(F32)
    finish(flow_x)
    gather_x = start(gather(xb))
    finish(flow_g)
    gather_g = start(gather(gb))
    finish(gather_x)

    def square(m, total):
        block = flat(xb[m]).astype(F32)
        return total + block * block

    squares = lax.fori_loop(0, 16, square, jnp.zeros((256, HEAD), F32))
    mean = jnp.sum(squares, axis=-1, keepdims=True) * (1.0 / 2048)
    inv[...] = jnp.broadcast_to(lax.rsqrt(mean + EPS), (256, HEAD))

    def normalise(m, carry):
        block = flat(xb[m]).astype(F32) * inv[...] * gain[pl.ds(m, 1), :]
        norm[:, pl.ds(pl.multiple_of(m * 128, 128), 128)] = block.astype(BF)
        return carry

    lax.fori_loop(0, 16, normalise, 0, unroll=2)
    passed(1.5)
    for load in loads[3:]:
        load.wait()
    qkv[...] = mm(norm[...], wqkv[...]).astype(BF)
    passed(1.0)

    scale = HEAD ** (-0.5)
    rows = lax.broadcasted_iota(jnp.int32, (256, 256), 0)
    cols = lax.broadcasted_iota(jnp.int32, (256, 256), 1)
    keep = (((rows - cols) & 15) == 0) & (cols <= rows)
    queries, keys, values = (qkv[:, pl.ds(i * 128, 128)] for i in range(3))
    scores = jnp.where(keep, mm_nt(queries, keys) * scale, -1e30)
    expo = jnp.exp(scores - jnp.max(scores, axis=-1, keepdims=True))
    soft = expo / jnp.sum(expo, axis=-1, keepdims=True)
    probs[...] = soft
    attended = mm(soft.astype(BF), values)
    att[...] = attended.astype(BF)
    passed(1.5)

    def out_term(i, carry):
        wide = mm(att[...], wout[:, pl.ds(pl.multiple_of(i * 256, 256), 256)]).astype(BF)
        term1[2 * i] = wide[:, :128]
        term1[2 * i + 1] = wide[:, 128:]
        return carry

    lax.fori_loop(0, 8, out_term, 0, unroll=4)
    passed(1.0)

    def layer_flow():
        yield from scatter_sum(term1, rb1, zs1, zb1)
        los[...] = (flat(xb[mp]).astype(F32) + summed(term1, rb1, zb1)).astype(BF).reshape(
            4, 4, 16, HEAD
        )
        yield 0.1
        yield from patches_to_frames(los, b1l, lod)
        store(lod, lo_hbm)

    start(layer_flow())
    att_t[...] = jnp.transpose(attended).astype(BF)
    probs_t[...] = jnp.transpose(soft).astype(BF)

    def turn(m, carry):
        at = pl.multiple_of(m * 128, 128)
        block = norm[:, pl.ds(at, 128)].astype(F32)
        norm_t[pl.ds(at, 128), :] = jnp.transpose(block).astype(BF)
        return carry

    lax.fori_loop(0, 16, turn, 0, unroll=2)
    finish(gather_g)

    def pair_of(i):
        return jnp.concatenate([flat(gb[2 * i]), flat(gb[2 * i + 1])], axis=1)

    total = jnp.zeros((256, HEAD), F32)
    for i in range(8):
        total += mm_nt(pair_of(i), wout[:, pl.ds(i * 256, 256)])
    gheads[...] = total.astype(BF)

    def out_weight(i, carry):
        wide = mm(att_t[...], pair_of(i)).astype(BF)
        wg[3, lax.div(i, 2), 2 * lax.rem(i, 2)] = wide[:, :128]
        wg[3, lax.div(i, 2), 2 * lax.rem(i, 2) + 1] = wide[:, 128:]
        return carry

    def in_weight(c):
        grad = dqkv[:, pl.ds(c * 128, 128)]

        def body(i, carry):
            tall = mm(norm_t[pl.ds(pl.multiple_of(i * 256, 256), 256), :], grad).astype(BF)
            wg[c, lax.div(i, 2), 2 * lax.rem(i, 2)] = tall[:128]
            wg[c, lax.div(i, 2), 2 * lax.rem(i, 2) + 1] = tall[128:]
            return carry

        lax.fori_loop(0, 8, body, 0, unroll=4)
        start(weight_sum(c, True))
        passed(1.5)

    dqkv[:, pl.ds(256, 128)] = mm(probs_t[...], gheads[...]).astype(BF)
    in_weight(2)
    dprobs = mm_nt(gheads[...], qkv[:, pl.ds(256, 128)]).astype(BF).astype(F32)
    soft = probs[...]
    delta = jnp.sum(soft * dprobs, axis=-1, keepdims=True)
    dscores = soft * (dprobs - delta) * scale
    high = dscores.astype(BF)
    low = (dscores - high.astype(F32)).astype(BF)
    keys = qkv[:, pl.ds(128, 128)]
    dqkv[:, pl.ds(0, 128)] = (mm(high, keys) + mm(low, keys)).astype(BF)
    in_weight(0)
    turned = jnp.transpose(dscores)
    high = turned.astype(BF)
    low = (turned - high.astype(F32)).astype(BF)
    queries = qkv[:, pl.ds(0, 128)]
    dqkv[:, pl.ds(128, 128)] = (mm(high, queries) + mm(low, queries)).astype(BF)
    in_weight(1)
    lax.fori_loop(0, 8, out_weight, 0, unroll=4)
    start(weight_sum(3, False))
    passed(1.5)

    def norm_term(i, total):
        tall = wqkv[pl.ds(pl.multiple_of(i * 256, 256), 256), :]
        wide = mm_nt(dqkv[...], tall).astype(BF)
        for half in (0, 1):
            part = wide[:, half * 128 : half * 128 + 128]
            term2[2 * i + half] = part
            total += gain[pl.ds(2 * i + half, 1), :] * part.astype(F32) * flat(
                xb[2 * i + half]
            ).astype(F32)
        return total

    inner = lax.fori_loop(0, 8, norm_term, jnp.zeros((256, HEAD), F32), unroll=2)
    rowb[mp] = jnp.broadcast_to(jnp.sum(jnp.transpose(inner), axis=0, keepdims=True), (8, 256))
    rows_flow = gather(rowb)

    def input_flow():
        yield from scatter_sum(term2, rb2, zs2, zb2)
        yield from rows_flow
        row = jnp.sum(rowb[...].reshape(16, 8, 256), axis=0)[:1]
        row = jnp.transpose(jnp.broadcast_to(row, (HEAD, 256)))
        grad = summed(term2, rb2, zb2)
        scale_own = inv[...]
        out = (
            flat(gb[mp]).astype(F32)
            + scale_own * gain[pl.ds(mp, 1), :] * grad
            - flat(xb[mp]).astype(F32) * (scale_own * scale_own * scale_own) * row * (1.0 / 2048)
        )
        igs[...] = out.astype(BF).reshape(4, 4, 16, HEAD)
        yield 0.1
        yield from patches_to_frames(igs, b1i, igd)
        store(igd, ig_hbm)

    start(input_flow())
    while flows:
        step(min(flows, key=lambda item: item[0]))

    for copy in started:
        copy.wait_send()
    for copy in stores:
        copy.wait()


def shards(frames_in, norm_gain, w_qkv, w_out, cotangent):
    hbm = pl.BlockSpec(memory_space=pltpu.HBM)

    def bf(*shape):
        return pltpu.VMEM(shape, BF)

    def f32(*shape):
        return pltpu.VMEM(shape, F32)

    scratch = [
        bf(4, 4, 16, HEAD), bf(4, 4, 16, HEAD), bf(16, HEAD),
        bf(4, 4, 16, HEAD), bf(4, 4, 16, HEAD),
        bf(16, 4, 4, 16, HEAD), bf(16, 4, 4, 16, HEAD),
        bf(2048, 384), bf(HEAD, 2048),
        f32(16, HEAD), f32(256, HEAD),
        bf(256, 2048), bf(2048, 256),
        bf(256, 384), bf(256, HEAD), bf(HEAD, 256),
        f32(256, 256), bf(256, 256),
        bf(256, HEAD), bf(256, 384),
        bf(16, 256, HEAD), bf(16, 256, HEAD),
        bf(14, 256, HEAD), bf(14, 256, HEAD),
        bf(256, HEAD), bf(256, HEAD), bf(256, HEAD), bf(256, HEAD),
        f32(16, 8, 256),
        bf(4, 4, 4, HEAD, HEAD),
        bf(4, 4, HEAD, HEAD), bf(4, 4, HEAD, HEAD),
        bf(4, 4, HEAD, HEAD), bf(4, 4, HEAD, HEAD),
        bf(4, 3, HEAD, HEAD),
        bf(3, 4, 4, HEAD, HEAD), bf(HEAD, HEAD),
        bf(4, 4, 16, HEAD), bf(4, 4, 16, HEAD), bf(4, 4, 16, HEAD),
        bf(4, 4, 16, HEAD), bf(4, 4, 16, HEAD), bf(4, 4, 16, HEAD),
        pltpu.SemaphoreType.DMA((COPIES,)),
        pltpu.SemaphoreType.DMA((COPIES,)),
        pltpu.SemaphoreType.DMA((11,)),
    ]
    layer_out, input_grad, qkv_weight_grad, out_weight_grad = pl.pallas_call(
        kernel,
        out_shape=(
            jax.ShapeDtypeStruct((4, 4, 16, HEAD), BF),
            jax.ShapeDtypeStruct((4, 4, 16, HEAD), BF),
            jax.ShapeDtypeStruct((4, 4, HEAD, 384), BF),
            jax.ShapeDtypeStruct((HEAD, HEAD), BF),
        ),
        in_specs=[hbm] * 5,
        out_specs=(hbm, hbm, hbm, hbm),
        scratch_shapes=scratch,
        compiler_params=pltpu.CompilerParams(
            collective_id=0, has_side_effects=True, vmem_limit_bytes=60 * 1024 * 1024
        ),
        name="sublayer",
    )(
        frames_in.reshape(4, 4, 16, HEAD),
        norm_gain.reshape(16, HEAD),
        w_qkv,
        w_out,
        cotangent.reshape(4, 4, 16, HEAD),
    )
    return (
        layer_out.reshape(1, 256, HEAD),
        input_grad.reshape(1, 256, HEAD),
        qkv_weight_grad.reshape(2048, 384),
        out_weight_grad,
    )


def solution(mesh):
    return jax.shard_map(
        shards,
        mesh=mesh,
        in_specs=(
            P(("clip", "seq"), None, "mp"),
            P(),
            P(None, "mp"),
            P("mp", None),
            P(("clip", "seq"), None, "mp"),
        ),
        out_specs=(
            P(("clip", "seq"), None, "mp"),
            P(("clip", "seq"), None, "mp"),
            P("clip", "mp"),
            P(("clip", "mp"), "seq"),
        ),
        check_vma=False,
    )
```

```python
import jax
import jax.numpy as jnp
from jax import lax
from jax.experimental import pallas as pl
from jax.experimental.pallas import tpu as pltpu
from jax.sharding import PartitionSpec as P

HEAD = 128
EPS = 1e-05
BF = jnp.bfloat16
F32 = jnp.float32
MESH = pl.DeviceIdType.MESH
COPIES = 232
CUT = 96
NT = (((1,), (1,)), ((), ()))


def mm(a, b):
    return jnp.dot(a, b, preferred_element_type=F32)


def mm_nt(a, b):
    return lax.dot_general(a, b, NT, preferred_element_type=F32)


def flat(block):
    return block.reshape(256, HEAD)


def kernel(
    x_hbm, gain_hbm, wqkv_hbm, wout_hbm, g_hbm,
    lo_out, ig_out, dwqkv_out, dwo_out,
    x_ref, g_ref, gain_ref, a1x, a1g, xb, gb, wqkv, wout, gain, inv, norm, norm_t, qkv, att, att_t,
    probs, probs_t, gheads, dqkv, term1, term2, rb1, rb2, zs1, zb1, zs2, zb2, rowb,
    wg, tx, px, mx, sx, tz, pz, mz, tzz, pzz, mzz, szz, rxx, res, dwo, los, igs, b1l, b1i, lod, igd,
    ssem, rsem, lsem,
):
    clip, seq, mp = lax.axis_index("clip"), lax.axis_index("seq"), lax.axis_index("mp")
    zh, x = seq // 4, seq & 3
    zl, y = mp // 8, mp & 7
    e = 1 - 2 * clip
    zp = 1 - zl

    def x_at(step):
        return (x + step) & 3

    def z_at(step):
        return (zh + step) & 3

    def y_at(step):
        return (y + step) & 7

    def dev_x(to):
        return (clip, zh * 4 + to, mp)

    def dev_z(to):
        return (clip, to * 4 + x, mp)

    def dev_y(to):
        return (clip, seq, zl * 8 + to)

    dev_pair = (clip, seq, zp * 8 + y)

    loads = [
        pltpu.make_async_copy(src, dst, lsem.at[at])
        for at, (src, dst) in enumerate(
            [(x_hbm, x_ref), (g_hbm, g_ref), (gain_hbm, gain_ref), (wqkv_hbm, wqkv), (wout_hbm, wout)]
        )
    ]
    for load in loads:
        load.start()

    barrier = pltpu.get_barrier_semaphore()
    peers = [dev_x(x_at(s)) for s in (1, 2, 3)] + [dev_z(z_at(s)) for s in (1, 2, 3)]
    peers += [dev_y(y_at(1)), dev_y(y_at(-1)), dev_pair]
    for peer in peers:
        pl.semaphore_signal(barrier, inc=1, device_id=peer, device_id_type=MESH)
    pl.semaphore_wait(barrier, len(peers))

    started = []

    def send(src, dst, device):
        at = len(started)
        copy = pltpu.make_async_remote_copy(
            src_ref=src,
            dst_ref=dst,
            send_sem=ssem.at[at],
            recv_sem=rsem.at[at],
            device_id=device,
            device_id_type=MESH,
        )
        copy.start()
        started.append(copy)
        return copy

    stores = []

    def store(src, dst):
        stores.append(pltpu.make_async_copy(src, dst, lsem.at[len(loads) + len(stores)]))
        stores[-1].start()

    def frames_to_patches(src, mid, dst):
        sent = [send(src.at[:, x_at(s)], mid.at[x], dev_x(x_at(s))) for s in (1, 3, 2)]
        mid[x] = src[:, x]
        yield 2.0
        for copy in sent:
            copy.wait_recv()
        sent = [send(mid.at[:, z_at(s)], dst.at[mp, zh], dev_z(z_at(s))) for s in (1, 3, 2)]
        dst[mp, zh] = mid[:, zh]
        yield 2.0
        for copy in sent:
            copy.wait_recv()

    def patches_to_frames(src, mid, dst):
        sent = [send(src.at[z_at(s)], mid.at[zh], dev_z(z_at(s))) for s in (1, 3, 2)]
        mid[zh] = src[zh]
        yield 2.0
        for copy in sent:
            copy.wait_recv()
        sent = [send(mid.at[:, x_at(s)], dst.at[:, x], dev_x(x_at(s))) for s in (1, 3, 2)]
        dst[:, x] = mid[:, x]
        yield 2.0
        for copy in sent:
            copy.wait_recv()

    def gather(buf):
        def pass_on(block, device):
            return send(buf.at[block], buf.at[block], device)

        ahead, back = dev_y(y_at(e)), dev_y(y_at(-e))

        def own(step):
            return zl * 8 + y_at(step)

        def other(step):
            return zp * 8 + y_at(step)

        a = pass_on(mp, ahead)
        b = pass_on(mp, back)
        pair = [pass_on(mp, dev_pair)]
        yield 2.0
        a.wait_recv()
        a = pass_on(own(-e), ahead)
        yield 0.1
        b.wait_recv()
        b = pass_on(own(e), back)
        yield 0.5
        pair[0].wait_recv()
        c = pass_on(other(0), ahead)
        d = pass_on(other(0), back)
        yield 1.0
        a.wait_recv()
        a = pass_on(own(-2 * e), ahead)
        yield 0.1
        b.wait_recv()
        b = pass_on(own(2 * e), back)
        pair.append(pass_on(own(2 * e), dev_pair))
        yield 1.0
        c.wait_recv()
        c = pass_on(other(-e), ahead)
        yield 0.1
        d.wait_recv()
        yield 1.0
        a.wait_recv()
        a = pass_on(own(-3 * e), ahead)
        pair.append(pass_on(own(-3 * e), dev_pair))
        yield 0.1
        b.wait_recv()
        pair.append(pass_on(own(3 * e), dev_pair))
        yield 0.5
        c.wait_recv()
        yield 1.0
        a.wait_recv()
        pair.append(pass_on(own(-4 * e), dev_pair))
        for copy in pair[1:]:
            yield 0.5
            copy.wait_recv()

    def scatter_sum(term, rb, zs, zb):
        def slot(i, j, k):
            return i * 7 + j * 4 + k - 1

        planes = (zp, zl)
        ways = ((e, 4), (-e, 3))
        order = [(i, j) for i in (0, 1) for j in (0, 1)]
        sent = {}
        for i, j in order:
            way, steps = ways[j]
            dest = planes[i] * 8 + y_at(steps * way)
            sent[i, j] = send(term.at[dest], rb.at[slot(i, j, 1)], dev_y(y_at(way)))
        last = None
        for k in (1, 2, 3, 4):
            for i, j in order:
                way, steps = ways[j]
                if k > steps:
                    continue
                yield 2.2 if (i, j) == (0, 0) else 0.5
                sent[i, j].wait_recv()
                if k < steps:
                    dest = planes[i] * 8 + y_at((steps - k) * way)
                    here = rb.at[slot(i, j, k)]
                    here[...] = (here[...].astype(F32) + term[dest].astype(F32)).astype(BF)
                    sent[i, j] = send(here, rb.at[slot(i, j, k + 1)], dev_y(y_at(way)))
                elif k == 4 and i == 0:
                    zs[...] = (
                        term[zp * 8 + y].astype(F32)
                        + rb[slot(0, 0, 4)].astype(F32)
                        + rb[slot(0, 1, 3)].astype(F32)
                    ).astype(BF)
                    last = send(zs, zb, dev_pair)
        yield 2.0
        last.wait_recv()

    def summed(term, rb, zb):
        return (
            term[mp].astype(F32)
            + rb[7 + 3].astype(F32)
            + rb[7 + 4 + 2].astype(F32)
            + zb[...].astype(F32)
        )

    def weight_sum(c, rows, gathered):
        r = pl.ds(0, rows)
        xp, xm, zm = x_at(e), x_at(-e), z_at(-e)
        ahead, back, z_ahead, z_back = dev_x(xp), dev_x(xm), dev_z(z_at(e)), dev_z(zm)
        q = (z_at(2), z_at(e), zm, zh)
        far = [send(wg.at[c, q[i], x_at(2), r], tx.at[c, i, r], ahead) for i in range(4)]
        plain = send(wg.at[c, :, xm, r], px.at[c, :, r], back)
        near = []

        def here(i):
            return (
                wg[c, q[i], x, r].astype(F32) + px[c, q[i], r].astype(F32) + mx[c, i, r].astype(F32)
            )

        for i in range(4):
            yield 4.0 if i == 0 else 1.0
            far[i].wait_recv()
            tx[c, i, r] = (tx[c, i, r].astype(F32) + wg[c, q[i], xp, r].astype(F32)).astype(BF)
            near.append(send(tx.at[c, i, r], mx.at[c, i, r], ahead))
        yield 1.0
        plain.wait_recv()
        near[0].wait_recv()
        sx[c, 0, r] = here(0).astype(BF)
        z_far = send(sx.at[c, 0, r], tz.at[c, r], z_ahead)
        yield 1.5
        near[1].wait_recv()
        near[2].wait_recv()
        sx[c, 1, r] = here(2).astype(BF)
        z_plain = send(sx.at[c, 1, r], pz.at[c, r], z_back)
        yield 1.5
        z_far.wait_recv()
        tz[c, r] = (tz[c, r].astype(F32) + here(1)).astype(BF)
        z_near = send(tz.at[c, r], mz.at[c, r], z_ahead)
        yield 3.0
        near[3].wait_recv()
        z_plain.wait_recv()
        z_near.wait_recv()
        total = (here(3) + pz[c, r].astype(F32) + mz[c, r].astype(F32)).astype(BF)
        if not gathered:
            dwo[...] = total
            store(dwo, dwo_out)
            return
        res[c, zh, x, r] = total

        def pass_on(at, column, device):
            return send(res.at[c, at, column, r], res.at[c, at, column, r], device)

        up = pass_on(zh, x, z_ahead)
        down = pass_on(zh, x, z_back)
        first, second = [pass_on(zh, x, ahead)], [pass_on(zh, x, back)]
        third = []
        yield 3.0
        up.wait_recv()
        up = pass_on(zm, x, z_ahead)
        first.append(pass_on(zm, x, ahead))
        second.append(pass_on(zm, x, back))
        yield 0.2
        down.wait_recv()
        first.append(pass_on(q[1], x, ahead))
        second.append(pass_on(q[1], x, back))
        yield 0.3
        first[0].wait_recv()
        third.append(pass_on(zh, xm, ahead))
        yield 2.5
        up.wait_recv()
        first.append(pass_on(q[0], x, ahead))
        second.append(pass_on(q[0], x, back))
        for i, at in ((1, zm), (2, q[1]), (3, q[0])):
            yield 1.0
            first[i].wait_recv()
            third.append(pass_on(at, xm, ahead))
        yield 3.0
        for copy in second + third:
            copy.wait_recv()
        store(res.at[c, :, :, r], dwqkv_out.at[:, :, r, pl.ds(c * 128, 128)])

    def weight_sum_z(c):
        r = pl.ds(CUT, 128 - CUT)
        zp_, zm = z_at(e), z_at(-e)
        ahead, back = dev_z(zp_), dev_z(zm)
        far = send(wg.at[c, z_at(2), :, r], tzz.at[c], ahead)
        plain = send(wg.at[c, zm, :, r], pzz.at[c], back)
        yield 5.0
        far.wait_recv()
        tzz[c] = (tzz[c].astype(F32) + wg[c, zp_, :, r].astype(F32)).astype(BF)
        near = send(tzz.at[c], mzz.at[c], ahead)
        yield 5.0
        plain.wait_recv()
        near.wait_recv()
        szz[c] = (
            wg[c, zh, :, r].astype(F32) + pzz[c].astype(F32) + mzz[c].astype(F32)
        ).astype(BF)
        across = [send(szz.at[c, x_at(s)], rxx.at[c, s - 1], dev_x(x_at(s))) for s in (1, 3, 2)]
        yield 2.5
        for copy in across:
            copy.wait_recv()
        total = wg[c, zh, x, r].astype(F32) + pzz[c, x].astype(F32) + mzz[c, x].astype(F32)
        for s in range(3):
            total += rxx[c, s].astype(F32)
        res[c, zh, x, r] = total.astype(BF)
        own = res.at[c, zh, x, r]
        across = [send(own, own, dev_x(x_at(s))) for s in (1, 3, 2)]
        yield 2.5
        for copy in across:
            copy.wait_recv()
        own = res.at[c, zh, :, r]
        up, down = send(own, own, ahead), send(own, own, back)
        yield 5.0
        up.wait_recv()
        other = res.at[c, zm, :, r]
        up = send(other, other, ahead)
        yield 5.0
        down.wait_recv()
        up.wait_recv()
        store(res.at[c, :, :, r], dwqkv_out.at[:, :, r, pl.ds(c * 128, 128)])

    flows = []
    clock = [0.0]

    def start(flow):
        flows.append([clock[0] + next(flow), flow])
        return flow

    def step(item):
        clock[0] = max(clock[0], item[0])
        wait = next(item[1], None)
        if wait is None:
            flows.remove(item)
        else:
            item[0] = clock[0] + wait

    def finish(flow):
        while any(item[1] is flow for item in flows):
            step(min(flows, key=lambda item: item[0]))

    def advance(flow, waits):
        for _ in range(waits):
            step(next(item for item in flows if item[1] is flow))

    def passed(time):
        target = clock[0] + time
        while flows and min(item[0] for item in flows) <= target:
            step(min(flows, key=lambda item: item[0]))
        clock[0] = target

    loads[0].wait()
    flow_x = start(frames_to_patches(x_ref, a1x, xb))
    loads[1].wait()
    flow_g = start(frames_to_patches(g_ref, a1g, gb))
    loads[2].wait()
    gain[...] = gain_ref[...].astype(F32)
    finish(flow_x)
    gather_x = start(gather(xb))
    finish(flow_g)
    advance(gather_x, 7)
    gather_g = start(gather(gb))
    finish(gather_x)

    def square(m, total):
        block = flat(xb[m]).astype(F32)
        return total + block * block

    squares = lax.fori_loop(0, 16, square, jnp.zeros((256, HEAD), F32))
    mean = jnp.sum(squares, axis=-1, keepdims=True) * (1.0 / 2048)
    inv[...] = jnp.broadcast_to(lax.rsqrt(mean + EPS), (256, HEAD))

    def normalise(m, carry):
        block = flat(xb[m]).astype(F32) * inv[...] * gain[pl.ds(m, 1), :]
        norm[:, pl.ds(pl.multiple_of(m * 128, 128), 128)] = block.astype(BF)
        return carry

    lax.fori_loop(0, 16, normalise, 0, unroll=2)
    passed(1.5)
    for load in loads[3:]:
        load.wait()
    qkv[...] = mm(norm[...], wqkv[...]).astype(BF)
    passed(1.0)

    scale = HEAD ** (-0.5)
    rows = lax.broadcasted_iota(jnp.int32, (256, 256), 0)
    cols = lax.broadcasted_iota(jnp.int32, (256, 256), 1)
    keep = (((rows - cols) & 15) == 0) & (cols <= rows)
    queries, keys, values = (qkv[:, pl.ds(i * 128, 128)] for i in range(3))
    scores = jnp.where(keep, mm_nt(queries, keys) * scale, -1e30)
    expo = jnp.exp(scores - jnp.max(scores, axis=-1, keepdims=True))
    soft = expo / jnp.sum(expo, axis=-1, keepdims=True)
    probs[...] = soft
    attended = mm(soft.astype(BF), values)
    att[...] = attended.astype(BF)
    passed(1.5)

    def out_term(i, carry):
        wide = mm(att[...], wout[:, pl.ds(pl.multiple_of(i * 256, 256), 256)]).astype(BF)
        term1[2 * i] = wide[:, :128]
        term1[2 * i + 1] = wide[:, 128:]
        return carry

    lax.fori_loop(0, 8, out_term, 0, unroll=4)
    passed(1.0)

    def layer_flow():
        yield from scatter_sum(term1, rb1, zs1, zb1)
        los[...] = (flat(xb[mp]).astype(F32) + summed(term1, rb1, zb1)).astype(BF).reshape(
            4, 4, 16, HEAD
        )
        yield 0.1
        yield from patches_to_frames(los, b1l, lod)
        store(lod, lo_out)

    start(layer_flow())
    att_t[...] = jnp.transpose(attended).astype(BF)
    probs_t[...] = jnp.transpose(soft).astype(BF)

    def turn(m, carry):
        at = pl.multiple_of(m * 128, 128)
        block = norm[:, pl.ds(at, 128)].astype(F32)
        norm_t[pl.ds(at, 128), :] = jnp.transpose(block).astype(BF)
        return carry

    lax.fori_loop(0, 16, turn, 0, unroll=2)
    finish(gather_g)

    def pair_of(i):
        return jnp.concatenate([flat(gb[2 * i]), flat(gb[2 * i + 1])], axis=1)

    def out_weight(i, carry):
        wide = mm(att_t[...], pair_of(i)).astype(BF)
        wg[3, lax.div(i, 2), 2 * lax.rem(i, 2)] = wide[:, :128]
        wg[3, lax.div(i, 2), 2 * lax.rem(i, 2) + 1] = wide[:, 128:]
        return carry

    lax.fori_loop(0, 8, out_weight, 0, unroll=4)
    start(weight_sum(3, 128, False))
    passed(1.0)
    total = jnp.zeros((256, HEAD), F32)
    for i in range(8):
        total += mm_nt(pair_of(i), wout[:, pl.ds(i * 256, 256)])
    gheads[...] = total.astype(BF)

    def in_weight(c):
        grad = dqkv[:, pl.ds(c * 128, 128)]

        def body(i, carry):
            tall = mm(norm_t[pl.ds(pl.multiple_of(i * 256, 256), 256), :], grad).astype(BF)
            wg[c, lax.div(i, 2), 2 * lax.rem(i, 2)] = tall[:128]
            wg[c, lax.div(i, 2), 2 * lax.rem(i, 2) + 1] = tall[128:]
            return carry

        lax.fori_loop(0, 8, body, 0, unroll=4)
        start(weight_sum(c, CUT, True))
        start(weight_sum_z(c))
        passed(1.5)

    dqkv[:, pl.ds(256, 128)] = mm(probs_t[...], gheads[...]).astype(BF)
    in_weight(2)
    dprobs = mm_nt(gheads[...], qkv[:, pl.ds(256, 128)]).astype(BF).astype(F32)
    soft = probs[...]
    delta = jnp.sum(soft * dprobs, axis=-1, keepdims=True)
    dscores = soft * (dprobs - delta) * scale
    high = dscores.astype(BF)
    low = (dscores - high.astype(F32)).astype(BF)
    keys = qkv[:, pl.ds(128, 128)]
    dqkv[:, pl.ds(0, 128)] = (mm(high, keys) + mm(low, keys)).astype(BF)
    turned = jnp.transpose(dscores)
    high = turned.astype(BF)
    low = (turned - high.astype(F32)).astype(BF)
    queries = qkv[:, pl.ds(0, 128)]
    dqkv[:, pl.ds(128, 128)] = (mm(high, queries) + mm(low, queries)).astype(BF)

    def norm_term(i, total):
        tall = wqkv[pl.ds(pl.multiple_of(i * 256, 256), 256), :]
        wide = mm_nt(dqkv[...], tall).astype(BF)
        for half in (0, 1):
            part = wide[:, half * 128 : half * 128 + 128]
            term2[2 * i + half] = part
            total += gain[pl.ds(2 * i + half, 1), :] * part.astype(F32) * flat(
                xb[2 * i + half]
            ).astype(F32)
        return total

    inner = lax.fori_loop(0, 8, norm_term, jnp.zeros((256, HEAD), F32), unroll=2)
    rowb[mp] = jnp.broadcast_to(jnp.sum(jnp.transpose(inner), axis=0, keepdims=True), (8, 256))
    rows_flow = gather(rowb)

    def input_flow():
        yield from scatter_sum(term2, rb2, zs2, zb2)
        yield from rows_flow
        row = jnp.sum(rowb[...].reshape(16, 8, 256), axis=0)[:1]
        row = jnp.transpose(jnp.broadcast_to(row, (HEAD, 256)))
        grad = summed(term2, rb2, zb2)
        scale_own = inv[...]
        out = (
            flat(gb[mp]).astype(F32)
            + scale_own * gain[pl.ds(mp, 1), :] * grad
            - flat(xb[mp]).astype(F32) * (scale_own * scale_own * scale_own) * row * (1.0 / 2048)
        )
        igs[...] = out.astype(BF).reshape(4, 4, 16, HEAD)
        yield 0.1
        yield from patches_to_frames(igs, b1i, igd)
        store(igd, ig_out)

    start(input_flow())
    passed(2.0)
    in_weight(0)
    in_weight(1)
    while flows:
        step(min(flows, key=lambda item: item[0]))

    for copy in started:
        copy.wait_send()
    for copy in stores:
        copy.wait()


def shards(frames_in, norm_gain, w_qkv, w_out, cotangent):
    hbm = pl.BlockSpec(memory_space=pltpu.HBM)

    def bf(*shape):
        return pltpu.VMEM(shape, BF)

    def f32(*shape):
        return pltpu.VMEM(shape, F32)

    scratch = [
        bf(4, 4, 16, HEAD), bf(4, 4, 16, HEAD), bf(16, HEAD),
        bf(4, 4, 16, HEAD), bf(4, 4, 16, HEAD),
        bf(16, 4, 4, 16, HEAD), bf(16, 4, 4, 16, HEAD),
        bf(2048, 384), bf(HEAD, 2048),
        f32(16, HEAD), f32(256, HEAD),
        bf(256, 2048), bf(2048, 256),
        bf(256, 384), bf(256, HEAD), bf(HEAD, 256),
        f32(256, 256), bf(256, 256),
        bf(256, HEAD), bf(256, 384),
        bf(16, 256, HEAD), bf(16, 256, HEAD),
        bf(14, 256, HEAD), bf(14, 256, HEAD),
        bf(256, HEAD), bf(256, HEAD), bf(256, HEAD), bf(256, HEAD),
        f32(16, 8, 256),
        bf(4, 4, 4, HEAD, HEAD),
        bf(4, 4, HEAD, HEAD), bf(4, 4, HEAD, HEAD),
        bf(4, 4, HEAD, HEAD), bf(4, 2, HEAD, HEAD),
        bf(4, HEAD, HEAD), bf(4, HEAD, HEAD), bf(4, HEAD, HEAD),
        bf(3, 4, 128 - CUT, HEAD), bf(3, 4, 128 - CUT, HEAD),
        bf(3, 4, 128 - CUT, HEAD), bf(3, 4, 128 - CUT, HEAD),
        bf(3, 3, 128 - CUT, HEAD),
        bf(3, 4, 4, HEAD, HEAD), bf(HEAD, HEAD),
        bf(4, 4, 16, HEAD), bf(4, 4, 16, HEAD), bf(4, 4, 16, HEAD),
        bf(4, 4, 16, HEAD), bf(4, 4, 16, HEAD), bf(4, 4, 16, HEAD),
        pltpu.SemaphoreType.DMA((COPIES,)),
        pltpu.SemaphoreType.DMA((COPIES,)),
        pltpu.SemaphoreType.DMA((14,)),
    ]
    layer_out, input_grad, qkv_weight_grad, out_weight_grad = pl.pallas_call(
        kernel,
        out_shape=(
            jax.ShapeDtypeStruct((4, 4, 16, HEAD), BF),
            jax.ShapeDtypeStruct((4, 4, 16, HEAD), BF),
            jax.ShapeDtypeStruct((4, 4, HEAD, 384), BF),
            jax.ShapeDtypeStruct((HEAD, HEAD), BF),
        ),
        in_specs=[hbm] * 5,
        out_specs=(hbm, hbm, hbm, hbm),
        scratch_shapes=scratch,
        compiler_params=pltpu.CompilerParams(
            collective_id=0, has_side_effects=True, vmem_limit_bytes=54656 * 1024
        ),
        name="sublayer",
    )(
        frames_in.reshape(4, 4, 16, HEAD),
        norm_gain.reshape(16, HEAD),
        w_qkv,
        w_out,
        cotangent.reshape(4, 4, 16, HEAD),
    )
    return (
        layer_out.reshape(1, 256, HEAD),
        input_grad.reshape(1, 256, HEAD),
        qkv_weight_grad.reshape(2048, 384),
        out_weight_grad,
    )


def solution(mesh):
    return jax.shard_map(
        shards,
        mesh=mesh,
        in_specs=(
            P(("clip", "seq"), None, "mp"),
            P(),
            P(None, "mp"),
            P("mp", None),
            P(("clip", "seq"), None, "mp"),
        ),
        out_specs=(
            P(("clip", "seq"), None, "mp"),
            P(("clip", "seq"), None, "mp"),
            P("clip", "mp"),
            P(("clip", "mp"), "seq"),
        ),
        check_vma=False,
    )
```

```python
import jax
import jax.numpy as jnp
from jax import lax
from jax.experimental import pallas as pl
from jax.experimental.pallas import tpu as pltpu
from jax.sharding import PartitionSpec as P

HEAD = 128
EPS = 1e-05
BF = jnp.bfloat16
F32 = jnp.float32
MESH = pl.DeviceIdType.MESH
COPIES = 232
NT = (((1,), (1,)), ((), ()))


def mm(a, b):
    return jnp.dot(a, b, preferred_element_type=F32)


def mm_nt(a, b):
    return lax.dot_general(a, b, NT, preferred_element_type=F32)


def flat(block):
    return block.reshape(256, HEAD)


def kernel(
    x_hbm, gain_hbm, wqkv_hbm, wout_hbm, g_hbm,
    lo_out, ig_out, dwqkv_out, dwo_out,
    x_ref, g_ref, gain_ref, xb, gb, wqkv, wout, gain, inv, norm, norm_t, qkv, att, att_t,
    probs, probs_t, gheads, dqkv, term1, term2, rb1, rb2, zs1, zb1, zs2, zb2, rowb,
    wg, tx, px, mx, sx, rz, res, dwo, los, igs, lod, igd,
    ssem, rsem, lsem,
):
    clip, seq, mp = lax.axis_index("clip"), lax.axis_index("seq"), lax.axis_index("mp")
    zh, x = seq // 4, seq & 3
    zl, y = mp // 8, mp & 7
    e = 1 - 2 * clip
    zp = 1 - zl

    def x_at(step):
        return (x + step) & 3

    def z_at(step):
        return (zh + step) & 3

    def y_at(step):
        return (y + step) & 7

    def dev_x(to):
        return (clip, zh * 4 + to, mp)

    def dev_z(to):
        return (clip, to * 4 + x, mp)

    def dev_y(to):
        return (clip, seq, zl * 8 + to)

    dev_pair = (clip, seq, zp * 8 + y)

    loads = [
        pltpu.make_async_copy(src, dst, lsem.at[at])
        for at, (src, dst) in enumerate(
            [(x_hbm, x_ref), (g_hbm, g_ref), (gain_hbm, gain_ref), (wqkv_hbm, wqkv), (wout_hbm, wout)]
        )
    ]
    for load in loads:
        load.start()

    barrier = pltpu.get_barrier_semaphore()
    peers = [(clip, (seq + s) & 15, mp) for s in range(1, 16)]
    peers += [dev_y(y_at(s)) for s in (1, -1, 2, -2)] + [dev_pair]
    for peer in peers:
        pl.semaphore_signal(barrier, inc=1, device_id=peer, device_id_type=MESH)
    pl.semaphore_wait(barrier, len(peers))

    started = []

    def send(src, dst, device):
        at = len(started)
        copy = pltpu.make_async_remote_copy(
            src_ref=src,
            dst_ref=dst,
            send_sem=ssem.at[at],
            recv_sem=rsem.at[at],
            device_id=device,
            device_id_type=MESH,
        )
        copy.start()
        started.append(copy)
        return copy

    stores = []

    def store(src, dst):
        stores.append(pltpu.make_async_copy(src, dst, lsem.at[len(loads) + len(stores)]))
        stores[-1].start()

    def frames_to_patches(src, dst):
        sent = []
        for s in range(1, 16):
            to = (seq + s) & 15
            sent.append(send(src.at[to], dst.at[mp, seq], (clip, to, mp)))
        dst[mp, seq] = src[seq]
        yield 4.0
        for copy in sent:
            copy.wait_recv()

    def patches_to_frames(src, dst):
        sent = []
        for s in range(1, 16):
            to = (seq + s) & 15
            sent.append(send(src.at[to], dst.at[seq], (clip, to, mp)))
        dst[seq] = src[seq]
        yield 4.0
        for copy in sent:
            copy.wait_recv()

    def gather(buf):
        def pass_on(block, device):
            return send(buf.at[block], buf.at[block], device)

        def own(step):
            return zl * 8 + y_at(step)

        def other(step):
            return zp * 8 + y_at(step)

        ahead, back, ahead_2, back_2 = (dev_y(y_at(s)) for s in (e, -e, 2 * e, -2 * e))
        a2 = pass_on(mp, ahead_2)
        b2 = pass_on(mp, back_2)
        pair = [pass_on(mp, dev_pair)]
        a1 = pass_on(mp, ahead)
        b1 = pass_on(mp, back)
        yield 4.0
        a2.wait_recv()
        a4 = pass_on(own(-2 * e), ahead_2)
        a3 = pass_on(own(-2 * e), ahead)
        pair.append(pass_on(own(-2 * e), dev_pair))
        yield 0.1
        b2.wait_recv()
        b3 = pass_on(own(2 * e), back)
        pair.append(pass_on(own(2 * e), dev_pair))
        yield 0.5
        pair[0].wait_recv()
        c1 = pass_on(other(0), ahead)
        d1 = pass_on(other(0), back)
        yield 0.5
        a1.wait_recv()
        b1.wait_recv()
        yield 3.0
        a3.wait_recv()
        pair.append(pass_on(own(-3 * e), dev_pair))
        yield 0.1
        b3.wait_recv()
        pair.append(pass_on(own(3 * e), dev_pair))
        yield 1.0
        a4.wait_recv()
        pair.append(pass_on(own(-4 * e), dev_pair))
        yield 0.2
        c1.wait_recv()
        d1.wait_recv()
        for copy in pair[1:]:
            yield 1.0
            copy.wait_recv()

    def scatter_sum(term, rb, zs, zb):
        planes = (zp, zl)

        def share(i, step):
            return term[planes[i] * 8 + y_at(step)].astype(F32)

        def push(i, step, slot, hop):
            return send(term.at[planes[i] * 8 + y_at(step)], rb.at[7 * i + slot], dev_y(y_at(hop)))

        a1, b1, a2, b2, a3, b3, a4 = ({} for _ in range(7))
        for i in (0, 1):
            a4[i] = push(i, 4, 0, 2 * e)
            a3[i] = push(i, 3 * e, 3, e)
            b3[i] = push(i, -3 * e, 6, -e)
        for i in (0, 1):
            a1[i] = push(i, e, 1, e)
            b1[i] = push(i, -e, 4, -e)
        for i in (0, 1):
            yield 4.0 if i == 0 else 1.0
            b3[i].wait_recv()
            far = rb.at[7 * i + 6]
            far[...] = (far[...].astype(F32) + share(i, -2 * e)).astype(BF)
            b2[i] = send(far, rb.at[7 * i + 5], dev_y(y_at(-2 * e)))
            yield 0.2
            a3[i].wait_recv()
            a4[i].wait_recv()
            far = rb.at[7 * i + 3]
            far[...] = (
                far[...].astype(F32) + rb[7 * i].astype(F32) + share(i, 2 * e)
            ).astype(BF)
            a2[i] = send(far, rb.at[7 * i + 2], dev_y(y_at(2 * e)))
        last = None
        for i in (0, 1):
            yield 4.0 if i == 0 else 1.5
            for copy in (a1[i], b1[i], a2[i], b2[i]):
                copy.wait_recv()
            if i == 0:
                zs[...] = received(term, rb, 0, zp).astype(BF)
                last = send(zs, zb, dev_pair)
        yield 2.5
        last.wait_recv()

    def received(term, rb, i, plane):
        total = term[plane * 8 + y].astype(F32)
        for slot in (1, 2, 4, 5):
            total += rb[7 * i + slot].astype(F32)
        return total

    def summed(term, rb, zb):
        return received(term, rb, 1, zl) + zb[...].astype(F32)

    def weight_sum(c, gathered):
        xp, xm = x_at(e), x_at(-e)
        ahead, back = dev_x(xp), dev_x(xm)
        q = (z_at(2), z_at(1), z_at(3), zh)
        far = [send(wg.at[c, q[i], x_at(2)], tx.at[c, i], ahead) for i in range(4)]
        plain = send(wg.at[c, :, xm], px.at[c], back)
        near = []

        def here(i):
            return wg[c, q[i], x].astype(F32) + px[c, q[i]].astype(F32) + mx[c, i].astype(F32)

        for i in range(4):
            yield 4.0 if i == 0 else 0.7
            far[i].wait_recv()
            tx[c, i] = (tx[c, i].astype(F32) + wg[c, q[i], xp].astype(F32)).astype(BF)
            near.append(send(tx.at[c, i], mx.at[c, i], ahead))
        across = []
        yield 1.0
        plain.wait_recv()
        for i in range(3):
            yield 0.7
            near[i].wait_recv()
            sx[c, i] = here(i).astype(BF)
            across.append(send(sx.at[c, i], rz.at[c, i], dev_z(q[i])))
        yield 0.7
        near[3].wait_recv()
        total = here(3)
        yield 3.0
        for i in range(3):
            across[i].wait_recv()
            total += rz[c, i].astype(F32)
        if not gathered:
            dwo[...] = total.astype(BF)
            store(dwo, dwo_out)
            return
        res[c, zh, x] = total.astype(BF)

        def pass_on(at, column, device):
            return send(res.at[c, at, column], res.at[c, at, column], device)

        across = [pass_on(zh, x, dev_z(q[i])) for i in range(3)]
        first, second = [pass_on(zh, x, ahead)], [pass_on(zh, x, back)]
        third = []
        at = (zh, z_at(3), z_at(1), z_at(2))
        for i, come in enumerate((1, 2, 0)):
            yield 3.5 if i == 0 else 0.3
            across[come].wait_recv()
            first.append(pass_on(at[i + 1], x, ahead))
            second.append(pass_on(at[i + 1], x, back))
        for i in range(4):
            yield 0.7
            first[i].wait_recv()
            third.append(pass_on(at[i], xm, ahead))
        yield 4.0
        for copy in second + third:
            copy.wait_recv()
        store(res.at[c], dwqkv_out.at[:, :, :, pl.ds(c * 128, 128)])

    flows = []
    clock = [0.0]

    def start(flow):
        flows.append([clock[0] + next(flow), flow])
        return flow

    def step(item):
        clock[0] = max(clock[0], item[0])
        wait = next(item[1], None)
        if wait is None:
            flows.remove(item)
        else:
            item[0] = clock[0] + wait

    def finish(flow):
        while any(item[1] is flow for item in flows):
            step(min(flows, key=lambda item: item[0]))

    def advance(flow, waits):
        for _ in range(waits):
            step(next(item for item in flows if item[1] is flow))

    def passed(time):
        target = clock[0] + time
        while flows and min(item[0] for item in flows) <= target:
            step(min(flows, key=lambda item: item[0]))
        clock[0] = target

    loads[0].wait()
    flow_x = start(frames_to_patches(x_ref, xb))
    loads[1].wait()
    flow_g = start(frames_to_patches(g_ref, gb))
    loads[2].wait()
    gain[...] = gain_ref[...].astype(F32)
    finish(flow_x)
    gather_x = start(gather(xb))
    finish(flow_g)
    advance(gather_x, 3)
    gather_g = start(gather(gb))
    finish(gather_x)

    def square(m, total):
        block = flat(xb[m]).astype(F32)
        return total + block * block

    squares = lax.fori_loop(0, 16, square, jnp.zeros((256, HEAD), F32))
    mean = jnp.sum(squares, axis=-1, keepdims=True) * (1.0 / 2048)
    inv[...] = jnp.broadcast_to(lax.rsqrt(mean + EPS), (256, HEAD))

    def normalise(m, carry):
        block = flat(xb[m]).astype(F32) * inv[...] * gain[pl.ds(m, 1), :]
        norm[:, pl.ds(pl.multiple_of(m * 128, 128), 128)] = block.astype(BF)
        return carry

    lax.fori_loop(0, 16, normalise, 0, unroll=2)
    passed(1.5)
    for load in loads[3:]:
        load.wait()
    qkv[...] = mm(norm[...], wqkv[...]).astype(BF)
    passed(1.0)

    scale = HEAD ** (-0.5)
    rows = lax.broadcasted_iota(jnp.int32, (256, 256), 0)
    cols = lax.broadcasted_iota(jnp.int32, (256, 256), 1)
    keep = (((rows - cols) & 15) == 0) & (cols <= rows)
    queries, keys, values = (qkv[:, pl.ds(i * 128, 128)] for i in range(3))
    scores = jnp.where(keep, mm_nt(queries, keys) * scale, -1e30)
    expo = jnp.exp(scores - jnp.max(scores, axis=-1, keepdims=True))
    soft = expo / jnp.sum(expo, axis=-1, keepdims=True)
    probs[...] = soft
    attended = mm(soft.astype(BF), values)
    att[...] = attended.astype(BF)
    passed(1.5)

    def out_term(i, carry):
        wide = mm(att[...], wout[:, pl.ds(pl.multiple_of(i * 256, 256), 256)]).astype(BF)
        term1[2 * i] = wide[:, :128]
        term1[2 * i + 1] = wide[:, 128:]
        return carry

    lax.fori_loop(0, 8, out_term, 0, unroll=4)
    passed(1.0)

    def layer_flow():
        yield from scatter_sum(term1, rb1, zs1, zb1)
        los[...] = (flat(xb[mp]).astype(F32) + summed(term1, rb1, zb1)).astype(BF).reshape(
            16, 16, HEAD
        )
        yield 0.1
        yield from patches_to_frames(los, lod)
        store(lod, lo_out)

    start(layer_flow())
    att_t[...] = jnp.transpose(attended).astype(BF)
    probs_t[...] = jnp.transpose(soft).astype(BF)

    def turn(m, carry):
        at = pl.multiple_of(m * 128, 128)
        block = norm[:, pl.ds(at, 128)].astype(F32)
        norm_t[pl.ds(at, 128), :] = jnp.transpose(block).astype(BF)
        return carry

    lax.fori_loop(0, 16, turn, 0, unroll=2)
    finish(gather_g)

    def pair_of(i):
        return jnp.concatenate([flat(gb[2 * i]), flat(gb[2 * i + 1])], axis=1)

    def out_weight(i, carry):
        wide = mm(att_t[...], pair_of(i)).astype(BF)
        wg[3, lax.div(i, 2), 2 * lax.rem(i, 2)] = wide[:, :128]
        wg[3, lax.div(i, 2), 2 * lax.rem(i, 2) + 1] = wide[:, 128:]
        return carry

    lax.fori_loop(0, 8, out_weight, 0, unroll=4)
    start(weight_sum(3, False))
    passed(1.0)
    total = jnp.zeros((256, HEAD), F32)
    for i in range(8):
        total += mm_nt(pair_of(i), wout[:, pl.ds(i * 256, 256)])
    gheads[...] = total.astype(BF)

    def in_weight(c):
        grad = dqkv[:, pl.ds(c * 128, 128)]

        def body(i, carry):
            tall = mm(norm_t[pl.ds(pl.multiple_of(i * 256, 256), 256), :], grad).astype(BF)
            wg[c, lax.div(i, 2), 2 * lax.rem(i, 2)] = tall[:128]
            wg[c, lax.div(i, 2), 2 * lax.rem(i, 2) + 1] = tall[128:]
            return carry

        lax.fori_loop(0, 8, body, 0, unroll=4)
        start(weight_sum(c, True))
        passed(1.5)

    dqkv[:, pl.ds(256, 128)] = mm(probs_t[...], gheads[...]).astype(BF)
    in_weight(2)
    dprobs = mm_nt(gheads[...], qkv[:, pl.ds(256, 128)]).astype(BF).astype(F32)
    soft = probs[...]
    delta = jnp.sum(soft * dprobs, axis=-1, keepdims=True)
    dscores = soft * (dprobs - delta) * scale
    high = dscores.astype(BF)
    low = (dscores - high.astype(F32)).astype(BF)
    keys = qkv[:, pl.ds(128, 128)]
    dqkv[:, pl.ds(0, 128)] = (mm(high, keys) + mm(low, keys)).astype(BF)
    turned = jnp.transpose(dscores)
    high = turned.astype(BF)
    low = (turned - high.astype(F32)).astype(BF)
    queries = qkv[:, pl.ds(0, 128)]
    dqkv[:, pl.ds(128, 128)] = (mm(high, queries) + mm(low, queries)).astype(BF)

    def norm_term(i, total):
        tall = wqkv[pl.ds(pl.multiple_of(i * 256, 256), 256), :]
        wide = mm_nt(dqkv[...], tall).astype(BF)
        for half in (0, 1):
            part = wide[:, half * 128 : half * 128 + 128]
            term2[2 * i + half] = part
            total += gain[pl.ds(2 * i + half, 1), :] * part.astype(F32) * flat(
                xb[2 * i + half]
            ).astype(F32)
        return total

    inner = lax.fori_loop(0, 8, norm_term, jnp.zeros((256, HEAD), F32), unroll=2)
    rowb[mp] = jnp.broadcast_to(jnp.sum(jnp.transpose(inner), axis=0, keepdims=True), (8, 256))
    rows_flow = gather(rowb)

    def input_flow():
        yield from scatter_sum(term2, rb2, zs2, zb2)
        yield from rows_flow
        row = jnp.sum(rowb[...].reshape(16, 8, 256), axis=0)[:1]
        row = jnp.transpose(jnp.broadcast_to(row, (HEAD, 256)))
        grad = summed(term2, rb2, zb2)
        scale_own = inv[...]
        out = (
            flat(gb[mp]).astype(F32)
            + scale_own * gain[pl.ds(mp, 1), :] * grad
            - flat(xb[mp]).astype(F32) * (scale_own * scale_own * scale_own) * row * (1.0 / 2048)
        )
        igs[...] = out.astype(BF).reshape(16, 16, HEAD)
        yield 0.1
        yield from patches_to_frames(igs, igd)
        store(igd, ig_out)

    start(input_flow())
    passed(2.0)
    in_weight(0)
    in_weight(1)
    while flows:
        step(min(flows, key=lambda item: item[0]))

    for copy in started:
        copy.wait_send()
    for copy in stores:
        copy.wait()


def shards(frames_in, norm_gain, w_qkv, w_out, cotangent):
    hbm = pl.BlockSpec(memory_space=pltpu.HBM)

    def bf(*shape):
        return pltpu.VMEM(shape, BF)

    def f32(*shape):
        return pltpu.VMEM(shape, F32)

    scratch = [
        bf(16, 16, HEAD), bf(16, 16, HEAD), bf(16, HEAD),
        bf(16, 16, 16, HEAD), bf(16, 16, 16, HEAD),
        bf(2048, 384), bf(HEAD, 2048),
        f32(16, HEAD), f32(256, HEAD),
        bf(256, 2048), bf(2048, 256),
        bf(256, 384), bf(256, HEAD), bf(HEAD, 256),
        f32(256, 256), bf(256, 256),
        bf(256, HEAD), bf(256, 384),
        bf(16, 256, HEAD), bf(16, 256, HEAD),
        bf(14, 256, HEAD), bf(14, 256, HEAD),
        bf(256, HEAD), bf(256, HEAD), bf(256, HEAD), bf(256, HEAD),
        f32(16, 8, 256),
        bf(4, 4, 4, HEAD, HEAD),
        bf(4, 4, HEAD, HEAD), bf(4, 4, HEAD, HEAD),
        bf(4, 4, HEAD, HEAD), bf(4, 3, HEAD, HEAD), bf(4, 3, HEAD, HEAD),
        bf(3, 4, 4, HEAD, HEAD), bf(HEAD, HEAD),
        bf(16, 16, HEAD), bf(16, 16, HEAD), bf(16, 16, HEAD), bf(16, 16, HEAD),
        pltpu.SemaphoreType.DMA((COPIES,)),
        pltpu.SemaphoreType.DMA((COPIES,)),
        pltpu.SemaphoreType.DMA((14,)),
    ]
    layer_out, input_grad, qkv_weight_grad, out_weight_grad = pl.pallas_call(
        kernel,
        out_shape=(
            jax.ShapeDtypeStruct((16, 16, HEAD), BF),
            jax.ShapeDtypeStruct((16, 16, HEAD), BF),
            jax.ShapeDtypeStruct((4, 4, HEAD, 384), BF),
            jax.ShapeDtypeStruct((HEAD, HEAD), BF),
        ),
        in_specs=[hbm] * 5,
        out_specs=(hbm, hbm, hbm, hbm),
        scratch_shapes=scratch,
        compiler_params=pltpu.CompilerParams(
            collective_id=0, has_side_effects=True, vmem_limit_bytes=56 * 1024 * 1024
        ),
        name="sublayer",
    )(
        frames_in.reshape(16, 16, HEAD),
        norm_gain.reshape(16, HEAD),
        w_qkv,
        w_out,
        cotangent.reshape(16, 16, HEAD),
    )
    return (
        layer_out.reshape(1, 256, HEAD),
        input_grad.reshape(1, 256, HEAD),
        qkv_weight_grad.reshape(2048, 384),
        out_weight_grad,
    )


def solution(mesh):
    return jax.shard_map(
        shards,
        mesh=mesh,
        in_specs=(
            P(("clip", "seq"), None, "mp"),
            P(),
            P(None, "mp"),
            P("mp", None),
            P(("clip", "seq"), None, "mp"),
        ),
        out_specs=(
            P(("clip", "seq"), None, "mp"),
            P(("clip", "seq"), None, "mp"),
            P("clip", "mp"),
            P(("clip", "mp"), "seq"),
        ),
        check_vma=False,
    )
```

```python
import jax
import jax.numpy as jnp
from jax import lax
from jax.experimental import pallas as pl
from jax.experimental.pallas import tpu as pltpu
from jax.sharding import PartitionSpec as P

HEAD = 128
EPS = 1e-05
BF = jnp.bfloat16
F32 = jnp.float32
MESH = pl.DeviceIdType.MESH
COPIES = 92
ROWS = 544
SCALE = HEAD ** (-0.5)
NT = (((1,), (1,)), ((), ()))


def mm(a, b):
    return jnp.dot(a, b, preferred_element_type=F32)


def mm_nt(a, b):
    return lax.dot_general(a, b, NT, preferred_element_type=F32)


def mm_tn(a, b):
    return lax.dot_general(a, b, (((0,), (0,)), ((), ())), preferred_element_type=F32)


class Net:
    def __init__(self, ssem, rsem):
        self.ssem, self.rsem, self.started, self.flows, self.clock = ssem, rsem, [], [], 0.0
        clip, seq, mp = lax.axis_index("clip"), lax.axis_index("seq"), lax.axis_index("mp")
        self.clip, self.seq, self.mp = clip, seq, mp
        self.zh, self.x = seq // 4, seq & 3
        self.zl, self.y = mp // 8, mp & 7
        self.e = 1 - 2 * clip
        self.zp = 1 - self.zl
        self.dev_pair = (clip, seq, self.zp * 8 + self.y)
        barrier = pltpu.get_barrier_semaphore()
        peers = [self.dev_x(self.x_at(s)) for s in (1, 2, 3)]
        peers += [self.dev_z(self.z_at(s)) for s in (1, 2, 3)]
        peers += [self.dev_y(self.y_at(s)) for s in (1, -1, 2, -2)] + [self.dev_pair]
        for peer in peers:
            pl.semaphore_signal(barrier, inc=1, device_id=peer, device_id_type=MESH)
        pl.semaphore_wait(barrier, len(peers))

    def x_at(self, step):
        return (self.x + step) & 3

    def z_at(self, step):
        return (self.zh + step) & 3

    def y_at(self, step):
        return (self.y + step) & 7

    def dev_x(self, to):
        return (self.clip, self.zh * 4 + to, self.mp)

    def dev_z(self, to):
        return (self.clip, to * 4 + self.x, self.mp)

    def dev_y(self, to):
        return (self.clip, self.seq, self.zl * 8 + to)

    def send(self, src, dst, device):
        at = len(self.started)
        copy = pltpu.make_async_remote_copy(
            src_ref=src,
            dst_ref=dst,
            send_sem=self.ssem.at[at],
            recv_sem=self.rsem.at[at],
            device_id=device,
            device_id_type=MESH,
        )
        copy.start()
        self.started.append(copy)
        return copy

    def start(self, flow):
        self.flows.append([self.clock + next(flow), flow])
        return flow

    def step(self):
        item = min(self.flows, key=lambda entry: entry[0])
        self.clock = max(self.clock, item[0])
        wait = next(item[1], None)
        if wait is None:
            self.flows.remove(item)
        else:
            item[0] = self.clock + wait

    def only(self, flow):
        item = next(entry for entry in self.flows if entry[1] is flow)
        self.clock = max(self.clock, item[0])
        item[0] = self.clock + next(flow)

    def finish(self, flow=None):
        while any(flow is None or item[1] is flow for item in self.flows):
            self.step()

    def passed(self, time):
        target = self.clock + time
        while self.flows and min(item[0] for item in self.flows) <= target:
            self.step()
        self.clock = target

    def close(self):
        for copy in self.started:
            copy.wait_send()

    def frames_to_patches(self, src, mid, xb, gb):
        zh, x, mp = self.zh, self.x, self.mp
        sent = []
        for s in (1, 3, 2):
            to = self.x_at(s)
            sent.append(self.send(src.at[:, to], mid.at[x], self.dev_x(to)))
        mid[x] = src[:, x]
        yield 3.0
        for copy in sent:
            copy.wait_recv()
        sent = []
        for half, dst in ((0, xb), (1, gb)):
            for s in (1, 3, 2):
                to = self.z_at(s)
                sent.append(self.send(mid.at[:, to, half], dst.at[mp, zh], self.dev_z(to)))
            dst[mp, zh] = mid[:, zh, half]
        for some in (sent[:3], sent[3:]):
            yield 3.0
            for copy in some:
                copy.wait_recv()

    def patches_to_frames(self, src, mid, dst):
        zh, x = self.zh, self.x
        sent = []
        for s in (1, 3, 2):
            to = self.z_at(s)
            sent.append(self.send(src.at[to], mid.at[zh], self.dev_z(to)))
        mid[zh] = src[zh]
        yield 3.0
        for copy in sent:
            copy.wait_recv()
        sent = []
        for s in (1, 3, 2):
            to = self.x_at(s)
            sent.append(self.send(mid.at[:, to], dst.at[:, x], self.dev_x(to)))
        dst[:, x] = mid[:, x]
        yield 3.0
        for copy in sent:
            copy.wait_recv()

    def gather(self, buf):
        def pass_on(block, device):
            return self.send(buf.at[block], buf.at[block], device)

        def own(step):
            return self.zl * 8 + self.y_at(step)

        def other(step):
            return self.zp * 8 + self.y_at(step)

        ahead, back, ahead_2, back_2 = (self.dev_y(self.y_at(s)) for s in (self.e, -self.e, 2 * self.e, -2 * self.e))
        a2 = pass_on(self.mp, ahead_2)
        b2 = pass_on(self.mp, back_2)
        pair = [pass_on(self.mp, self.dev_pair)]
        a1 = pass_on(self.mp, ahead)
        b1 = pass_on(self.mp, back)
        yield 4.0
        a2.wait_recv()
        a4 = pass_on(own(-2 * self.e), ahead_2)
        a3 = pass_on(own(-2 * self.e), ahead)
        pair.append(pass_on(own(-2 * self.e), self.dev_pair))
        yield 0.1
        b2.wait_recv()
        b3 = pass_on(own(2 * self.e), back)
        pair.append(pass_on(own(2 * self.e), self.dev_pair))
        yield 0.5
        pair[0].wait_recv()
        c1 = pass_on(other(0), ahead)
        d1 = pass_on(other(0), back)
        yield 0.5
        a1.wait_recv()
        b1.wait_recv()
        yield 3.0
        a3.wait_recv()
        pair.append(pass_on(own(-3 * self.e), self.dev_pair))
        yield 0.1
        b3.wait_recv()
        pair.append(pass_on(own(3 * self.e), self.dev_pair))
        yield 1.0
        a4.wait_recv()
        pair.append(pass_on(own(-4 * self.e), self.dev_pair))
        yield 0.2
        c1.wait_recv()
        d1.wait_recv()
        for copy in pair[1:]:
            yield 1.0
            copy.wait_recv()

    def scatter_sum(self, term, rb, zs, zb):
        planes = (self.zp, self.zl)
        ways = ((self.e, 4), (-self.e, 3))
        order = [(i, j) for i in (0, 1) for j in (0, 1)]

        def slot(i, j, k):
            return i * 7 + j * 4 + k - 1

        sent = {}
        for i, j in order:
            way, steps = ways[j]
            dest = planes[i] * 8 + self.y_at(steps * way)
            sent[i, j] = self.send(term.at[dest], rb.at[slot(i, j, 1)], self.dev_y(self.y_at(way)))
        last = None
        for k in (1, 2, 3, 4):
            for i, j in order:
                way, steps = ways[j]
                if k > steps:
                    continue
                yield 5.0 if (i, j) == (0, 0) else 0.6
                sent[i, j].wait_recv()
                here = rb.at[slot(i, j, k)]
                if k < steps:
                    dest = planes[i] * 8 + self.y_at((steps - k) * way)
                    fold(here, here[...].astype(F32) + term[dest].astype(F32))
                    after = rb.at[slot(i, j, k + 1)]
                    sent[i, j] = self.send(here, after, self.dev_y(self.y_at(way)))
                elif k == 4 and i == 0:
                    fold(zs, self.received(term, rb, 0, self.zp))
                    last = self.send(zs, zb, self.dev_pair)
        yield 3.0
        last.wait_recv()

    def received(self, term, rb, i, plane):
        return (
            term[plane * 8 + self.y].astype(F32)
            + rb[7 * i + 3].astype(F32)
            + rb[7 * i + 6].astype(F32)
        )

    def weight_sum(self, piece, wg, tx, px, mx, sx, tz, pz, mz, res, dwo, done):
        zh, x, e = self.zh, self.x, self.e
        xp, xm, zm = self.x_at(e), self.x_at(-e), self.z_at(-e)
        ahead, back = self.dev_x(xp), self.dev_x(xm)
        z_ahead, z_back = self.dev_z(self.z_at(e)), self.dev_z(zm)
        q = (self.z_at(2), self.z_at(e), zm, zh)
        far, plain, near = [], [], []

        def here(i):
            return wg[q[i], x].astype(F32) + px[i].astype(F32) + mx[i].astype(F32)

        for i in range(4):
            piece(q[i])
            far.append(self.send(wg.at[q[i], self.x_at(2)], tx.at[i], ahead))
            plain.append(self.send(wg.at[q[i], xm], px.at[i], back))
            if i < 3:
                yield 0.8
        for i in range(4):
            yield 3.0
            far[i].wait_recv()
            tx[i] = (tx[i].astype(F32) + wg[q[i], xp].astype(F32)).astype(BF)
            near.append(self.send(tx.at[i], mx.at[i], ahead))
        yield 2.0
        plain[0].wait_recv()
        near[0].wait_recv()
        sx[0] = here(0).astype(BF)
        z_far = self.send(sx.at[0], tz, z_ahead)
        for i in (1, 2):
            yield 1.5
            plain[i].wait_recv()
            near[i].wait_recv()
        sx[1] = here(2).astype(BF)
        z_plain = self.send(sx.at[1], pz, z_back)
        yield 1.0
        z_far.wait_recv()
        tz[...] = (tz[...].astype(F32) + here(1)).astype(BF)
        z_near = self.send(tz, mz, z_ahead)
        yield 2.0
        plain[3].wait_recv()
        near[3].wait_recv()
        yield 3.0
        z_plain.wait_recv()
        z_near.wait_recv()
        total = (here(3) + pz[...].astype(F32) + mz[...].astype(F32)).astype(BF)
        res[zh, x] = total[:3]

        def pass_on(at, column, device):
            return self.send(res.at[at, column], res.at[at, column], device)

        up, down = pass_on(zh, x, z_ahead), pass_on(zh, x, z_back)
        first, second, third = [pass_on(zh, x, ahead)], [pass_on(zh, x, back)], []
        dwo[...] = total[3]
        yield 4.0
        up.wait_recv()
        up = pass_on(zm, x, z_ahead)
        first.append(pass_on(zm, x, ahead))
        second.append(pass_on(zm, x, back))
        yield 0.2
        down.wait_recv()
        first.append(pass_on(q[1], x, ahead))
        second.append(pass_on(q[1], x, back))
        yield 0.5
        first[0].wait_recv()
        third.append(pass_on(zh, xm, ahead))
        yield 2.0
        up.wait_recv()
        first.append(pass_on(q[0], x, ahead))
        second.append(pass_on(q[0], x, back))
        for i, at in ((1, zm), (2, q[1]), (3, q[0])):
            yield 2.0
            first[i].wait_recv()
            third.append(pass_on(at, xm, ahead))
        for copy in second + third:
            yield 1.0
            copy.wait_recv()
        done()


def flat(block):
    return block.reshape(256, HEAD)


def fold(ref, total):
    inner = total[512:528] + total[528:544]
    high = inner.astype(BF)
    ref[pl.ds(0, 512)] = total[:512].astype(BF)
    ref[pl.ds(512, 16)] = high
    ref[pl.ds(528, 16)] = (inner - high.astype(F32)).astype(BF)


def kernel(
    x_hbm, gain_hbm, wqkv_hbm, wout_hbm, g_hbm,
    lo_out, ig_out, dwqkv_out, dwo_out,
    both, mid, gain_ref, xb, gb, wqkv, wout, gain, inv, norm, norm_t, qkv, att, att_t,
    probs, probs_t, gheads, dqkv, term, rb, zs, zb,
    wg, tx, px, mx, sx, tz, pz, mz, res, dwo, done_both, back_mid, back_both,
    ssem, rsem, lsem,
):
    loads = [
        pltpu.make_async_copy(src, dst, lsem.at[at])
        for at, (src, dst) in enumerate(
            [
                (x_hbm, both.at[:, :, 0]),
                (g_hbm, both.at[:, :, 1]),
                (gain_hbm, gain_ref),
                (wqkv_hbm, wqkv),
                (wout_hbm, wout),
            ]
        )
    ]
    for load in loads:
        load.start()
    stores = []

    def store(src, dst):
        stores.append(pltpu.make_async_copy(src, dst, lsem.at[len(loads) + len(stores)]))
        stores[-1].start()

    net = Net(ssem, rsem)
    mp = net.mp

    for load in loads[:3]:
        load.wait()
    bring = net.start(net.frames_to_patches(both, mid, xb, gb))
    gain[...] = gain_ref[...].astype(F32)
    net.step()
    net.step()
    gather_x = net.start(net.gather(xb))
    net.finish(bring)
    for _ in range(3):
        net.only(gather_x)
    gather_g = net.start(net.gather(gb))
    net.finish(gather_x)

    def square(m, total):
        block = flat(xb[m]).astype(F32)
        return total + block * block

    squares = lax.fori_loop(0, 16, square, jnp.zeros((256, HEAD), F32))
    mean = jnp.sum(squares, axis=-1, keepdims=True) * (1.0 / 2048)
    inv[...] = jnp.broadcast_to(lax.rsqrt(mean + EPS), (256, HEAD))

    def normalise(m, carry):
        block = flat(xb[m]).astype(F32) * inv[...] * gain[pl.ds(m, 1), :]
        norm[:, pl.ds(pl.multiple_of(m * 128, 128), 128)] = block.astype(BF)
        return carry

    lax.fori_loop(0, 16, normalise, 0, unroll=2)
    net.passed(1.5)
    for load in loads[3:]:
        load.wait()
    qkv[...] = mm(norm[...], wqkv[...]).astype(BF)
    net.passed(1.0)

    scale = HEAD ** (-0.5)
    rows = lax.broadcasted_iota(jnp.int32, (256, 256), 0)
    cols = lax.broadcasted_iota(jnp.int32, (256, 256), 1)
    keep = (((rows - cols) & 15) == 0) & (cols <= rows)
    queries, keys, values = (qkv[:, pl.ds(i * 128, 128)] for i in range(3))
    scores = jnp.where(keep, mm_nt(queries, keys) * scale, -1e30)
    expo = jnp.exp(scores - jnp.max(scores, axis=-1, keepdims=True))
    soft = expo / jnp.sum(expo, axis=-1, keepdims=True)
    probs[...] = soft
    attended = mm(soft.astype(BF), values)
    att[...] = attended.astype(BF)
    net.passed(1.5)

    def out_term(i, carry):
        wide = mm(att[...], wout[:, pl.ds(pl.multiple_of(i * 256, 256), 256)]).astype(BF)
        term[2 * i, pl.ds(0, 256)] = wide[:, :128]
        term[2 * i + 1, pl.ds(0, 256)] = wide[:, 128:]
        return carry

    lax.fori_loop(0, 8, out_term, 0, unroll=4)
    net.passed(1.0)

    att_t[...] = jnp.transpose(attended).astype(BF)
    probs_t[...] = jnp.transpose(soft).astype(BF)

    def turn(m, carry):
        at = pl.multiple_of(m * 128, 128)
        block = norm[:, pl.ds(at, 128)].astype(F32)
        norm_t[pl.ds(at, 128), :] = jnp.transpose(block).astype(BF)
        return carry

    lax.fori_loop(0, 16, turn, 0, unroll=2)
    net.finish(gather_g)

    def pair_of(i):
        return jnp.concatenate([flat(gb[2 * i]), flat(gb[2 * i + 1])], axis=1)

    total = jnp.zeros((256, HEAD), F32)
    for i in range(8):
        total += mm_nt(pair_of(i), wout[:, pl.ds(i * 256, 256)])
    gheads[...] = total.astype(BF)

    dqkv[:, pl.ds(256, 128)] = mm(probs_t[...], gheads[...]).astype(BF)
    dprobs = mm_nt(gheads[...], qkv[:, pl.ds(256, 128)]).astype(BF).astype(F32)
    soft = probs[...]
    delta = jnp.sum(soft * dprobs, axis=-1, keepdims=True)
    dscores = soft * (dprobs - delta) * scale
    high = dscores.astype(BF)
    low = (dscores - high.astype(F32)).astype(BF)
    keys = qkv[:, pl.ds(128, 128)]
    dqkv[:, pl.ds(0, 128)] = (mm(high, keys) + mm(low, keys)).astype(BF)
    turned = jnp.transpose(dscores)
    high = turned.astype(BF)
    low = (turned - high.astype(F32)).astype(BF)
    queries = qkv[:, pl.ds(0, 128)]
    dqkv[:, pl.ds(128, 128)] = (mm(high, queries) + mm(low, queries)).astype(BF)

    def piece(q):
        for half in range(2):
            at = q * 4 + half * 2
            rows = norm_t[pl.ds(pl.multiple_of(at * 128, 256), 256), :]
            tall = mm(rows, dqkv[...]).astype(BF)
            wide = mm(att_t[...], jnp.concatenate([flat(gb[at]), flat(gb[at + 1])], axis=1)).astype(BF)
            for k in range(2):
                for c in range(3):
                    wg[q, 2 * half + k, c] = tall[k * 128 : k * 128 + 128, c * 128 : c * 128 + 128]
                wg[q, 2 * half + k, 3] = wide[:, k * 128 : k * 128 + 128]

    def stored():
        for c in range(3):
            store(res.at[:, :, c], dwqkv_out.at[:, :, :, pl.ds(c * 128, 128)])
        store(dwo, dwo_out)

    net.start(net.weight_sum(piece, wg, tx, px, mx, sx, tz, pz, mz, res, dwo, stored))
    net.passed(1.0)

    def norm_term(i, total):
        tall = wqkv[pl.ds(pl.multiple_of(i * 256, 256), 256), :]
        wide = mm_nt(dqkv[...], tall).astype(BF)
        for half in (0, 1):
            part = wide[:, half * 128 : half * 128 + 128]
            term[2 * i + half, pl.ds(256, 256)] = part
            total += gain[pl.ds(2 * i + half, 1), :] * part.astype(F32) * flat(
                xb[2 * i + half]
            ).astype(F32)
        return total

    inner = lax.fori_loop(0, 8, norm_term, jnp.zeros((256, HEAD), F32), unroll=2)
    inner = jnp.sum(jnp.transpose(inner), axis=0, keepdims=True)
    at_row = lax.broadcasted_iota(jnp.int32, (16, HEAD), 0)
    inner = jnp.where(at_row == 0, inner[:, :128], jnp.where(at_row == 1, inner[:, 128:], 0.0))
    high = inner.astype(BF)
    low = (inner - high.astype(F32)).astype(BF)
    for m in range(16):
        term[m, pl.ds(512, 16)] = high
        term[m, pl.ds(528, 16)] = low

    def token_flow():
        yield from net.scatter_sum(term, rb, zs, zb)
        total = net.received(term, rb, 1, net.zl) + zb[...].astype(F32)
        local = flat(xb[mp]).astype(F32)
        done_both[:, :, 0] = (local + total[:256]).astype(BF).reshape(4, 4, 16, HEAD)
        rows = total[512:528] + total[528:544]
        rows = jnp.concatenate(
            [jnp.transpose(jnp.broadcast_to(rows[k : k + 1], (HEAD, HEAD))) for k in (0, 1)], axis=0
        )
        scale_own = inv[...]
        grad = (
            flat(gb[mp]).astype(F32)
            + scale_own * gain[pl.ds(mp, 1), :] * total[256:512]
            - local * (scale_own * scale_own * scale_own) * rows * (1.0 / 2048)
        )
        done_both[:, :, 1] = grad.astype(BF).reshape(4, 4, 16, HEAD)
        yield 0.1
        yield from net.patches_to_frames(done_both, back_mid, back_both)
        store(back_both.at[:, :, 0], lo_out)
        store(back_both.at[:, :, 1], ig_out)

    net.start(token_flow())
    net.finish()
    net.close()
    for copy in stores:
        copy.wait()


def bf(*shape):
    return pltpu.VMEM(shape, BF)


def f32(*shape):
    return pltpu.VMEM(shape, F32)


def shards(frames_in, norm_gain, w_qkv, w_out, cotangent):
    hbm = pl.BlockSpec(memory_space=pltpu.HBM)
    block = (4, 4, 16, HEAD)
    scratch = [
        bf(4, 4, 2, 16, HEAD), bf(4, 4, 2, 16, HEAD), bf(16, HEAD),
        bf(16, *block), bf(16, *block),
        bf(2048, 384), bf(HEAD, 2048),
        f32(16, HEAD), f32(256, HEAD),
        bf(256, 2048), bf(2048, 256),
        bf(256, 384), bf(256, HEAD), bf(HEAD, 256),
        f32(256, 256), bf(256, 256),
        bf(256, HEAD), bf(256, 384),
        bf(16, ROWS, HEAD), bf(14, ROWS, HEAD), bf(ROWS, HEAD), bf(ROWS, HEAD),
        bf(4, 4, 4, HEAD, HEAD),
        bf(4, 4, HEAD, HEAD), bf(4, 4, HEAD, HEAD), bf(4, 4, HEAD, HEAD),
        bf(2, 4, HEAD, HEAD),
        bf(4, HEAD, HEAD), bf(4, HEAD, HEAD), bf(4, HEAD, HEAD),
        bf(4, 4, 3, HEAD, HEAD), bf(HEAD, HEAD),
        bf(4, 4, 2, 16, HEAD), bf(4, 4, 2, 16, HEAD), bf(4, 4, 2, 16, HEAD),
        pltpu.SemaphoreType.DMA((COPIES,)),
        pltpu.SemaphoreType.DMA((COPIES,)),
        pltpu.SemaphoreType.DMA((11,)),
    ]
    layer_out, input_grad, qkv_weight_grad, out_weight_grad = pl.pallas_call(
        kernel,
        out_shape=(
            jax.ShapeDtypeStruct(block, BF),
            jax.ShapeDtypeStruct(block, BF),
            jax.ShapeDtypeStruct((4, 4, HEAD, 384), BF),
            jax.ShapeDtypeStruct((HEAD, HEAD), BF),
        ),
        in_specs=[hbm] * 5,
        out_specs=(hbm,) * 4,
        scratch_shapes=scratch,
        compiler_params=pltpu.CompilerParams(
            collective_id=0, has_side_effects=True, vmem_limit_bytes=56 * 1024 * 1024
        ),
        name="sublayer",
    )(frames_in.reshape(block), norm_gain.reshape(16, HEAD), w_qkv, w_out, cotangent.reshape(block))
    return (
        layer_out.reshape(1, 256, HEAD),
        input_grad.reshape(1, 256, HEAD),
        qkv_weight_grad.reshape(2048, 384),
        out_weight_grad,
    )


def solution(mesh):
    return jax.shard_map(
        shards,
        mesh=mesh,
        in_specs=(
            P(("clip", "seq"), None, "mp"),
            P(),
            P(None, "mp"),
            P("mp", None),
            P(("clip", "seq"), None, "mp"),
        ),
        out_specs=(
            P(("clip", "seq"), None, "mp"),
            P(("clip", "seq"), None, "mp"),
            P("clip", "mp"),
            P(("clip", "mp"), "seq"),
        ),
        check_vma=False,
    )
```

```python
import jax
import jax.numpy as jnp
from jax import lax
from jax.experimental import pallas as pl
from jax.experimental.pallas import tpu as pltpu
from jax.sharding import PartitionSpec as P

HEAD = 128
EPS = 1e-05
BF = jnp.bfloat16
F32 = jnp.float32
MESH = pl.DeviceIdType.MESH
COPIES = 106
ROWS = 288
SCALE = HEAD ** (-0.5)
NT = (((1,), (1,)), ((), ()))


def mm(a, b):
    return jnp.dot(a, b, preferred_element_type=F32)


def mm_nt(a, b):
    return lax.dot_general(a, b, NT, preferred_element_type=F32)


def mm_tn(a, b):
    return lax.dot_general(a, b, (((0,), (0,)), ((), ())), preferred_element_type=F32)


class Net:
    def __init__(self, ssem, rsem):
        self.ssem, self.rsem, self.started, self.flows, self.clock, self.steps = ssem, rsem, [], [], 0.0, {}
        clip, seq, mp = lax.axis_index("clip"), lax.axis_index("seq"), lax.axis_index("mp")
        self.clip, self.seq, self.mp = clip, seq, mp
        self.zh, self.x = seq // 4, seq & 3
        self.zl, self.y = mp // 8, mp & 7
        self.e = 1 - 2 * clip
        self.zp = 1 - self.zl
        self.dev_pair = (clip, seq, self.zp * 8 + self.y)
        barrier = pltpu.get_barrier_semaphore()
        peers = [self.dev_x(self.x_at(s)) for s in (1, 2, 3)]
        peers += [self.dev_z(self.z_at(s)) for s in (1, 2, 3)]
        peers += [self.dev_y(self.y_at(s)) for s in (1, -1, 2, -2)] + [self.dev_pair]
        for peer in peers:
            pl.semaphore_signal(barrier, inc=1, device_id=peer, device_id_type=MESH)
        pl.semaphore_wait(barrier, len(peers))

    def x_at(self, step):
        return (self.x + step) & 3

    def z_at(self, step):
        return (self.zh + step) & 3

    def y_at(self, step):
        return (self.y + step) & 7

    def dev_x(self, to):
        return (self.clip, self.zh * 4 + to, self.mp)

    def dev_z(self, to):
        return (self.clip, to * 4 + self.x, self.mp)

    def dev_y(self, to):
        return (self.clip, self.seq, self.zl * 8 + to)

    def send(self, src, dst, device):
        at = len(self.started)
        copy = pltpu.make_async_remote_copy(
            src_ref=src,
            dst_ref=dst,
            send_sem=self.ssem.at[at],
            recv_sem=self.rsem.at[at],
            device_id=device,
            device_id_type=MESH,
        )
        copy.start()
        self.started.append(copy)
        return copy

    def start(self, flow):
        self.flows.append([self.clock + next(flow), flow])
        return flow

    def step(self, item=None):
        item = item or min(self.flows, key=lambda entry: entry[0])
        self.clock = max(self.clock, item[0])
        wait = next(item[1], None)
        self.steps[id(item[1])] = self.steps.get(id(item[1]), 0) + 1
        if wait is None:
            self.flows.remove(item)
        else:
            item[0] = self.clock + wait

    def until(self, flow, steps):
        while self.steps.get(id(flow), 0) < steps:
            self.step(next(entry for entry in self.flows if entry[1] is flow))

    def finish(self, flow=None):
        while any(flow is None or item[1] is flow for item in self.flows):
            self.step()

    def passed(self, time):
        target = self.clock + time
        while self.flows and min(item[0] for item in self.flows) <= target:
            self.step()
        self.clock = target

    def close(self):
        for copy in self.started:
            copy.wait_send()

    def frames_to_patches(self, src, mid, xb, gb):
        zh, x, mp = self.zh, self.x, self.mp
        sent = []
        for s in (1, 3, 2):
            to = self.x_at(s)
            sent.append(self.send(src.at[:, to], mid.at[x], self.dev_x(to)))
        mid[x] = src[:, x]
        yield 3.0
        for copy in sent:
            copy.wait_recv()
        sent = []
        for half, dst in ((0, xb), (1, gb)):
            for s in (1, 3, 2):
                to = self.z_at(s)
                sent.append(self.send(mid.at[:, to, half], dst.at[mp, zh], self.dev_z(to)))
            dst[mp, zh] = mid[:, zh, half]
        for some in (sent[:3], sent[3:]):
            yield 3.0
            for copy in some:
                copy.wait_recv()

    def patches_to_frames(self, src, mid, dst):
        zh, x = self.zh, self.x
        sent = []
        for s in (1, 3, 2):
            to = self.z_at(s)
            sent.append(self.send(src.at[to], mid.at[zh], self.dev_z(to)))
        mid[zh] = src[zh]
        yield 3.0
        for copy in sent:
            copy.wait_recv()
        sent = []
        for s in (1, 3, 2):
            to = self.x_at(s)
            sent.append(self.send(mid.at[:, to], dst.at[:, x], self.dev_x(to)))
        dst[:, x] = mid[:, x]
        yield 3.0
        for copy in sent:
            copy.wait_recv()

    def gather(self, buf):
        def pass_on(block, device):
            return self.send(buf.at[block], buf.at[block], device)

        def own(step):
            return self.zl * 8 + self.y_at(step)

        def other(step):
            return self.zp * 8 + self.y_at(step)

        ahead, back, ahead_2, back_2 = (self.dev_y(self.y_at(s)) for s in (self.e, -self.e, 2 * self.e, -2 * self.e))
        a2 = pass_on(self.mp, ahead_2)
        b2 = pass_on(self.mp, back_2)
        pair = [pass_on(self.mp, self.dev_pair)]
        a1 = pass_on(self.mp, ahead)
        b1 = pass_on(self.mp, back)
        yield 4.0
        a2.wait_recv()
        a4 = pass_on(own(-2 * self.e), ahead_2)
        a3 = pass_on(own(-2 * self.e), ahead)
        pair.append(pass_on(own(-2 * self.e), self.dev_pair))
        yield 0.1
        b2.wait_recv()
        b3 = pass_on(own(2 * self.e), back)
        pair.append(pass_on(own(2 * self.e), self.dev_pair))
        yield 0.5
        pair[0].wait_recv()
        c1 = pass_on(other(0), ahead)
        d1 = pass_on(other(0), back)
        yield 0.5
        a1.wait_recv()
        b1.wait_recv()
        yield 3.0
        a3.wait_recv()
        pair.append(pass_on(own(-3 * self.e), self.dev_pair))
        yield 0.1
        b3.wait_recv()
        pair.append(pass_on(own(3 * self.e), self.dev_pair))
        yield 1.0
        a4.wait_recv()
        pair.append(pass_on(own(-4 * self.e), self.dev_pair))
        yield 0.2
        c1.wait_recv()
        d1.wait_recv()
        for copy in pair[1:]:
            yield 1.0
            copy.wait_recv()

    def scatter_sum(self, term, rb, zs, zb):
        planes = (self.zp, self.zl)

        def share(i, step):
            return term[planes[i] * 8 + self.y_at(step)].astype(F32)

        def push(i, step, slot, hop):
            return self.send(term.at[planes[i] * 8 + self.y_at(step)], rb.at[7 * i + slot], self.dev_y(self.y_at(hop)))

        a1, b1, a2, b2, a3, b3, a4 = ({} for _ in range(7))
        for i in (0, 1):
            a4[i] = push(i, 4, 0, 2 * self.e)
            a3[i] = push(i, 3 * self.e, 3, self.e)
            b3[i] = push(i, -3 * self.e, 6, -self.e)
        for i in (0, 1):
            a1[i] = push(i, self.e, 1, self.e)
            b1[i] = push(i, -self.e, 4, -self.e)
        for i in (0, 1):
            yield 4.0 if i == 0 else 1.0
            b3[i].wait_recv()
            far = rb.at[7 * i + 6]
            fold(far, far[...].astype(F32) + share(i, -2 * self.e))
            b2[i] = self.send(far, rb.at[7 * i + 5], self.dev_y(self.y_at(-2 * self.e)))
            yield 0.2
            a3[i].wait_recv()
            a4[i].wait_recv()
            far = rb.at[7 * i + 3]
            fold(far, far[...].astype(F32) + rb[7 * i].astype(F32) + share(i, 2 * self.e))
            a2[i] = self.send(far, rb.at[7 * i + 2], self.dev_y(self.y_at(2 * self.e)))
        last = None
        for i in (0, 1):
            yield 4.0 if i == 0 else 1.5
            for copy in (a1[i], b1[i], a2[i], b2[i]):
                copy.wait_recv()
            if i == 0:
                fold(zs, self.received(term, rb, 0, self.zp))
                last = self.send(zs, zb, self.dev_pair)
        yield 2.5
        last.wait_recv()

    def received(self, term, rb, i, plane):
        total = term[plane * 8 + self.y].astype(F32)
        for slot in (1, 2, 4, 5):
            total += rb[7 * i + slot].astype(F32)
        return total

    def weight_sum(self, piece, wg, tx, px, mx, sx, tz, pz, mz, res, dwo, done):
        zh, x, e = self.zh, self.x, self.e
        xp, xm, zm = self.x_at(e), self.x_at(-e), self.z_at(-e)
        ahead, back = self.dev_x(xp), self.dev_x(xm)
        z_ahead, z_back = self.dev_z(self.z_at(e)), self.dev_z(zm)
        q = (self.z_at(2), self.z_at(e), zm, zh)
        far, plain, near = [], [], []

        def here(i):
            return wg[q[i], x].astype(F32) + px[i].astype(F32) + mx[i].astype(F32)

        for i in range(4):
            piece(q[i])
            far.append(self.send(wg.at[q[i], self.x_at(2)], tx.at[i], ahead))
            plain.append(self.send(wg.at[q[i], xm], px.at[i], back))
            if i < 3:
                yield 0.8
        for i in range(4):
            yield 3.0
            far[i].wait_recv()
            tx[i] = (tx[i].astype(F32) + wg[q[i], xp].astype(F32)).astype(BF)
            near.append(self.send(tx.at[i], mx.at[i], ahead))
        yield 2.0
        plain[0].wait_recv()
        near[0].wait_recv()
        sx[0] = here(0).astype(BF)
        z_far = self.send(sx.at[0], tz, z_ahead)
        for i in (1, 2):
            yield 1.5
            plain[i].wait_recv()
            near[i].wait_recv()
        sx[1] = here(2).astype(BF)
        z_plain = self.send(sx.at[1], pz, z_back)
        yield 1.0
        z_far.wait_recv()
        tz[...] = (tz[...].astype(F32) + here(1)).astype(BF)
        z_near = self.send(tz, mz, z_ahead)
        yield 2.0
        plain[3].wait_recv()
        near[3].wait_recv()
        yield 3.0
        z_plain.wait_recv()
        z_near.wait_recv()
        total = (here(3) + pz[...].astype(F32) + mz[...].astype(F32)).astype(BF)
        res[zh, x] = total[:3]

        def pass_on(at, column, device):
            return self.send(res.at[at, column], res.at[at, column], device)

        across = [pass_on(zh, x, self.dev_z(self.z_at(s))) for s in (2, 1, 3)]
        at = (zh, self.z_at(3), self.z_at(1), self.z_at(2))
        first, second, third = [pass_on(zh, x, ahead)], [pass_on(zh, x, back)], []
        dwo[...] = total[3]
        for i, come in enumerate((1, 2, 0)):
            yield 4.0 if i == 0 else 0.5
            across[come].wait_recv()
            first.append(pass_on(at[i + 1], x, ahead))
            second.append(pass_on(at[i + 1], x, back))
        for i in range(4):
            yield 0.5 if i == 0 else 2.0
            first[i].wait_recv()
            third.append(pass_on(at[i], xm, ahead))
        for copy in second + third:
            yield 1.0
            copy.wait_recv()
        done()


def flat(block):
    return block.reshape(256, HEAD)


def fold(ref, total):
    ref[pl.ds(0, 256)] = total[:256].astype(BF)
    if total.shape[0] == ROWS:
        inner = total[256:272] + total[272:288]
        high = inner.astype(BF)
        ref[pl.ds(256, 16)] = high
        ref[pl.ds(272, 16)] = (inner - high.astype(F32)).astype(BF)


def kernel(
    x_hbm, gain_hbm, wqkv_hbm, wout_hbm, g_hbm,
    lo_out, ig_out, dwqkv_out, dwo_out,
    both, mid, gain_ref, xb, gb, wqkv, wout, gain, inv, norm, norm_t, qkv, att, att_t,
    probs, probs_t, gheads, dqkv, term1, rb1, zs1, zb1, term2, rb2, zs2, zb2,
    wg, tx, px, mx, sx, tz, pz, mz, res, dwo, done_both, back_mid, back_both,
    ssem, rsem, lsem,
):
    loads = [
        pltpu.make_async_copy(src, dst, lsem.at[at])
        for at, (src, dst) in enumerate(
            [
                (x_hbm, both.at[:, :, 0]),
                (g_hbm, both.at[:, :, 1]),
                (gain_hbm, gain_ref),
                (wqkv_hbm, wqkv),
                (wout_hbm, wout),
            ]
        )
    ]
    for load in loads:
        load.start()
    stores = []

    def store(src, dst):
        stores.append(pltpu.make_async_copy(src, dst, lsem.at[len(loads) + len(stores)]))
        stores[-1].start()

    net = Net(ssem, rsem)
    mp = net.mp

    for load in loads[:3]:
        load.wait()
    bring = net.start(net.frames_to_patches(both, mid, xb, gb))
    gain[...] = gain_ref[...].astype(F32)
    net.step()
    net.step()
    gather_x = net.start(net.gather(xb))
    net.finish(bring)
    net.until(gather_x, 3)
    gather_g = net.start(net.gather(gb))
    net.finish(gather_x)

    def square(m, total):
        block = flat(xb[m]).astype(F32)
        return total + block * block

    squares = lax.fori_loop(0, 16, square, jnp.zeros((256, HEAD), F32))
    mean = jnp.sum(squares, axis=-1, keepdims=True) * (1.0 / 2048)
    inv[...] = jnp.broadcast_to(lax.rsqrt(mean + EPS), (256, HEAD))

    def normalise(m, carry):
        block = flat(xb[m]).astype(F32) * inv[...] * gain[pl.ds(m, 1), :]
        norm[:, pl.ds(pl.multiple_of(m * 128, 128), 128)] = block.astype(BF)
        return carry

    lax.fori_loop(0, 16, normalise, 0, unroll=2)
    net.passed(1.5)
    for load in loads[3:]:
        load.wait()
    qkv[...] = mm(norm[...], wqkv[...]).astype(BF)
    net.passed(1.0)

    scale = HEAD ** (-0.5)
    rows = lax.broadcasted_iota(jnp.int32, (256, 256), 0)
    cols = lax.broadcasted_iota(jnp.int32, (256, 256), 1)
    keep = (((rows - cols) & 15) == 0) & (cols <= rows)
    queries, keys, values = (qkv[:, pl.ds(i * 128, 128)] for i in range(3))
    scores = jnp.where(keep, mm_nt(queries, keys) * scale, -1e30)
    expo = jnp.exp(scores - jnp.max(scores, axis=-1, keepdims=True))
    soft = expo / jnp.sum(expo, axis=-1, keepdims=True)
    probs[...] = soft
    attended = mm(soft.astype(BF), values)
    att[...] = attended.astype(BF)
    net.passed(1.5)

    def out_term(i, carry):
        wide = mm(att[...], wout[:, pl.ds(pl.multiple_of(i * 256, 256), 256)]).astype(BF)
        term1[2 * i] = wide[:, :128]
        term1[2 * i + 1] = wide[:, 128:]
        return carry

    lax.fori_loop(0, 8, out_term, 0, unroll=4)
    net.until(gather_g, 4)
    sum_1 = net.start(net.scatter_sum(term1, rb1, zs1, zb1))

    att_t[...] = jnp.transpose(attended).astype(BF)
    probs_t[...] = jnp.transpose(soft).astype(BF)

    def turn(m, carry):
        at = pl.multiple_of(m * 128, 128)
        block = norm[:, pl.ds(at, 128)].astype(F32)
        norm_t[pl.ds(at, 128), :] = jnp.transpose(block).astype(BF)
        return carry

    lax.fori_loop(0, 16, turn, 0, unroll=2)
    net.finish(gather_g)

    def pair_of(i):
        return jnp.concatenate([flat(gb[2 * i]), flat(gb[2 * i + 1])], axis=1)

    total = jnp.zeros((256, HEAD), F32)
    for i in range(8):
        total += mm_nt(pair_of(i), wout[:, pl.ds(i * 256, 256)])
    gheads[...] = total.astype(BF)

    dqkv[:, pl.ds(256, 128)] = mm(probs_t[...], gheads[...]).astype(BF)
    dprobs = mm_nt(gheads[...], qkv[:, pl.ds(256, 128)]).astype(BF).astype(F32)
    soft = probs[...]
    delta = jnp.sum(soft * dprobs, axis=-1, keepdims=True)
    dscores = soft * (dprobs - delta) * scale
    high = dscores.astype(BF)
    low = (dscores - high.astype(F32)).astype(BF)
    keys = qkv[:, pl.ds(128, 128)]
    dqkv[:, pl.ds(0, 128)] = (mm(high, keys) + mm(low, keys)).astype(BF)
    turned = jnp.transpose(dscores)
    high = turned.astype(BF)
    low = (turned - high.astype(F32)).astype(BF)
    queries = qkv[:, pl.ds(0, 128)]
    dqkv[:, pl.ds(128, 128)] = (mm(high, queries) + mm(low, queries)).astype(BF)

    def piece(q):
        for half in range(2):
            at = q * 4 + half * 2
            rows = norm_t[pl.ds(pl.multiple_of(at * 128, 256), 256), :]
            tall = mm(rows, dqkv[...]).astype(BF)
            wide = mm(att_t[...], jnp.concatenate([flat(gb[at]), flat(gb[at + 1])], axis=1)).astype(BF)
            for k in range(2):
                for c in range(3):
                    wg[q, 2 * half + k, c] = tall[k * 128 : k * 128 + 128, c * 128 : c * 128 + 128]
                wg[q, 2 * half + k, 3] = wide[:, k * 128 : k * 128 + 128]

    def stored():
        for c in range(3):
            store(res.at[:, :, c], dwqkv_out.at[:, :, :, pl.ds(c * 128, 128)])
        store(dwo, dwo_out)

    net.start(net.weight_sum(piece, wg, tx, px, mx, sx, tz, pz, mz, res, dwo, stored))
    net.passed(1.0)

    def norm_term(i, total):
        tall = wqkv[pl.ds(pl.multiple_of(i * 256, 256), 256), :]
        wide = mm_nt(dqkv[...], tall).astype(BF)
        for half in (0, 1):
            part = wide[:, half * 128 : half * 128 + 128]
            term2[2 * i + half, pl.ds(0, 256)] = part
            total += gain[pl.ds(2 * i + half, 1), :] * part.astype(F32) * flat(
                xb[2 * i + half]
            ).astype(F32)
        return total

    inner = lax.fori_loop(0, 8, norm_term, jnp.zeros((256, HEAD), F32), unroll=2)
    inner = jnp.sum(jnp.transpose(inner), axis=0, keepdims=True)
    at_row = lax.broadcasted_iota(jnp.int32, (16, HEAD), 0)
    inner = jnp.where(at_row == 0, inner[:, :128], jnp.where(at_row == 1, inner[:, 128:], 0.0))
    high = inner.astype(BF)
    low = (inner - high.astype(F32)).astype(BF)
    for m in range(16):
        term2[m, pl.ds(256, 16)] = high
        term2[m, pl.ds(272, 16)] = low

    def token_flow():
        yield from net.scatter_sum(term2, rb2, zs2, zb2)
        total = net.received(term2, rb2, 1, net.zl) + zb2[...].astype(F32)
        while any(item[1] is sum_1 for item in net.flows):
            yield 0.5
        summed = net.received(term1, rb1, 1, net.zl) + zb1[...].astype(F32)
        local = flat(xb[mp]).astype(F32)
        done_both[:, :, 0] = (local + summed).astype(BF).reshape(4, 4, 16, HEAD)
        rows = total[256:272] + total[272:288]
        rows = jnp.concatenate(
            [jnp.transpose(jnp.broadcast_to(rows[k : k + 1], (HEAD, HEAD))) for k in (0, 1)], axis=0
        )
        scale_own = inv[...]
        grad = (
            flat(gb[mp]).astype(F32)
            + scale_own * gain[pl.ds(mp, 1), :] * total[:256]
            - local * (scale_own * scale_own * scale_own) * rows * (1.0 / 2048)
        )
        done_both[:, :, 1] = grad.astype(BF).reshape(4, 4, 16, HEAD)
        yield 0.1
        yield from net.patches_to_frames(done_both, back_mid, back_both)
        store(back_both.at[:, :, 0], lo_out)
        store(back_both.at[:, :, 1], ig_out)

    net.start(token_flow())
    net.finish()
    net.close()
    for copy in stores:
        copy.wait()


def bf(*shape):
    return pltpu.VMEM(shape, BF)


def f32(*shape):
    return pltpu.VMEM(shape, F32)


def shards(frames_in, norm_gain, w_qkv, w_out, cotangent):
    hbm = pl.BlockSpec(memory_space=pltpu.HBM)
    block = (4, 4, 16, HEAD)
    scratch = [
        bf(4, 4, 2, 16, HEAD), bf(4, 4, 2, 16, HEAD), bf(16, HEAD),
        bf(16, *block), bf(16, *block),
        bf(2048, 384), bf(HEAD, 2048),
        f32(16, HEAD), f32(256, HEAD),
        bf(256, 2048), bf(2048, 256),
        bf(256, 384), bf(256, HEAD), bf(HEAD, 256),
        f32(256, 256), bf(256, 256),
        bf(256, HEAD), bf(256, 384),
        bf(16, 256, HEAD), bf(14, 256, HEAD), bf(256, HEAD), bf(256, HEAD),
        bf(16, ROWS, HEAD), bf(14, ROWS, HEAD), bf(ROWS, HEAD), bf(ROWS, HEAD),
        bf(4, 4, 4, HEAD, HEAD),
        bf(4, 4, HEAD, HEAD), bf(4, 4, HEAD, HEAD), bf(4, 4, HEAD, HEAD),
        bf(2, 4, HEAD, HEAD),
        bf(4, HEAD, HEAD), bf(4, HEAD, HEAD), bf(4, HEAD, HEAD),
        bf(4, 4, 3, HEAD, HEAD), bf(HEAD, HEAD),
        bf(4, 4, 2, 16, HEAD), bf(4, 4, 2, 16, HEAD), bf(4, 4, 2, 16, HEAD),
        pltpu.SemaphoreType.DMA((COPIES,)),
        pltpu.SemaphoreType.DMA((COPIES,)),
        pltpu.SemaphoreType.DMA((11,)),
    ]
    layer_out, input_grad, qkv_weight_grad, out_weight_grad = pl.pallas_call(
        kernel,
        out_shape=(
            jax.ShapeDtypeStruct(block, BF),
            jax.ShapeDtypeStruct(block, BF),
            jax.ShapeDtypeStruct((4, 4, HEAD, 384), BF),
            jax.ShapeDtypeStruct((HEAD, HEAD), BF),
        ),
        in_specs=[hbm] * 5,
        out_specs=(hbm,) * 4,
        scratch_shapes=scratch,
        compiler_params=pltpu.CompilerParams(
            collective_id=0, has_side_effects=True, vmem_limit_bytes=55040 * 1024
        ),
        name="sublayer",
    )(frames_in.reshape(block), norm_gain.reshape(16, HEAD), w_qkv, w_out, cotangent.reshape(block))
    return (
        layer_out.reshape(1, 256, HEAD),
        input_grad.reshape(1, 256, HEAD),
        qkv_weight_grad.reshape(2048, 384),
        out_weight_grad,
    )


def solution(mesh):
    return jax.shard_map(
        shards,
        mesh=mesh,
        in_specs=(
            P(("clip", "seq"), None, "mp"),
            P(),
            P(None, "mp"),
            P("mp", None),
            P(("clip", "seq"), None, "mp"),
        ),
        out_specs=(
            P(("clip", "seq"), None, "mp"),
            P(("clip", "seq"), None, "mp"),
            P("clip", "mp"),
            P(("clip", "mp"), "seq"),
        ),
        check_vma=False,
    )
```

```python
import jax
import jax.numpy as jnp
from jax import lax
from jax.experimental import pallas as pl
from jax.experimental.pallas import tpu as pltpu
from jax.sharding import PartitionSpec as P

HEAD = 128
EPS = 1e-05
BF = jnp.bfloat16
F32 = jnp.float32
MESH = pl.DeviceIdType.MESH
COPIES = 112
ROWS = 288
SCALE = HEAD ** (-0.5)
NT = (((1,), (1,)), ((), ()))


def mm(a, b):
    return jnp.dot(a, b, preferred_element_type=F32)


def mm_nt(a, b):
    return lax.dot_general(a, b, NT, preferred_element_type=F32)


def mm_tn(a, b):
    return lax.dot_general(a, b, (((0,), (0,)), ((), ())), preferred_element_type=F32)


class Net:
    def __init__(self, ssem, rsem):
        self.ssem, self.rsem, self.started, self.flows, self.clock, self.steps = ssem, rsem, [], [], 0.0, {}
        clip, seq, mp = lax.axis_index("clip"), lax.axis_index("seq"), lax.axis_index("mp")
        self.clip, self.seq, self.mp = clip, seq, mp
        self.zh, self.x = seq // 4, seq & 3
        self.zl, self.y = mp // 8, mp & 7
        self.e = 1 - 2 * clip
        self.zp = 1 - self.zl
        self.dev_pair = (clip, seq, self.zp * 8 + self.y)
        barrier = pltpu.get_barrier_semaphore()
        peers = [self.dev_x(self.x_at(s)) for s in (1, 2, 3)]
        peers += [self.dev_z(self.z_at(s)) for s in (1, 2, 3)]
        peers += [self.dev_y(self.y_at(s)) for s in (1, -1, 2, -2)] + [self.dev_pair]
        for peer in peers:
            pl.semaphore_signal(barrier, inc=1, device_id=peer, device_id_type=MESH)
        pl.semaphore_wait(barrier, len(peers))

    def x_at(self, step):
        return (self.x + step) & 3

    def z_at(self, step):
        return (self.zh + step) & 3

    def y_at(self, step):
        return (self.y + step) & 7

    def dev_x(self, to):
        return (self.clip, self.zh * 4 + to, self.mp)

    def dev_z(self, to):
        return (self.clip, to * 4 + self.x, self.mp)

    def dev_y(self, to):
        return (self.clip, self.seq, self.zl * 8 + to)

    def send(self, src, dst, device):
        at = len(self.started)
        copy = pltpu.make_async_remote_copy(
            src_ref=src,
            dst_ref=dst,
            send_sem=self.ssem.at[at],
            recv_sem=self.rsem.at[at],
            device_id=device,
            device_id_type=MESH,
        )
        copy.start()
        self.started.append(copy)
        return copy

    def start(self, flow):
        self.flows.append([self.clock + next(flow), flow])
        return flow

    def step(self, item=None):
        item = item or min(self.flows, key=lambda entry: entry[0])
        self.clock = max(self.clock, item[0])
        wait = next(item[1], None)
        self.steps[id(item[1])] = self.steps.get(id(item[1]), 0) + 1
        if wait is None:
            self.flows.remove(item)
        else:
            item[0] = self.clock + wait

    def until(self, flow, steps):
        while self.steps.get(id(flow), 0) < steps:
            self.step(next(entry for entry in self.flows if entry[1] is flow))

    def finish(self, flow=None):
        while any(flow is None or item[1] is flow for item in self.flows):
            self.step()

    def passed(self, time):
        target = self.clock + time
        while self.flows and min(item[0] for item in self.flows) <= target:
            self.step()
        self.clock = target

    def close(self):
        for copy in self.started:
            copy.wait_send()

    def frames_to_patches(self, src, mid, xb, gb):
        zh, x, mp = self.zh, self.x, self.mp
        sent = []
        for s in (1, 3, 2):
            to = self.x_at(s)
            sent.append(self.send(src.at[:, to], mid.at[x], self.dev_x(to)))
        mid[x] = src[:, x]
        yield 3.0
        for copy in sent:
            copy.wait_recv()
        sent = []
        for half, dst in ((0, xb), (1, gb)):
            for s in (1, 3, 2):
                to = self.z_at(s)
                sent.append(self.send(mid.at[:, to, half], dst.at[mp, zh], self.dev_z(to)))
            dst[mp, zh] = mid[:, zh, half]
        for some in (sent[:3], sent[3:]):
            yield 3.0
            for copy in some:
                copy.wait_recv()

    def patches_to_frames(self, src, mid, dst):
        zh, x = self.zh, self.x
        sent = []
        for s in (1, 3, 2):
            to = self.z_at(s)
            sent.append(self.send(src.at[to], mid.at[zh], self.dev_z(to)))
        mid[zh] = src[zh]
        yield 3.0
        for copy in sent:
            copy.wait_recv()
        sent = []
        for s in (1, 3, 2):
            to = self.x_at(s)
            sent.append(self.send(mid.at[:, to], dst.at[:, x], self.dev_x(to)))
        dst[:, x] = mid[:, x]
        yield 3.0
        for copy in sent:
            copy.wait_recv()

    def gather(self, buf):
        def pass_on(block, device):
            return self.send(buf.at[block], buf.at[block], device)

        ahead, back = self.dev_y(self.y_at(self.e)), self.dev_y(self.y_at(-self.e))

        def own(step):
            return self.zl * 8 + self.y_at(step)

        def other(step):
            return self.zp * 8 + self.y_at(step)

        a = pass_on(self.mp, ahead)
        b = pass_on(self.mp, back)
        pair = [pass_on(self.mp, self.dev_pair)]
        yield 4.0
        a.wait_recv()
        a = pass_on(own(-self.e), ahead)
        yield 0.1
        b.wait_recv()
        b = pass_on(own(self.e), back)
        yield 0.5
        pair[0].wait_recv()
        c = pass_on(other(0), ahead)
        d = pass_on(other(0), back)
        yield 2.5
        a.wait_recv()
        a = pass_on(own(-2 * self.e), ahead)
        yield 0.1
        b.wait_recv()
        b = pass_on(own(2 * self.e), back)
        pair.append(pass_on(own(2 * self.e), self.dev_pair))
        yield 1.0
        c.wait_recv()
        c = pass_on(other(-self.e), ahead)
        yield 0.1
        d.wait_recv()
        yield 2.5
        a.wait_recv()
        a = pass_on(own(-3 * self.e), ahead)
        pair.append(pass_on(own(-3 * self.e), self.dev_pair))
        yield 0.1
        b.wait_recv()
        pair.append(pass_on(own(3 * self.e), self.dev_pair))
        yield 0.5
        c.wait_recv()
        yield 2.5
        a.wait_recv()
        pair.append(pass_on(own(-4 * self.e), self.dev_pair))
        for copy in pair[1:]:
            yield 0.5
            copy.wait_recv()

    def scatter_sum(self, term, rb, zs, zb):
        planes = (self.zp, self.zl)
        ways = ((self.e, 4), (-self.e, 3))
        order = [(i, j) for i in (0, 1) for j in (0, 1)]

        def slot(i, j, k):
            return i * 7 + j * 4 + k - 1

        sent = {}
        for i, j in order:
            way, steps = ways[j]
            dest = planes[i] * 8 + self.y_at(steps * way)
            sent[i, j] = self.send(term.at[dest], rb.at[slot(i, j, 1)], self.dev_y(self.y_at(way)))
        last = None
        for k in (1, 2, 3, 4):
            for i, j in order:
                way, steps = ways[j]
                if k > steps:
                    continue
                yield 4.0 if (i, j) == (0, 0) else 0.6
                sent[i, j].wait_recv()
                here = rb.at[slot(i, j, k)]
                if k < steps:
                    dest = planes[i] * 8 + self.y_at((steps - k) * way)
                    fold(here, here[...].astype(F32) + term[dest].astype(F32))
                    after = rb.at[slot(i, j, k + 1)]
                    sent[i, j] = self.send(here, after, self.dev_y(self.y_at(way)))
                elif k == 4 and i == 0:
                    fold(zs, self.received(term, rb, 0, self.zp))
                    last = self.send(zs, zb, self.dev_pair)
        yield 3.0
        last.wait_recv()

    def received(self, term, rb, i, plane):
        return (
            term[plane * 8 + self.y].astype(F32)
            + rb[7 * i + 3].astype(F32)
            + rb[7 * i + 6].astype(F32)
        )

    def weight_sum(self, piece, wg, tx, px, mx, sx, tz, pz, mz, res, done):
        zh, x, e = self.zh, self.x, self.e
        xp, xm, zm = self.x_at(e), self.x_at(-e), self.z_at(-e)
        ahead, back = self.dev_x(xp), self.dev_x(xm)
        z_ahead, z_back = self.dev_z(self.z_at(e)), self.dev_z(zm)
        q = (self.z_at(2), self.z_at(e), zm, zh)
        far, plain, near = [], [], []

        def here(i):
            return wg[q[i], x].astype(F32) + px[i].astype(F32) + mx[i].astype(F32)

        for i in range(4):
            piece(q[i])
            far.append(self.send(wg.at[q[i], self.x_at(2)], tx.at[i], ahead))
            plain.append(self.send(wg.at[q[i], xm], px.at[i], back))
            if i < 3:
                yield 0.8
        for i in range(4):
            yield 3.0
            far[i].wait_recv()
            tx[i] = (tx[i].astype(F32) + wg[q[i], xp].astype(F32)).astype(BF)
            near.append(self.send(tx.at[i], mx.at[i], ahead))
        yield 2.0
        plain[0].wait_recv()
        near[0].wait_recv()
        sx[0] = here(0).astype(BF)
        z_far = self.send(sx.at[0], tz, z_ahead)
        for i in (1, 2):
            yield 1.5
            plain[i].wait_recv()
            near[i].wait_recv()
        sx[1] = here(2).astype(BF)
        z_plain = self.send(sx.at[1], pz, z_back)
        yield 1.0
        z_far.wait_recv()
        tz[...] = (tz[...].astype(F32) + here(1)).astype(BF)
        z_near = self.send(tz, mz, z_ahead)
        yield 2.0
        plain[3].wait_recv()
        near[3].wait_recv()
        yield 3.0
        z_plain.wait_recv()
        z_near.wait_recv()
        total = (here(3) + pz[...].astype(F32) + mz[...].astype(F32)).astype(BF)
        res[zh, x] = total

        def pass_on(at, column, device):
            return self.send(res.at[at, column], res.at[at, column], device)

        up, down = pass_on(zh, x, z_ahead), pass_on(zh, x, z_back)
        first, second, third = [pass_on(zh, x, ahead)], [pass_on(zh, x, back)], []
        yield 4.0
        up.wait_recv()
        up = pass_on(zm, x, z_ahead)
        first.append(pass_on(zm, x, ahead))
        second.append(pass_on(zm, x, back))
        yield 0.2
        down.wait_recv()
        first.append(pass_on(q[1], x, ahead))
        second.append(pass_on(q[1], x, back))
        yield 0.5
        first[0].wait_recv()
        third.append(pass_on(zh, xm, ahead))
        yield 2.0
        up.wait_recv()
        first.append(pass_on(q[0], x, ahead))
        second.append(pass_on(q[0], x, back))
        for i, at in ((1, zm), (2, q[1]), (3, q[0])):
            yield 2.0
            first[i].wait_recv()
            third.append(pass_on(at, xm, ahead))
        for copy in second + third:
            yield 1.0
            copy.wait_recv()
        done()

    def out_sum(self, wo, tx, px, mx, sx, tz, pz, mz, done):
        zh, x, e = self.zh, self.x, self.e
        xp, xm, zm = self.x_at(e), self.x_at(-e), self.z_at(-e)
        ahead, back = self.dev_x(xp), self.dev_x(xm)
        z_ahead, z_back = self.dev_z(self.z_at(e)), self.dev_z(zm)
        far = self.send(wo.at[:, self.x_at(2)], tx, ahead)
        plain = self.send(wo.at[:, xm], px, back)
        yield 7.0
        far.wait_recv()
        tx[...] = (tx[...].astype(F32) + wo[:, xp].astype(F32)).astype(BF)
        near = self.send(tx, mx, ahead)
        yield 6.0
        plain.wait_recv()
        near.wait_recv()
        sx[...] = (wo[:, x].astype(F32) + px[...].astype(F32) + mx[...].astype(F32)).astype(BF)
        z_far = self.send(sx.at[self.z_at(2)], tz, z_ahead)
        z_plain = self.send(sx.at[zm], pz, z_back)
        yield 5.0
        z_far.wait_recv()
        tz[...] = (tz[...].astype(F32) + sx[self.z_at(e)].astype(F32)).astype(BF)
        z_near = self.send(tz, mz, z_ahead)
        yield 5.0
        z_plain.wait_recv()
        z_near.wait_recv()
        total = wo[zh, x].astype(F32) + px[zh].astype(F32) + mx[zh].astype(F32)
        done((total + pz[...].astype(F32) + mz[...].astype(F32)).astype(BF))


def flat(block):
    return block.reshape(256, HEAD)


def fold(ref, total):
    ref[pl.ds(0, 256)] = total[:256].astype(BF)
    if total.shape[0] == ROWS:
        inner = total[256:272] + total[272:288]
        high = inner.astype(BF)
        ref[pl.ds(256, 16)] = high
        ref[pl.ds(272, 16)] = (inner - high.astype(F32)).astype(BF)


def kernel(
    x_hbm, gain_hbm, wqkv_hbm, wout_hbm, g_hbm,
    lo_out, ig_out, dwqkv_out, dwo_out,
    both, mid, gain_ref, xb, gb, wqkv, wout, gain, inv, norm, norm_t, qkv, att, att_t,
    probs, probs_t, gheads, dqkv, term1, rb1, zs1, zb1, term2, rb2, zs2, zb2,
    wg, tx, px, mx, sx, tz, pz, mz, wo, txo, pxo, mxo, sxo, tzo, pzo, mzo, res, dwo, done_both, back_mid, back_both,
    ssem, rsem, lsem,
):
    loads = [
        pltpu.make_async_copy(src, dst, lsem.at[at])
        for at, (src, dst) in enumerate(
            [
                (x_hbm, both.at[:, :, 0]),
                (g_hbm, both.at[:, :, 1]),
                (gain_hbm, gain_ref),
                (wqkv_hbm, wqkv),
                (wout_hbm, wout),
            ]
        )
    ]
    for load in loads:
        load.start()
    stores = []

    def store(src, dst):
        stores.append(pltpu.make_async_copy(src, dst, lsem.at[len(loads) + len(stores)]))
        stores[-1].start()

    net = Net(ssem, rsem)
    mp = net.mp

    for load in loads[:3]:
        load.wait()
    bring = net.start(net.frames_to_patches(both, mid, xb, gb))
    gain[...] = gain_ref[...].astype(F32)
    net.step()
    net.step()
    gather_x = net.start(net.gather(xb))
    net.finish(bring)
    net.until(gather_x, 7)
    gather_g = net.start(net.gather(gb))
    net.finish(gather_x)

    def square(m, total):
        block = flat(xb[m]).astype(F32)
        return total + block * block

    squares = lax.fori_loop(0, 16, square, jnp.zeros((256, HEAD), F32))
    mean = jnp.sum(squares, axis=-1, keepdims=True) * (1.0 / 2048)
    inv[...] = jnp.broadcast_to(lax.rsqrt(mean + EPS), (256, HEAD))

    def normalise(m, carry):
        block = flat(xb[m]).astype(F32) * inv[...] * gain[pl.ds(m, 1), :]
        norm[:, pl.ds(pl.multiple_of(m * 128, 128), 128)] = block.astype(BF)
        return carry

    lax.fori_loop(0, 16, normalise, 0, unroll=2)
    net.passed(2.2)
    for load in loads[3:]:
        load.wait()
    qkv[...] = mm(norm[...], wqkv[...]).astype(BF)
    net.passed(1.2)

    scale = HEAD ** (-0.5)
    rows = lax.broadcasted_iota(jnp.int32, (256, 256), 0)
    cols = lax.broadcasted_iota(jnp.int32, (256, 256), 1)
    keep = (((rows - cols) & 15) == 0) & (cols <= rows)
    queries, keys, values = (qkv[:, pl.ds(i * 128, 128)] for i in range(3))
    scores = jnp.where(keep, mm_nt(queries, keys) * scale, -1e30)
    expo = jnp.exp(scores - jnp.max(scores, axis=-1, keepdims=True))
    soft = expo / jnp.sum(expo, axis=-1, keepdims=True)
    probs[...] = soft
    attended = mm(soft.astype(BF), values)
    att[...] = attended.astype(BF)
    net.passed(1.8)

    def out_term(i, carry):
        wide = mm(att[...], wout[:, pl.ds(pl.multiple_of(i * 256, 256), 256)]).astype(BF)
        term1[2 * i] = wide[:, :128]
        term1[2 * i + 1] = wide[:, 128:]
        return carry

    lax.fori_loop(0, 8, out_term, 0, unroll=4)
    net.passed(1.0)

    att_t[...] = jnp.transpose(attended).astype(BF)
    probs_t[...] = jnp.transpose(soft).astype(BF)

    def turn(m, carry):
        at = pl.multiple_of(m * 128, 128)
        block = norm[:, pl.ds(at, 128)].astype(F32)
        norm_t[pl.ds(at, 128), :] = jnp.transpose(block).astype(BF)
        return carry

    lax.fori_loop(0, 16, turn, 0, unroll=2)
    net.finish(gather_g)

    def pair_of(i):
        return jnp.concatenate([flat(gb[2 * i]), flat(gb[2 * i + 1])], axis=1)

    sum_1 = net.start(net.scatter_sum(term1, rb1, zs1, zb1))
    for i in range(8):
        wide = mm(att_t[...], pair_of(i)).astype(BF)
        wo[i // 2, 2 * (i % 2)] = wide[:, :128]
        wo[i // 2, 2 * (i % 2) + 1] = wide[:, 128:]

    def out_stored(total):
        dwo[...] = total
        store(dwo, dwo_out)

    net.start(net.out_sum(wo, txo, pxo, mxo, sxo, tzo, pzo, mzo, out_stored))
    total = jnp.zeros((256, HEAD), F32)
    for i in range(8):
        total += mm_nt(pair_of(i), wout[:, pl.ds(i * 256, 256)])
    gheads[...] = total.astype(BF)
    net.passed(2.5)

    dqkv[:, pl.ds(256, 128)] = mm(probs_t[...], gheads[...]).astype(BF)
    dprobs = mm_nt(gheads[...], qkv[:, pl.ds(256, 128)]).astype(BF).astype(F32)
    soft = probs[...]
    delta = jnp.sum(soft * dprobs, axis=-1, keepdims=True)
    dscores = soft * (dprobs - delta) * scale
    high = dscores.astype(BF)
    low = (dscores - high.astype(F32)).astype(BF)
    keys = qkv[:, pl.ds(128, 128)]
    dqkv[:, pl.ds(0, 128)] = (mm(high, keys) + mm(low, keys)).astype(BF)
    turned = jnp.transpose(dscores)
    high = turned.astype(BF)
    low = (turned - high.astype(F32)).astype(BF)
    queries = qkv[:, pl.ds(0, 128)]
    dqkv[:, pl.ds(128, 128)] = (mm(high, queries) + mm(low, queries)).astype(BF)

    def piece(q):
        for half in range(2):
            at = q * 4 + half * 2
            rows = norm_t[pl.ds(pl.multiple_of(at * 128, 256), 256), :]
            tall = mm(rows, dqkv[...]).astype(BF)
            for k in range(2):
                for c in range(3):
                    wg[q, 2 * half + k, c] = tall[k * 128 : k * 128 + 128, c * 128 : c * 128 + 128]

    def stored():
        for c in range(3):
            store(res.at[:, :, c], dwqkv_out.at[:, :, :, pl.ds(c * 128, 128)])

    net.start(net.weight_sum(piece, wg, tx, px, mx, sx, tz, pz, mz, res, stored))
    net.passed(1.0)

    def norm_term(i, total):
        tall = wqkv[pl.ds(pl.multiple_of(i * 256, 256), 256), :]
        wide = mm_nt(dqkv[...], tall).astype(BF)
        for half in (0, 1):
            part = wide[:, half * 128 : half * 128 + 128]
            term2[2 * i + half, pl.ds(0, 256)] = part
            total += gain[pl.ds(2 * i + half, 1), :] * part.astype(F32) * flat(
                xb[2 * i + half]
            ).astype(F32)
        return total

    inner = lax.fori_loop(0, 8, norm_term, jnp.zeros((256, HEAD), F32), unroll=2)
    inner = jnp.sum(jnp.transpose(inner), axis=0, keepdims=True)
    at_row = lax.broadcasted_iota(jnp.int32, (16, HEAD), 0)
    inner = jnp.where(at_row == 0, inner[:, :128], jnp.where(at_row == 1, inner[:, 128:], 0.0))
    high = inner.astype(BF)
    low = (inner - high.astype(F32)).astype(BF)
    for m in range(16):
        term2[m, pl.ds(256, 16)] = high
        term2[m, pl.ds(272, 16)] = low

    def token_flow():
        yield from net.scatter_sum(term2, rb2, zs2, zb2)
        total = net.received(term2, rb2, 1, net.zl) + zb2[...].astype(F32)
        while any(item[1] is sum_1 for item in net.flows):
            yield 0.5
        summed = net.received(term1, rb1, 1, net.zl) + zb1[...].astype(F32)
        local = flat(xb[mp]).astype(F32)
        done_both[:, :, 0] = (local + summed).astype(BF).reshape(4, 4, 16, HEAD)
        rows = total[256:272] + total[272:288]
        rows = jnp.concatenate(
            [jnp.transpose(jnp.broadcast_to(rows[k : k + 1], (HEAD, HEAD))) for k in (0, 1)], axis=0
        )
        scale_own = inv[...]
        grad = (
            flat(gb[mp]).astype(F32)
            + scale_own * gain[pl.ds(mp, 1), :] * total[:256]
            - local * (scale_own * scale_own * scale_own) * rows * (1.0 / 2048)
        )
        done_both[:, :, 1] = grad.astype(BF).reshape(4, 4, 16, HEAD)
        yield 0.1
        yield from net.patches_to_frames(done_both, back_mid, back_both)
        store(back_both.at[:, :, 0], lo_out)
        store(back_both.at[:, :, 1], ig_out)

    net.start(token_flow())
    net.finish()
    net.close()
    for copy in stores:
        copy.wait()


def bf(*shape):
    return pltpu.VMEM(shape, BF)


def f32(*shape):
    return pltpu.VMEM(shape, F32)


def shards(frames_in, norm_gain, w_qkv, w_out, cotangent):
    hbm = pl.BlockSpec(memory_space=pltpu.HBM)
    block = (4, 4, 16, HEAD)
    scratch = [
        bf(4, 4, 2, 16, HEAD), bf(4, 4, 2, 16, HEAD), bf(16, HEAD),
        bf(16, *block), bf(16, *block),
        bf(2048, 384), bf(HEAD, 2048),
        f32(16, HEAD), f32(256, HEAD),
        bf(256, 2048), bf(2048, 256),
        bf(256, 384), bf(256, HEAD), bf(HEAD, 256),
        f32(256, 256), bf(256, 256),
        bf(256, HEAD), bf(256, 384),
        bf(16, 256, HEAD), bf(14, 256, HEAD), bf(256, HEAD), bf(256, HEAD),
        bf(16, ROWS, HEAD), bf(14, ROWS, HEAD), bf(ROWS, HEAD), bf(ROWS, HEAD),
        bf(4, 4, 3, HEAD, HEAD),
        bf(4, 3, HEAD, HEAD), bf(4, 3, HEAD, HEAD), bf(4, 3, HEAD, HEAD),
        bf(2, 3, HEAD, HEAD),
        bf(3, HEAD, HEAD), bf(3, HEAD, HEAD), bf(3, HEAD, HEAD),
        bf(4, 4, HEAD, HEAD), bf(4, HEAD, HEAD), bf(4, HEAD, HEAD),
        bf(4, HEAD, HEAD), bf(4, HEAD, HEAD),
        bf(HEAD, HEAD), bf(HEAD, HEAD), bf(HEAD, HEAD),
        bf(4, 4, 3, HEAD, HEAD), bf(HEAD, HEAD),
        bf(4, 4, 2, 16, HEAD), bf(4, 4, 2, 16, HEAD), bf(4, 4, 2, 16, HEAD),
        pltpu.SemaphoreType.DMA((COPIES,)),
        pltpu.SemaphoreType.DMA((COPIES,)),
        pltpu.SemaphoreType.DMA((11,)),
    ]
    layer_out, input_grad, qkv_weight_grad, out_weight_grad = pl.pallas_call(
        kernel,
        out_shape=(
            jax.ShapeDtypeStruct(block, BF),
            jax.ShapeDtypeStruct(block, BF),
            jax.ShapeDtypeStruct((4, 4, HEAD, 384), BF),
            jax.ShapeDtypeStruct((HEAD, HEAD), BF),
        ),
        in_specs=[hbm] * 5,
        out_specs=(hbm,) * 4,
        scratch_shapes=scratch,
        compiler_params=pltpu.CompilerParams(
            collective_id=0, has_side_effects=True, vmem_limit_bytes=55040 * 1024
        ),
        name="sublayer",
    )(frames_in.reshape(block), norm_gain.reshape(16, HEAD), w_qkv, w_out, cotangent.reshape(block))
    return (
        layer_out.reshape(1, 256, HEAD),
        input_grad.reshape(1, 256, HEAD),
        qkv_weight_grad.reshape(2048, 384),
        out_weight_grad,
    )


def solution(mesh):
    return jax.shard_map(
        shards,
        mesh=mesh,
        in_specs=(
            P(("clip", "seq"), None, "mp"),
            P(),
            P(None, "mp"),
            P("mp", None),
            P(("clip", "seq"), None, "mp"),
        ),
        out_specs=(
            P(("clip", "seq"), None, "mp"),
            P(("clip", "seq"), None, "mp"),
            P("clip", "mp"),
            P(("clip", "mp"), "seq"),
        ),
        check_vma=False,
    )
```

```python
import jax
import jax.numpy as jnp
from jax import lax
from jax.experimental import pallas as pl
from jax.experimental.pallas import tpu as pltpu
from jax.sharding import PartitionSpec as P

HEAD = 128
EPS = 1e-05
BF = jnp.bfloat16
F32 = jnp.float32
MESH = pl.DeviceIdType.MESH
COPIES = 112
ROWS = 288
SCALE = HEAD ** (-0.5)
NT = (((1,), (1,)), ((), ()))


def mm(a, b):
    return jnp.dot(a, b, preferred_element_type=F32)


def mm_nt(a, b):
    return lax.dot_general(a, b, NT, preferred_element_type=F32)


def mm_tn(a, b):
    return lax.dot_general(a, b, (((0,), (0,)), ((), ())), preferred_element_type=F32)


class Net:
    def __init__(self, ssem, rsem):
        self.ssem, self.rsem, self.started, self.flows, self.clock, self.steps = ssem, rsem, [], [], 0.0, {}
        clip, seq, mp = lax.axis_index("clip"), lax.axis_index("seq"), lax.axis_index("mp")
        self.clip, self.seq, self.mp = clip, seq, mp
        self.zh, self.x = seq // 4, seq & 3
        self.zl, self.y = mp // 8, mp & 7
        self.e = 1 - 2 * clip
        self.zp = 1 - self.zl
        self.dev_pair = (clip, seq, self.zp * 8 + self.y)
        barrier = pltpu.get_barrier_semaphore()
        peers = [self.dev_x(self.x_at(s)) for s in (1, 2, 3)]
        peers += [self.dev_z(self.z_at(s)) for s in (1, 2, 3)]
        peers += [self.dev_y(self.y_at(s)) for s in (1, -1, 2, -2)] + [self.dev_pair]
        for peer in peers:
            pl.semaphore_signal(barrier, inc=1, device_id=peer, device_id_type=MESH)
        pl.semaphore_wait(barrier, len(peers))

    def x_at(self, step):
        return (self.x + step) & 3

    def z_at(self, step):
        return (self.zh + step) & 3

    def y_at(self, step):
        return (self.y + step) & 7

    def dev_x(self, to):
        return (self.clip, self.zh * 4 + to, self.mp)

    def dev_z(self, to):
        return (self.clip, to * 4 + self.x, self.mp)

    def dev_y(self, to):
        return (self.clip, self.seq, self.zl * 8 + to)

    def send(self, src, dst, device):
        at = len(self.started)
        copy = pltpu.make_async_remote_copy(
            src_ref=src,
            dst_ref=dst,
            send_sem=self.ssem.at[at],
            recv_sem=self.rsem.at[at],
            device_id=device,
            device_id_type=MESH,
        )
        copy.start()
        self.started.append(copy)
        return copy

    def start(self, flow):
        self.flows.append([self.clock + next(flow), flow])
        return flow

    def step(self, item=None):
        item = item or min(self.flows, key=lambda entry: entry[0])
        self.clock = max(self.clock, item[0])
        wait = next(item[1], None)
        self.steps[id(item[1])] = self.steps.get(id(item[1]), 0) + 1
        if wait is None:
            self.flows.remove(item)
        else:
            item[0] = self.clock + wait

    def until(self, flow, steps):
        while self.steps.get(id(flow), 0) < steps:
            self.step(next(entry for entry in self.flows if entry[1] is flow))

    def finish(self, flow=None):
        while any(flow is None or item[1] is flow for item in self.flows):
            self.step()

    def passed(self, time):
        target = self.clock + time
        while self.flows and min(item[0] for item in self.flows) <= target:
            self.step()
        self.clock = target

    def close(self):
        for copy in self.started:
            copy.wait_send()

    def frames_to_patches(self, src, mid, xb, gb):
        zh, x, mp = self.zh, self.x, self.mp
        sent = []
        for s in (1, 3, 2):
            to = self.x_at(s)
            sent.append(self.send(src.at[:, to], mid.at[x], self.dev_x(to)))
        mid[x] = src[:, x]
        yield 9.96
        for copy in sent:
            copy.wait_recv()
        sent = []
        for half, dst in ((0, xb), (1, gb)):
            for s in (1, 3, 2):
                to = self.z_at(s)
                sent.append(self.send(mid.at[:, to, half], dst.at[mp, zh], self.dev_z(to)))
            dst[mp, zh] = mid[:, zh, half]
        for some in (sent[:3], sent[3:]):
            yield 2.2
            for copy in some:
                copy.wait_recv()

    def patches_to_frames(self, src, mid, dst):
        zh, x = self.zh, self.x
        sent = []
        for s in (1, 3, 2):
            to = self.z_at(s)
            sent.append(self.send(src.at[to], mid.at[zh], self.dev_z(to)))
        mid[zh] = src[zh]
        yield 2.41
        for copy in sent:
            copy.wait_recv()
        sent = []
        for s in (1, 3, 2):
            to = self.x_at(s)
            sent.append(self.send(mid.at[:, to], dst.at[:, x], self.dev_x(to)))
        dst[:, x] = mid[:, x]
        yield 36.64
        for copy in sent:
            copy.wait_recv()

    def gather(self, buf):
        def pass_on(block, device):
            return self.send(buf.at[block], buf.at[block], device)

        ahead, back = self.dev_y(self.y_at(self.e)), self.dev_y(self.y_at(-self.e))

        def own(step):
            return self.zl * 8 + self.y_at(step)

        def other(step):
            return self.zp * 8 + self.y_at(step)

        a = pass_on(self.mp, ahead)
        b = pass_on(self.mp, back)
        pair = [pass_on(self.mp, self.dev_pair)]
        yield 4.0
        a.wait_recv()
        a = pass_on(own(-self.e), ahead)
        yield 0.3
        b.wait_recv()
        b = pass_on(own(self.e), back)
        yield 0.42
        pair[0].wait_recv()
        c = pass_on(other(0), ahead)
        d = pass_on(other(0), back)
        yield 2.25
        a.wait_recv()
        a = pass_on(own(-2 * self.e), ahead)
        yield 0.62
        b.wait_recv()
        b = pass_on(own(2 * self.e), back)
        pair.append(pass_on(own(2 * self.e), self.dev_pair))
        yield 0.31
        c.wait_recv()
        c = pass_on(other(-self.e), ahead)
        yield 0.92
        d.wait_recv()
        yield 1.75
        a.wait_recv()
        a = pass_on(own(-3 * self.e), ahead)
        pair.append(pass_on(own(-3 * self.e), self.dev_pair))
        yield 0.89
        b.wait_recv()
        pair.append(pass_on(own(3 * self.e), self.dev_pair))
        yield 0.4
        c.wait_recv()
        yield 2.5
        a.wait_recv()
        pair.append(pass_on(own(-4 * self.e), self.dev_pair))
        for copy in pair[1:]:
            yield 1.05
            copy.wait_recv()

    def scatter_sum(self, term, rb, zs, zb):
        planes = (self.zp, self.zl)
        ways = ((self.e, 4), (-self.e, 3))
        order = [(i, j) for i in (0, 1) for j in (0, 1)]

        def slot(i, j, k):
            return i * 7 + j * 4 + k - 1

        sent = {}
        for i, j in order:
            way, steps = ways[j]
            dest = planes[i] * 8 + self.y_at(steps * way)
            sent[i, j] = self.send(term.at[dest], rb.at[slot(i, j, 1)], self.dev_y(self.y_at(way)))
        last = None
        for k in (1, 2, 3, 4):
            for i, j in order:
                way, steps = ways[j]
                if k > steps:
                    continue
                yield 5.6 if (i, j) == (0, 0) else 0.6
                sent[i, j].wait_recv()
                here = rb.at[slot(i, j, k)]
                if k < steps:
                    dest = planes[i] * 8 + self.y_at((steps - k) * way)
                    fold(here, here[...].astype(F32) + term[dest].astype(F32))
                    after = rb.at[slot(i, j, k + 1)]
                    sent[i, j] = self.send(here, after, self.dev_y(self.y_at(way)))
                elif k == 4 and i == 0:
                    fold(zs, self.received(term, rb, 0, self.zp))
                    last = self.send(zs, zb, self.dev_pair)
        yield 2.2
        last.wait_recv()

    def received(self, term, rb, i, plane):
        return (
            term[plane * 8 + self.y].astype(F32)
            + rb[7 * i + 3].astype(F32)
            + rb[7 * i + 6].astype(F32)
        )

    def weight_sum(self, piece, wg, tx, px, mx, sx, tz, pz, mz, res, done):
        zh, x, e = self.zh, self.x, self.e
        xp, xm, zm = self.x_at(e), self.x_at(-e), self.z_at(-e)
        ahead, back = self.dev_x(xp), self.dev_x(xm)
        z_ahead, z_back = self.dev_z(self.z_at(e)), self.dev_z(zm)
        q = (self.z_at(2), self.z_at(e), zm, zh)
        far, plain, near = [], [], []

        def here(i):
            return wg[q[i], x].astype(F32) + px[i].astype(F32) + mx[i].astype(F32)

        for i in range(4):
            piece(q[i])
            far.append(self.send(wg.at[q[i], self.x_at(2)], tx.at[i], ahead))
            plain.append(self.send(wg.at[q[i], xm], px.at[i], back))
            if i < 3:
                yield 0.78
        for i in range(4):
            yield 2.1
            far[i].wait_recv()
            tx[i] = (tx[i].astype(F32) + wg[q[i], xp].astype(F32)).astype(BF)
            near.append(self.send(tx.at[i], mx.at[i], ahead))
        yield 2.0
        plain[0].wait_recv()
        near[0].wait_recv()
        sx[0] = here(0).astype(BF)
        z_far = self.send(sx.at[0], tz, z_ahead)
        for i in (1, 2):
            yield 1.26
            plain[i].wait_recv()
            near[i].wait_recv()
        sx[1] = here(2).astype(BF)
        z_plain = self.send(sx.at[1], pz, z_back)
        yield 1.2
        z_far.wait_recv()
        tz[...] = (tz[...].astype(F32) + here(1)).astype(BF)
        z_near = self.send(tz, mz, z_ahead)
        yield 3.56
        plain[3].wait_recv()
        near[3].wait_recv()
        yield 3.0
        z_plain.wait_recv()
        z_near.wait_recv()
        total = (here(3) + pz[...].astype(F32) + mz[...].astype(F32)).astype(BF)
        res[zh, x] = total

        def pass_on(at, column, device):
            return self.send(res.at[at, column], res.at[at, column], device)

        up, down = pass_on(zh, x, z_ahead), pass_on(zh, x, z_back)
        first, second, third = [pass_on(zh, x, ahead)], [pass_on(zh, x, back)], []
        yield 6.1
        up.wait_recv()
        up = pass_on(zm, x, z_ahead)
        first.append(pass_on(zm, x, ahead))
        second.append(pass_on(zm, x, back))
        yield 1.45
        down.wait_recv()
        first.append(pass_on(q[1], x, ahead))
        second.append(pass_on(q[1], x, back))
        yield 0.8
        first[0].wait_recv()
        third.append(pass_on(zh, xm, ahead))
        yield 0.98
        up.wait_recv()
        first.append(pass_on(q[0], x, ahead))
        second.append(pass_on(q[0], x, back))
        for i, at in ((1, zm), (2, q[1]), (3, q[0])):
            yield 0.15
            first[i].wait_recv()
            third.append(pass_on(at, xm, ahead))
        for copy in second + third:
            yield 2.59
            copy.wait_recv()
        done()

    def out_sum(self, wo, tx, px, mx, sx, tz, pz, mz, done):
        zh, x, e = self.zh, self.x, self.e
        xp, xm, zm = self.x_at(e), self.x_at(-e), self.z_at(-e)
        ahead, back = self.dev_x(xp), self.dev_x(xm)
        z_ahead, z_back = self.dev_z(self.z_at(e)), self.dev_z(zm)
        far = self.send(wo.at[:, self.x_at(2)], tx, ahead)
        plain = self.send(wo.at[:, xm], px, back)
        yield 14.5
        far.wait_recv()
        tx[...] = (tx[...].astype(F32) + wo[:, xp].astype(F32)).astype(BF)
        near = self.send(tx, mx, ahead)
        yield 8.23
        plain.wait_recv()
        near.wait_recv()
        sx[...] = (wo[:, x].astype(F32) + px[...].astype(F32) + mx[...].astype(F32)).astype(BF)
        z_far = self.send(sx.at[self.z_at(2)], tz, z_ahead)
        z_plain = self.send(sx.at[zm], pz, z_back)
        yield 13.72
        z_far.wait_recv()
        tz[...] = (tz[...].astype(F32) + sx[self.z_at(e)].astype(F32)).astype(BF)
        z_near = self.send(tz, mz, z_ahead)
        yield 0.88
        z_plain.wait_recv()
        z_near.wait_recv()
        total = wo[zh, x].astype(F32) + px[zh].astype(F32) + mx[zh].astype(F32)
        done((total + pz[...].astype(F32) + mz[...].astype(F32)).astype(BF))


def flat(block):
    return block.reshape(256, HEAD)


def fold(ref, total):
    ref[pl.ds(0, 256)] = total[:256].astype(BF)
    if total.shape[0] == ROWS:
        inner = total[256:272] + total[272:288]
        high = inner.astype(BF)
        ref[pl.ds(256, 16)] = high
        ref[pl.ds(272, 16)] = (inner - high.astype(F32)).astype(BF)


def kernel(
    x_hbm, gain_hbm, wqkv_hbm, wout_hbm, g_hbm,
    lo_out, ig_out, dwqkv_out, dwo_out,
    both, mid, gain_ref, xb, gb, wqkv, wout, gain, inv, norm, norm_t, qkv, att, att_t,
    probs, probs_t, gheads, dqkv, term1, rb1, zs1, zb1, term2, rb2, zs2, zb2,
    wg, tx, px, mx, sx, tz, pz, mz, wo, txo, pxo, mxo, sxo, tzo, pzo, mzo, res, dwo, done_both, back_mid, back_both,
    ssem, rsem, lsem,
):
    loads = [
        pltpu.make_async_copy(src, dst, lsem.at[at])
        for at, (src, dst) in enumerate(
            [
                (x_hbm, both.at[:, :, 0]),
                (g_hbm, both.at[:, :, 1]),
                (gain_hbm, gain_ref),
                (wqkv_hbm, wqkv),
                (wout_hbm, wout),
            ]
        )
    ]
    for load in loads:
        load.start()
    stores = []

    def store(src, dst):
        stores.append(pltpu.make_async_copy(src, dst, lsem.at[len(loads) + len(stores)]))
        stores[-1].start()

    net = Net(ssem, rsem)
    mp = net.mp

    for load in loads[:3]:
        load.wait()
    bring = net.start(net.frames_to_patches(both, mid, xb, gb))
    gain[...] = gain_ref[...].astype(F32)
    net.step()
    net.step()
    gather_x = net.start(net.gather(xb))
    net.finish(bring)
    net.until(gather_x, 4)
    gather_g = net.start(net.gather(gb))
    net.finish(gather_x)

    def square(m, total):
        block = flat(xb[m]).astype(F32)
        return total + block * block

    squares = lax.fori_loop(0, 16, square, jnp.zeros((256, HEAD), F32))
    mean = jnp.sum(squares, axis=-1, keepdims=True) * (1.0 / 2048)
    inv[...] = jnp.broadcast_to(lax.rsqrt(mean + EPS), (256, HEAD))

    def normalise(m, carry):
        block = flat(xb[m]).astype(F32) * inv[...] * gain[pl.ds(m, 1), :]
        norm[:, pl.ds(pl.multiple_of(m * 128, 128), 128)] = block.astype(BF)
        return carry

    lax.fori_loop(0, 16, normalise, 0, unroll=2)
    net.passed(0.14)
    for load in loads[3:]:
        load.wait()
    qkv[...] = mm(norm[...], wqkv[...]).astype(BF)
    net.passed(1.7)

    scale = HEAD ** (-0.5)
    rows = lax.broadcasted_iota(jnp.int32, (256, 256), 0)
    cols = lax.broadcasted_iota(jnp.int32, (256, 256), 1)
    keep = (((rows - cols) & 15) == 0) & (cols <= rows)
    queries, keys, values = (qkv[:, pl.ds(i * 128, 128)] for i in range(3))
    scores = jnp.where(keep, mm_nt(queries, keys) * scale, -1e30)
    expo = jnp.exp(scores - jnp.max(scores, axis=-1, keepdims=True))
    soft = expo / jnp.sum(expo, axis=-1, keepdims=True)
    probs[...] = soft
    attended = mm(soft.astype(BF), values)
    att[...] = attended.astype(BF)
    net.passed(2.17)

    def out_term(i, carry):
        wide = mm(att[...], wout[:, pl.ds(pl.multiple_of(i * 256, 256), 256)]).astype(BF)
        term1[2 * i] = wide[:, :128]
        term1[2 * i + 1] = wide[:, 128:]
        return carry

    lax.fori_loop(0, 8, out_term, 0, unroll=4)
    net.passed(0.19)

    att_t[...] = jnp.transpose(attended).astype(BF)
    probs_t[...] = jnp.transpose(soft).astype(BF)

    def turn(m, carry):
        at = pl.multiple_of(m * 128, 128)
        block = norm[:, pl.ds(at, 128)].astype(F32)
        norm_t[pl.ds(at, 128), :] = jnp.transpose(block).astype(BF)
        return carry

    lax.fori_loop(0, 16, turn, 0, unroll=2)
    net.finish(gather_g)

    def pair_of(i):
        return jnp.concatenate([flat(gb[2 * i]), flat(gb[2 * i + 1])], axis=1)

    sum_1 = net.start(net.scatter_sum(term1, rb1, zs1, zb1))
    for i in range(8):
        wide = mm(att_t[...], pair_of(i)).astype(BF)
        wo[i // 2, 2 * (i % 2)] = wide[:, :128]
        wo[i // 2, 2 * (i % 2) + 1] = wide[:, 128:]

    def out_stored(total):
        dwo[...] = total
        store(dwo, dwo_out)

    net.start(net.out_sum(wo, txo, pxo, mxo, sxo, tzo, pzo, mzo, out_stored))
    total = jnp.zeros((256, HEAD), F32)
    for i in range(8):
        total += mm_nt(pair_of(i), wout[:, pl.ds(i * 256, 256)])
    gheads[...] = total.astype(BF)
    net.passed(0.82)

    dqkv[:, pl.ds(256, 128)] = mm(probs_t[...], gheads[...]).astype(BF)
    dprobs = mm_nt(gheads[...], qkv[:, pl.ds(256, 128)]).astype(BF).astype(F32)
    soft = probs[...]
    delta = jnp.sum(soft * dprobs, axis=-1, keepdims=True)
    dscores = soft * (dprobs - delta) * scale
    high = dscores.astype(BF)
    low = (dscores - high.astype(F32)).astype(BF)
    keys = qkv[:, pl.ds(128, 128)]
    dqkv[:, pl.ds(0, 128)] = (mm(high, keys) + mm(low, keys)).astype(BF)
    turned = jnp.transpose(dscores)
    high = turned.astype(BF)
    low = (turned - high.astype(F32)).astype(BF)
    queries = qkv[:, pl.ds(0, 128)]
    dqkv[:, pl.ds(128, 128)] = (mm(high, queries) + mm(low, queries)).astype(BF)

    def piece(q):
        for half in range(2):
            at = q * 4 + half * 2
            rows = norm_t[pl.ds(pl.multiple_of(at * 128, 256), 256), :]
            tall = mm(rows, dqkv[...]).astype(BF)
            for k in range(2):
                for c in range(3):
                    wg[q, 2 * half + k, c] = tall[k * 128 : k * 128 + 128, c * 128 : c * 128 + 128]

    def stored():
        for c in range(3):
            store(res.at[:, :, c], dwqkv_out.at[:, :, :, pl.ds(c * 128, 128)])

    net.start(net.weight_sum(piece, wg, tx, px, mx, sx, tz, pz, mz, res, stored))
    net.passed(1.0)

    def norm_term(i, total):
        tall = wqkv[pl.ds(pl.multiple_of(i * 256, 256), 256), :]
        wide = mm_nt(dqkv[...], tall).astype(BF)
        for half in (0, 1):
            part = wide[:, half * 128 : half * 128 + 128]
            term2[2 * i + half, pl.ds(0, 256)] = part
            total += gain[pl.ds(2 * i + half, 1), :] * part.astype(F32) * flat(
                xb[2 * i + half]
            ).astype(F32)
        return total

    inner = lax.fori_loop(0, 8, norm_term, jnp.zeros((256, HEAD), F32), unroll=2)
    inner = jnp.sum(jnp.transpose(inner), axis=0, keepdims=True)
    at_row = lax.broadcasted_iota(jnp.int32, (16, HEAD), 0)
    inner = jnp.where(at_row == 0, inner[:, :128], jnp.where(at_row == 1, inner[:, 128:], 0.0))
    high = inner.astype(BF)
    low = (inner - high.astype(F32)).astype(BF)
    for m in range(16):
        term2[m, pl.ds(256, 16)] = high
        term2[m, pl.ds(272, 16)] = low

    def token_flow():
        yield from net.scatter_sum(term2, rb2, zs2, zb2)
        total = net.received(term2, rb2, 1, net.zl) + zb2[...].astype(F32)
        while any(item[1] is sum_1 for item in net.flows):
            yield 6.43
        summed = net.received(term1, rb1, 1, net.zl) + zb1[...].astype(F32)
        local = flat(xb[mp]).astype(F32)
        done_both[:, :, 0] = (local + summed).astype(BF).reshape(4, 4, 16, HEAD)
        rows = total[256:272] + total[272:288]
        rows = jnp.concatenate(
            [jnp.transpose(jnp.broadcast_to(rows[k : k + 1], (HEAD, HEAD))) for k in (0, 1)], axis=0
        )
        scale_own = inv[...]
        grad = (
            flat(gb[mp]).astype(F32)
            + scale_own * gain[pl.ds(mp, 1), :] * total[:256]
            - local * (scale_own * scale_own * scale_own) * rows * (1.0 / 2048)
        )
        done_both[:, :, 1] = grad.astype(BF).reshape(4, 4, 16, HEAD)
        yield 0.14
        yield from net.patches_to_frames(done_both, back_mid, back_both)
        store(back_both.at[:, :, 0], lo_out)
        store(back_both.at[:, :, 1], ig_out)

    net.start(token_flow())
    net.finish()
    net.close()
    for copy in stores:
        copy.wait()


def bf(*shape):
    return pltpu.VMEM(shape, BF)


def f32(*shape):
    return pltpu.VMEM(shape, F32)


def shards(frames_in, norm_gain, w_qkv, w_out, cotangent):
    hbm = pl.BlockSpec(memory_space=pltpu.HBM)
    block = (4, 4, 16, HEAD)
    scratch = [
        bf(4, 4, 2, 16, HEAD), bf(4, 4, 2, 16, HEAD), bf(16, HEAD),
        bf(16, *block), bf(16, *block),
        bf(2048, 384), bf(HEAD, 2048),
        f32(16, HEAD), f32(256, HEAD),
        bf(256, 2048), bf(2048, 256),
        bf(256, 384), bf(256, HEAD), bf(HEAD, 256),
        f32(256, 256), bf(256, 256),
        bf(256, HEAD), bf(256, 384),
        bf(16, 256, HEAD), bf(14, 256, HEAD), bf(256, HEAD), bf(256, HEAD),
        bf(16, ROWS, HEAD), bf(14, ROWS, HEAD), bf(ROWS, HEAD), bf(ROWS, HEAD),
        bf(4, 4, 3, HEAD, HEAD),
        bf(4, 3, HEAD, HEAD), bf(4, 3, HEAD, HEAD), bf(4, 3, HEAD, HEAD),
        bf(2, 3, HEAD, HEAD),
        bf(3, HEAD, HEAD), bf(3, HEAD, HEAD), bf(3, HEAD, HEAD),
        bf(4, 4, HEAD, HEAD), bf(4, HEAD, HEAD), bf(4, HEAD, HEAD),
        bf(4, HEAD, HEAD), bf(4, HEAD, HEAD),
        bf(HEAD, HEAD), bf(HEAD, HEAD), bf(HEAD, HEAD),
        bf(4, 4, 3, HEAD, HEAD), bf(HEAD, HEAD),
        bf(4, 4, 2, 16, HEAD), bf(4, 4, 2, 16, HEAD), bf(4, 4, 2, 16, HEAD),
        pltpu.SemaphoreType.DMA((COPIES,)),
        pltpu.SemaphoreType.DMA((COPIES,)),
        pltpu.SemaphoreType.DMA((11,)),
    ]
    layer_out, input_grad, qkv_weight_grad, out_weight_grad = pl.pallas_call(
        kernel,
        out_shape=(
            jax.ShapeDtypeStruct(block, BF),
            jax.ShapeDtypeStruct(block, BF),
            jax.ShapeDtypeStruct((4, 4, HEAD, 384), BF),
            jax.ShapeDtypeStruct((HEAD, HEAD), BF),
        ),
        in_specs=[hbm] * 5,
        out_specs=(hbm,) * 4,
        scratch_shapes=scratch,
        compiler_params=pltpu.CompilerParams(
            collective_id=0, has_side_effects=True, vmem_limit_bytes=55040 * 1024
        ),
        name="sublayer",
    )(frames_in.reshape(block), norm_gain.reshape(16, HEAD), w_qkv, w_out, cotangent.reshape(block))
    return (
        layer_out.reshape(1, 256, HEAD),
        input_grad.reshape(1, 256, HEAD),
        qkv_weight_grad.reshape(2048, 384),
        out_weight_grad,
    )


def solution(mesh):
    return jax.shard_map(
        shards,
        mesh=mesh,
        in_specs=(
            P(("clip", "seq"), None, "mp"),
            P(),
            P(None, "mp"),
            P("mp", None),
            P(("clip", "seq"), None, "mp"),
        ),
        out_specs=(
            P(("clip", "seq"), None, "mp"),
            P(("clip", "seq"), None, "mp"),
            P("clip", "mp"),
            P(("clip", "mp"), "seq"),
        ),
        check_vma=False,
    )
```

```python
import jax
import jax.numpy as jnp
from jax import lax
from jax.experimental import pallas as pl
from jax.experimental.pallas import tpu as pltpu
from jax.sharding import PartitionSpec as P

HEAD = 128
EPS = 1e-05
BF = jnp.bfloat16
F32 = jnp.float32
MESH = pl.DeviceIdType.MESH
COPIES = 112
ROWS = 288
SCALE = HEAD ** (-0.5)
NT = (((1,), (1,)), ((), ()))


def mm(a, b):
    return jnp.dot(a, b, preferred_element_type=F32)


def mm_nt(a, b):
    return lax.dot_general(a, b, NT, preferred_element_type=F32)


def mm_tn(a, b):
    return lax.dot_general(a, b, (((0,), (0,)), ((), ())), preferred_element_type=F32)


class Net:
    def __init__(self, ssem, rsem):
        self.ssem, self.rsem, self.started, self.flows, self.clock, self.steps = ssem, rsem, [], [], 0.0, {}
        self.drained = 0
        clip, seq, mp = lax.axis_index("clip"), lax.axis_index("seq"), lax.axis_index("mp")
        self.clip, self.seq, self.mp = clip, seq, mp
        self.zh, self.x = seq // 4, seq & 3
        self.zl, self.y = mp // 8, mp & 7
        self.e = 1 - 2 * clip
        self.zp = 1 - self.zl
        self.dev_pair = (clip, seq, self.zp * 8 + self.y)
        barrier = pltpu.get_barrier_semaphore()
        peers = [self.dev_x(self.x_at(s)) for s in (1, 2, 3)]
        peers += [self.dev_z(self.z_at(s)) for s in (1, 2, 3)]
        peers += [self.dev_y(self.y_at(s)) for s in (1, -1, 2, -2)] + [self.dev_pair]
        for peer in peers:
            pl.semaphore_signal(barrier, inc=1, device_id=peer, device_id_type=MESH)
        pl.semaphore_wait(barrier, len(peers))

    def x_at(self, step):
        return (self.x + step) & 3

    def z_at(self, step):
        return (self.zh + step) & 3

    def y_at(self, step):
        return (self.y + step) & 7

    def dev_x(self, to):
        return (self.clip, self.zh * 4 + to, self.mp)

    def dev_z(self, to):
        return (self.clip, to * 4 + self.x, self.mp)

    def dev_y(self, to):
        return (self.clip, self.seq, self.zl * 8 + to)

    def send(self, src, dst, device):
        at = len(self.started)
        copy = pltpu.make_async_remote_copy(
            src_ref=src,
            dst_ref=dst,
            send_sem=self.ssem.at[at],
            recv_sem=self.rsem.at[at],
            device_id=device,
            device_id_type=MESH,
        )
        copy.start()
        self.started.append(copy)
        return copy

    def start(self, flow):
        self.flows.append([self.clock + next(flow), flow])
        return flow

    def step(self, item=None):
        item = item or min(self.flows, key=lambda entry: entry[0])
        for _ in range(2):
            if self.drained < len(self.started) - 24:
                self.started[self.drained].wait_send()
                self.drained += 1
        self.clock = max(self.clock, item[0])
        wait = next(item[1], None)
        self.steps[id(item[1])] = self.steps.get(id(item[1]), 0) + 1
        if wait is None:
            self.flows.remove(item)
        else:
            item[0] = self.clock + wait

    def until(self, flow, steps):
        while self.steps.get(id(flow), 0) < steps:
            self.step(next(entry for entry in self.flows if entry[1] is flow))

    def finish(self, flow=None):
        while any(flow is None or item[1] is flow for item in self.flows):
            self.step()

    def passed(self, time):
        target = self.clock + time
        while self.flows and min(item[0] for item in self.flows) <= target:
            self.step()
        self.clock = target

    def close(self):
        for copy in self.started[self.drained :]:
            copy.wait_send()

    def frames_to_patches(self, src, mid, xb, gb):
        zh, x, mp = self.zh, self.x, self.mp
        sent = []
        for s in (1, 3, 2):
            to = self.x_at(s)
            sent.append(self.send(src.at[:, to], mid.at[x], self.dev_x(to)))
        mid[x] = src[:, x]
        yield 7.15
        for copy in sent:
            copy.wait_recv()
        sent = []
        for half, dst in ((0, xb), (1, gb)):
            for s in (1, 3, 2):
                to = self.z_at(s)
                sent.append(self.send(mid.at[:, to, half], dst.at[mp, zh], self.dev_z(to)))
            dst[mp, zh] = mid[:, zh, half]
        for some in (sent[:3], sent[3:]):
            yield 6.52
            for copy in some:
                copy.wait_recv()

    def patches_to_frames(self, src, mid, dst):
        zh, x = self.zh, self.x
        sent = []
        for s in (1, 3, 2):
            to = self.z_at(s)
            sent.append(self.send(src.at[to], mid.at[zh], self.dev_z(to)))
        mid[zh] = src[zh]
        yield 27.35
        for copy in sent:
            copy.wait_recv()
        sent = []
        for s in (1, 3, 2):
            to = self.x_at(s)
            sent.append(self.send(mid.at[:, to], dst.at[:, x], self.dev_x(to)))
        dst[:, x] = mid[:, x]
        yield 1984.76
        for copy in sent:
            copy.wait_recv()

    def gather(self, buf):
        def pass_on(block, device):
            return self.send(buf.at[block], buf.at[block], device)

        ahead, back = self.dev_y(self.y_at(self.e)), self.dev_y(self.y_at(-self.e))

        def own(step):
            return self.zl * 8 + self.y_at(step)

        def other(step):
            return self.zp * 8 + self.y_at(step)

        a = pass_on(self.mp, ahead)
        b = pass_on(self.mp, back)
        pair = [pass_on(self.mp, self.dev_pair)]
        yield 3.68
        a.wait_recv()
        a = pass_on(own(-self.e), ahead)
        yield 0.51
        b.wait_recv()
        b = pass_on(own(self.e), back)
        yield 1.02
        pair[0].wait_recv()
        c = pass_on(other(0), ahead)
        d = pass_on(other(0), back)
        yield 2.08
        a.wait_recv()
        a = pass_on(own(-2 * self.e), ahead)
        yield 2.06
        b.wait_recv()
        b = pass_on(own(2 * self.e), back)
        pair.append(pass_on(own(2 * self.e), self.dev_pair))
        yield 0.71
        c.wait_recv()
        c = pass_on(other(-self.e), ahead)
        yield 0.45
        d.wait_recv()
        yield 0.94
        a.wait_recv()
        a = pass_on(own(-3 * self.e), ahead)
        pair.append(pass_on(own(-3 * self.e), self.dev_pair))
        yield 0.38
        b.wait_recv()
        pair.append(pass_on(own(3 * self.e), self.dev_pair))
        yield 2.71
        c.wait_recv()
        yield 0.3
        a.wait_recv()
        pair.append(pass_on(own(-4 * self.e), self.dev_pair))
        for copy in pair[1:]:
            yield 1.54
            copy.wait_recv()

    def scatter_sum(self, term, rb, zs, zb):
        planes = (self.zp, self.zl)
        ways = ((self.e, 4), (-self.e, 3))
        order = [(i, j) for i in (0, 1) for j in (0, 1)]

        def slot(i, j, k):
            return i * 7 + j * 4 + k - 1

        sent = {}
        for i, j in order:
            way, steps = ways[j]
            dest = planes[i] * 8 + self.y_at(steps * way)
            sent[i, j] = self.send(term.at[dest], rb.at[slot(i, j, 1)], self.dev_y(self.y_at(way)))
        last = None
        for k in (1, 2, 3, 4):
            for i, j in order:
                way, steps = ways[j]
                if k > steps:
                    continue
                yield 5.6 if (i, j) == (0, 0) else 0.7
                sent[i, j].wait_recv()
                here = rb.at[slot(i, j, k)]
                if k < steps:
                    dest = planes[i] * 8 + self.y_at((steps - k) * way)
                    fold(here, here[...].astype(F32) + term[dest].astype(F32))
                    after = rb.at[slot(i, j, k + 1)]
                    sent[i, j] = self.send(here, after, self.dev_y(self.y_at(way)))
                elif k == 4 and i == 0:
                    fold(zs, self.received(term, rb, 0, self.zp))
                    last = self.send(zs, zb, self.dev_pair)
        yield 60.63
        last.wait_recv()

    def received(self, term, rb, i, plane):
        return (
            term[plane * 8 + self.y].astype(F32)
            + rb[7 * i + 3].astype(F32)
            + rb[7 * i + 6].astype(F32)
        )

    def weight_sum(self, piece, wg, tx, px, mx, sx, tz, pz, mz, res, done):
        zh, x, e = self.zh, self.x, self.e
        xp, xm, zm = self.x_at(e), self.x_at(-e), self.z_at(-e)
        ahead, back = self.dev_x(xp), self.dev_x(xm)
        z_ahead, z_back = self.dev_z(self.z_at(e)), self.dev_z(zm)
        q = (self.z_at(2), self.z_at(e), zm, zh)
        far, plain, near = [], [], []

        def here(i):
            return wg[q[i], x].astype(F32) + px[i].astype(F32) + mx[i].astype(F32)

        for i in range(4):
            piece(q[i])
            far.append(self.send(wg.at[q[i], self.x_at(2)], tx.at[i], ahead))
            plain.append(self.send(wg.at[q[i], xm], px.at[i], back))
            if i < 3:
                yield 0.38
        for i in range(4):
            yield 2.1
            far[i].wait_recv()
            tx[i] = (tx[i].astype(F32) + wg[q[i], xp].astype(F32)).astype(BF)
            near.append(self.send(tx.at[i], mx.at[i], ahead))
        yield 1.77
        plain[0].wait_recv()
        near[0].wait_recv()
        sx[0] = here(0).astype(BF)
        z_far = self.send(sx.at[0], tz, z_ahead)
        for i in (1, 2):
            yield 0.55
            plain[i].wait_recv()
            near[i].wait_recv()
        sx[1] = here(2).astype(BF)
        z_plain = self.send(sx.at[1], pz, z_back)
        yield 1.95
        z_far.wait_recv()
        tz[...] = (tz[...].astype(F32) + here(1)).astype(BF)
        z_near = self.send(tz, mz, z_ahead)
        yield 2.93
        plain[3].wait_recv()
        near[3].wait_recv()
        yield 4.72
        z_plain.wait_recv()
        z_near.wait_recv()
        total = (here(3) + pz[...].astype(F32) + mz[...].astype(F32)).astype(BF)
        res[zh, x] = total

        def pass_on(at, column, device):
            return self.send(res.at[at, column], res.at[at, column], device)

        up, down = pass_on(zh, x, z_ahead), pass_on(zh, x, z_back)
        first, second, third = [pass_on(zh, x, ahead)], [pass_on(zh, x, back)], []
        yield 12.46
        up.wait_recv()
        up = pass_on(zm, x, z_ahead)
        first.append(pass_on(zm, x, ahead))
        second.append(pass_on(zm, x, back))
        yield 9.17
        down.wait_recv()
        first.append(pass_on(q[1], x, ahead))
        second.append(pass_on(q[1], x, back))
        yield 0.39
        first[0].wait_recv()
        third.append(pass_on(zh, xm, ahead))
        yield 61.54
        up.wait_recv()
        first.append(pass_on(q[0], x, ahead))
        second.append(pass_on(q[0], x, back))
        for i, at in ((1, zm), (2, q[1]), (3, q[0])):
            yield 1.41
            first[i].wait_recv()
            third.append(pass_on(at, xm, ahead))
        for copy in second + third:
            yield 3.28
            copy.wait_recv()
        done()

    def out_sum(self, wo, tx, px, mx, sx, tz, pz, mz, done):
        zh, x, e = self.zh, self.x, self.e
        xp, xm, zm = self.x_at(e), self.x_at(-e), self.z_at(-e)
        ahead, back = self.dev_x(xp), self.dev_x(xm)
        z_ahead, z_back = self.dev_z(self.z_at(e)), self.dev_z(zm)
        far = self.send(wo.at[:, self.x_at(2)], tx, ahead)
        plain = self.send(wo.at[:, xm], px, back)
        yield 14.21
        far.wait_recv()
        tx[...] = (tx[...].astype(F32) + wo[:, xp].astype(F32)).astype(BF)
        near = self.send(tx, mx, ahead)
        yield 9.55
        plain.wait_recv()
        near.wait_recv()
        sx[...] = (wo[:, x].astype(F32) + px[...].astype(F32) + mx[...].astype(F32)).astype(BF)
        z_far = self.send(sx.at[self.z_at(2)], tz, z_ahead)
        z_plain = self.send(sx.at[zm], pz, z_back)
        yield 1.99
        z_far.wait_recv()
        tz[...] = (tz[...].astype(F32) + sx[self.z_at(e)].astype(F32)).astype(BF)
        z_near = self.send(tz, mz, z_ahead)
        yield 47.05
        z_plain.wait_recv()
        z_near.wait_recv()
        total = wo[zh, x].astype(F32) + px[zh].astype(F32) + mx[zh].astype(F32)
        done((total + pz[...].astype(F32) + mz[...].astype(F32)).astype(BF))


def flat(block):
    return block.reshape(256, HEAD)


def fold(ref, total):
    ref[pl.ds(0, 256)] = total[:256].astype(BF)
    if total.shape[0] == ROWS:
        inner = total[256:272] + total[272:288]
        high = inner.astype(BF)
        ref[pl.ds(256, 16)] = high
        ref[pl.ds(272, 16)] = (inner - high.astype(F32)).astype(BF)


def kernel(
    x_hbm, gain_hbm, wqkv_hbm, wout_hbm, g_hbm,
    lo_out, ig_out, dwqkv_out, dwo_out,
    both, mid, gain_ref, xb, gb, wqkv, wout, gain, inv, norm, norm_t, qkv, att, att_t,
    probs, probs_t, gheads, dqkv, term1, rb1, zs1, zb1, term2, rb2, zs2, zb2,
    wg, tx, px, mx, sx, tz, pz, mz, wo, txo, pxo, mxo, sxo, tzo, pzo, mzo, res, dwo, done_both, back_mid, back_both,
    ssem, rsem, lsem,
):
    loads = [
        pltpu.make_async_copy(src, dst, lsem.at[at])
        for at, (src, dst) in enumerate(
            [
                (x_hbm, both.at[:, :, 0]),
                (g_hbm, both.at[:, :, 1]),
                (gain_hbm, gain_ref),
                (wqkv_hbm, wqkv),
                (wout_hbm, wout),
            ]
        )
    ]
    for load in loads:
        load.start()
    stores = []

    def store(src, dst):
        stores.append(pltpu.make_async_copy(src, dst, lsem.at[len(loads) + len(stores)]))
        stores[-1].start()

    net = Net(ssem, rsem)
    mp = net.mp

    for load in loads[:3]:
        load.wait()
    bring = net.start(net.frames_to_patches(both, mid, xb, gb))
    gain[...] = gain_ref[...].astype(F32)
    net.step()
    net.step()
    gather_x = net.start(net.gather(xb))
    net.finish(bring)
    net.until(gather_x, 1)
    gather_g = net.start(net.gather(gb))
    net.finish(gather_x)

    def square(m, total):
        block = flat(xb[m]).astype(F32)
        return total + block * block

    squares = lax.fori_loop(0, 16, square, jnp.zeros((256, HEAD), F32))
    mean = jnp.sum(squares, axis=-1, keepdims=True) * (1.0 / 2048)
    inv[...] = jnp.broadcast_to(lax.rsqrt(mean + EPS), (256, HEAD))

    def normalise(m, carry):
        block = flat(xb[m]).astype(F32) * inv[...] * gain[pl.ds(m, 1), :]
        norm[:, pl.ds(pl.multiple_of(m * 128, 128), 128)] = block.astype(BF)
        return carry

    lax.fori_loop(0, 16, normalise, 0, unroll=2)
    net.passed(0.85)
    for load in loads[3:]:
        load.wait()
    qkv[...] = mm(norm[...], wqkv[...]).astype(BF)
    net.passed(0.07)

    scale = HEAD ** (-0.5)
    rows = lax.broadcasted_iota(jnp.int32, (256, 256), 0)
    cols = lax.broadcasted_iota(jnp.int32, (256, 256), 1)
    keep = (((rows - cols) & 15) == 0) & (cols <= rows)
    queries, keys, values = (qkv[:, pl.ds(i * 128, 128)] for i in range(3))
    scores = jnp.where(keep, mm_nt(queries, keys) * scale, -1e30)
    expo = jnp.exp(scores - jnp.max(scores, axis=-1, keepdims=True))
    soft = expo / jnp.sum(expo, axis=-1, keepdims=True)
    probs[...] = soft
    attended = mm(soft.astype(BF), values)
    att[...] = attended.astype(BF)
    net.passed(1.58)

    def out_term(i, carry):
        wide = mm(att[...], wout[:, pl.ds(pl.multiple_of(i * 256, 256), 256)]).astype(BF)
        term1[2 * i] = wide[:, :128]
        term1[2 * i + 1] = wide[:, 128:]
        return carry

    lax.fori_loop(0, 8, out_term, 0, unroll=4)
    net.passed(0.2)

    att_t[...] = jnp.transpose(attended).astype(BF)
    probs_t[...] = jnp.transpose(soft).astype(BF)

    def turn(m, carry):
        at = pl.multiple_of(m * 128, 128)
        block = norm[:, pl.ds(at, 128)].astype(F32)
        norm_t[pl.ds(at, 128), :] = jnp.transpose(block).astype(BF)
        return carry

    lax.fori_loop(0, 16, turn, 0, unroll=2)
    net.finish(gather_g)

    def pair_of(i):
        return jnp.concatenate([flat(gb[2 * i]), flat(gb[2 * i + 1])], axis=1)

    sum_1 = net.start(net.scatter_sum(term1, rb1, zs1, zb1))
    for i in range(8):
        wide = mm(att_t[...], pair_of(i)).astype(BF)
        wo[i // 2, 2 * (i % 2)] = wide[:, :128]
        wo[i // 2, 2 * (i % 2) + 1] = wide[:, 128:]

    def out_stored(total):
        dwo[...] = total
        store(dwo, dwo_out)

    net.start(net.out_sum(wo, txo, pxo, mxo, sxo, tzo, pzo, mzo, out_stored))
    total = jnp.zeros((256, HEAD), F32)
    for i in range(8):
        total += mm_nt(pair_of(i), wout[:, pl.ds(i * 256, 256)])
    gheads[...] = total.astype(BF)
    net.passed(2.96)

    dqkv[:, pl.ds(256, 128)] = mm(probs_t[...], gheads[...]).astype(BF)
    dprobs = mm_nt(gheads[...], qkv[:, pl.ds(256, 128)]).astype(BF).astype(F32)
    soft = probs[...]
    delta = jnp.sum(soft * dprobs, axis=-1, keepdims=True)
    dscores = soft * (dprobs - delta) * scale
    high = dscores.astype(BF)
    low = (dscores - high.astype(F32)).astype(BF)
    keys = qkv[:, pl.ds(128, 128)]
    dqkv[:, pl.ds(0, 128)] = (mm(high, keys) + mm(low, keys)).astype(BF)
    turned = jnp.transpose(dscores)
    high = turned.astype(BF)
    low = (turned - high.astype(F32)).astype(BF)
    queries = qkv[:, pl.ds(0, 128)]
    dqkv[:, pl.ds(128, 128)] = (mm(high, queries) + mm(low, queries)).astype(BF)

    def piece(q):
        for half in range(2):
            at = q * 4 + half * 2
            rows = norm_t[pl.ds(pl.multiple_of(at * 128, 256), 256), :]
            tall = mm(rows, dqkv[...]).astype(BF)
            for k in range(2):
                for c in range(3):
                    wg[q, 2 * half + k, c] = tall[k * 128 : k * 128 + 128, c * 128 : c * 128 + 128]

    def stored():
        for c in range(3):
            store(res.at[:, :, c], dwqkv_out.at[:, :, :, pl.ds(c * 128, 128)])

    net.start(net.weight_sum(piece, wg, tx, px, mx, sx, tz, pz, mz, res, stored))
    net.passed(0.78)

    def norm_term(i, total):
        tall = wqkv[pl.ds(pl.multiple_of(i * 256, 256), 256), :]
        wide = mm_nt(dqkv[...], tall).astype(BF)
        for half in (0, 1):
            part = wide[:, half * 128 : half * 128 + 128]
            term2[2 * i + half, pl.ds(0, 256)] = part
            total += gain[pl.ds(2 * i + half, 1), :] * part.astype(F32) * flat(
                xb[2 * i + half]
            ).astype(F32)
        return total

    inner = lax.fori_loop(0, 8, norm_term, jnp.zeros((256, HEAD), F32), unroll=2)
    inner = jnp.sum(jnp.transpose(inner), axis=0, keepdims=True)
    at_row = lax.broadcasted_iota(jnp.int32, (16, HEAD), 0)
    inner = jnp.where(at_row == 0, inner[:, :128], jnp.where(at_row == 1, inner[:, 128:], 0.0))
    high = inner.astype(BF)
    low = (inner - high.astype(F32)).astype(BF)
    for m in range(16):
        term2[m, pl.ds(256, 16)] = high
        term2[m, pl.ds(272, 16)] = low

    def token_flow():
        yield from net.scatter_sum(term2, rb2, zs2, zb2)
        total = net.received(term2, rb2, 1, net.zl) + zb2[...].astype(F32)
        while any(item[1] is sum_1 for item in net.flows):
            yield 6.73
        summed = net.received(term1, rb1, 1, net.zl) + zb1[...].astype(F32)
        local = flat(xb[mp]).astype(F32)
        done_both[:, :, 0] = (local + summed).astype(BF).reshape(4, 4, 16, HEAD)
        rows = total[256:272] + total[272:288]
        rows = jnp.concatenate(
            [jnp.transpose(jnp.broadcast_to(rows[k : k + 1], (HEAD, HEAD))) for k in (0, 1)], axis=0
        )
        scale_own = inv[...]
        grad = (
            flat(gb[mp]).astype(F32)
            + scale_own * gain[pl.ds(mp, 1), :] * total[:256]
            - local * (scale_own * scale_own * scale_own) * rows * (1.0 / 2048)
        )
        done_both[:, :, 1] = grad.astype(BF).reshape(4, 4, 16, HEAD)
        yield 1.41
        yield from net.patches_to_frames(done_both, back_mid, back_both)
        store(back_both.at[:, :, 0], lo_out)
        store(back_both.at[:, :, 1], ig_out)

    net.start(token_flow())
    net.finish()
    net.close()
    for copy in stores:
        copy.wait()


def bf(*shape):
    return pltpu.VMEM(shape, BF)


def f32(*shape):
    return pltpu.VMEM(shape, F32)


def shards(frames_in, norm_gain, w_qkv, w_out, cotangent):
    hbm = pl.BlockSpec(memory_space=pltpu.HBM)
    block = (4, 4, 16, HEAD)
    scratch = [
        bf(4, 4, 2, 16, HEAD), bf(4, 4, 2, 16, HEAD), bf(16, HEAD),
        bf(16, *block), bf(16, *block),
        bf(2048, 384), bf(HEAD, 2048),
        f32(16, HEAD), f32(256, HEAD),
        bf(256, 2048), bf(2048, 256),
        bf(256, 384), bf(256, HEAD), bf(HEAD, 256),
        f32(256, 256), bf(256, 256),
        bf(256, HEAD), bf(256, 384),
        bf(16, 256, HEAD), bf(14, 256, HEAD), bf(256, HEAD), bf(256, HEAD),
        bf(16, ROWS, HEAD), bf(14, ROWS, HEAD), bf(ROWS, HEAD), bf(ROWS, HEAD),
        bf(4, 4, 3, HEAD, HEAD),
        bf(4, 3, HEAD, HEAD), bf(4, 3, HEAD, HEAD), bf(4, 3, HEAD, HEAD),
        bf(2, 3, HEAD, HEAD),
        bf(3, HEAD, HEAD), bf(3, HEAD, HEAD), bf(3, HEAD, HEAD),
        bf(4, 4, HEAD, HEAD), bf(4, HEAD, HEAD), bf(4, HEAD, HEAD),
        bf(4, HEAD, HEAD), bf(4, HEAD, HEAD),
        bf(HEAD, HEAD), bf(HEAD, HEAD), bf(HEAD, HEAD),
        bf(4, 4, 3, HEAD, HEAD), bf(HEAD, HEAD),
        bf(4, 4, 2, 16, HEAD), bf(4, 4, 2, 16, HEAD), bf(4, 4, 2, 16, HEAD),
        pltpu.SemaphoreType.DMA((COPIES,)),
        pltpu.SemaphoreType.DMA((COPIES,)),
        pltpu.SemaphoreType.DMA((11,)),
    ]
    layer_out, input_grad, qkv_weight_grad, out_weight_grad = pl.pallas_call(
        kernel,
        out_shape=(
            jax.ShapeDtypeStruct(block, BF),
            jax.ShapeDtypeStruct(block, BF),
            jax.ShapeDtypeStruct((4, 4, HEAD, 384), BF),
            jax.ShapeDtypeStruct((HEAD, HEAD), BF),
        ),
        in_specs=[hbm] * 5,
        out_specs=(hbm,) * 4,
        scratch_shapes=scratch,
        compiler_params=pltpu.CompilerParams(
            collective_id=0, has_side_effects=True, vmem_limit_bytes=55040 * 1024
        ),
        name="sublayer",
    )(frames_in.reshape(block), norm_gain.reshape(16, HEAD), w_qkv, w_out, cotangent.reshape(block))
    return (
        layer_out.reshape(1, 256, HEAD),
        input_grad.reshape(1, 256, HEAD),
        qkv_weight_grad.reshape(2048, 384),
        out_weight_grad,
    )


def solution(mesh):
    return jax.shard_map(
        shards,
        mesh=mesh,
        in_specs=(
            P(("clip", "seq"), None, "mp"),
            P(),
            P(None, "mp"),
            P("mp", None),
            P(("clip", "seq"), None, "mp"),
        ),
        out_specs=(
            P(("clip", "seq"), None, "mp"),
            P(("clip", "seq"), None, "mp"),
            P("clip", "mp"),
            P(("clip", "mp"), "seq"),
        ),
        check_vma=False,
    )
```

```python
import jax
import jax.numpy as jnp
from jax import lax
from jax.experimental import pallas as pl
from jax.experimental.pallas import tpu as pltpu
from jax.sharding import PartitionSpec as P

HEAD = 128
EPS = 1e-05
BF = jnp.bfloat16
F32 = jnp.float32
MESH = pl.DeviceIdType.MESH
COPIES = 159
ROWS = 288
SCALE = HEAD ** (-0.5)
NT = (((1,), (1,)), ((), ()))


def mm(a, b):
    return jnp.dot(a, b, preferred_element_type=F32)


def mm_nt(a, b):
    return lax.dot_general(a, b, NT, preferred_element_type=F32)


def mm_tn(a, b):
    return lax.dot_general(a, b, (((0,), (0,)), ((), ())), preferred_element_type=F32)


class Net:
    def __init__(self, ssem, rsem):
        self.ssem, self.rsem, self.started, self.flows, self.clock, self.steps = ssem, rsem, [], [], 0.0, {}
        self.drained = 0
        clip, seq, mp = lax.axis_index("clip"), lax.axis_index("seq"), lax.axis_index("mp")
        self.clip, self.seq, self.mp = clip, seq, mp
        self.zh, self.x = seq // 4, seq & 3
        self.zl, self.y = mp // 8, mp & 7
        self.e = 1 - 2 * clip
        self.zp = 1 - self.zl
        self.dev_pair = (clip, seq, self.zp * 8 + self.y)
        barrier = pltpu.get_barrier_semaphore()
        peers = [(clip, (seq + s) & 15, mp) for s in range(1, 16)]
        peers += [self.dev_y(self.y_at(s)) for s in (1, -1, 2, -2)] + [self.dev_pair]
        for peer in peers:
            pl.semaphore_signal(barrier, inc=1, device_id=peer, device_id_type=MESH)
        pl.semaphore_wait(barrier, len(peers))

    def x_at(self, step):
        return (self.x + step) & 3

    def z_at(self, step):
        return (self.zh + step) & 3

    def y_at(self, step):
        return (self.y + step) & 7

    def dev_x(self, to):
        return (self.clip, self.zh * 4 + to, self.mp)

    def dev_z(self, to):
        return (self.clip, to * 4 + self.x, self.mp)

    def dev_y(self, to):
        return (self.clip, self.seq, self.zl * 8 + to)

    def send(self, src, dst, device):
        at = len(self.started)
        copy = pltpu.make_async_remote_copy(
            src_ref=src,
            dst_ref=dst,
            send_sem=self.ssem.at[at],
            recv_sem=self.rsem.at[at],
            device_id=device,
            device_id_type=MESH,
        )
        copy.start()
        self.started.append(copy)
        return copy

    def start(self, flow):
        self.flows.append([self.clock + next(flow), flow])
        return flow

    def step(self, item=None):
        item = item or min(self.flows, key=lambda entry: entry[0])
        for _ in range(2):
            if self.drained < len(self.started) - 24:
                self.started[self.drained].wait_send()
                self.drained += 1
        self.clock = max(self.clock, item[0])
        wait = next(item[1], None)
        self.steps[id(item[1])] = self.steps.get(id(item[1]), 0) + 1
        if wait is None:
            self.flows.remove(item)
        else:
            item[0] = self.clock + wait

    def until(self, flow, steps):
        while self.steps.get(id(flow), 0) < steps:
            self.step(next(entry for entry in self.flows if entry[1] is flow))

    def finish(self, flow=None):
        while any(flow is None or item[1] is flow for item in self.flows):
            self.step()

    def passed(self, time):
        target = self.clock + time
        while self.flows and min(item[0] for item in self.flows) <= target:
            self.step()
        self.clock = target

    def close(self):
        for copy in self.started[self.drained :]:
            copy.wait_send()

    def frames_to_patches(self, src, mid, xb, gb):
        zh, x, mp = self.zh, self.x, self.mp
        sent = []
        for s in range(1, 16):
            to = (self.seq + s) & 15
            there = (self.clip, to, mp)
            sent.append(self.send(src.at[to // 4, to & 3], mid.at[zh, x], there))
        mid[zh, x] = src[zh, x]
        yield 2.99
        for copy in sent:
            copy.wait_recv()
        xb[mp] = mid[:, :, 0]
        gb[mp] = mid[:, :, 1]

    def patches_to_frames(self, src, dst):
        sent = []
        for s in range(1, 16):
            to = (self.seq + s) & 15
            there = self.dev_far(to)
            sent.append(self.send(src.at[to // 4, to & 3], dst.at[self.zh, self.x], there))
        dst[self.zh, self.x] = src[self.zh, self.x]
        yield 71.26
        for copy in sent:
            copy.wait_recv()

    def dev_far(self, seq):
        return (self.clip, seq, self.mp)

    def gather(self, buf):
        def pass_on(block, device):
            return self.send(buf.at[block], buf.at[block], device)

        ahead, back = self.dev_y(self.y_at(self.e)), self.dev_y(self.y_at(-self.e))

        def own(step):
            return self.zl * 8 + self.y_at(step)

        def other(step):
            return self.zp * 8 + self.y_at(step)

        a = pass_on(self.mp, ahead)
        b = pass_on(self.mp, back)
        pair = [pass_on(self.mp, self.dev_pair)]
        yield 3.61
        a.wait_recv()
        a = pass_on(own(-self.e), ahead)
        yield 2.72
        b.wait_recv()
        b = pass_on(own(self.e), back)
        yield 0.5
        pair[0].wait_recv()
        c = pass_on(other(0), ahead)
        d = pass_on(other(0), back)
        yield 1.77
        a.wait_recv()
        a = pass_on(own(-2 * self.e), ahead)
        yield 1.94
        b.wait_recv()
        b = pass_on(own(2 * self.e), back)
        pair.append(pass_on(own(2 * self.e), self.dev_pair))
        yield 0.06
        c.wait_recv()
        c = pass_on(other(-self.e), ahead)
        yield 1.11
        d.wait_recv()
        yield 1.01
        a.wait_recv()
        a = pass_on(own(-3 * self.e), ahead)
        pair.append(pass_on(own(-3 * self.e), self.dev_pair))
        yield 0.84
        b.wait_recv()
        pair.append(pass_on(own(3 * self.e), self.dev_pair))
        yield 2.24
        c.wait_recv()
        yield 0.05
        a.wait_recv()
        pair.append(pass_on(own(-4 * self.e), self.dev_pair))
        for copy in pair[1:]:
            yield 1.54
            copy.wait_recv()

    def scatter_sum(self, term, rb, zs, zb):
        planes = (self.zp, self.zl)
        ways = ((self.e, 4), (-self.e, 3))
        order = [(i, j) for i in (0, 1) for j in (0, 1)]

        def slot(i, j, k):
            return i * 7 + j * 4 + k - 1

        sent = {}
        for i, j in order:
            way, steps = ways[j]
            dest = planes[i] * 8 + self.y_at(steps * way)
            sent[i, j] = self.send(term.at[dest], rb.at[slot(i, j, 1)], self.dev_y(self.y_at(way)))
        last = None
        for k in (1, 2, 3, 4):
            for i, j in order:
                way, steps = ways[j]
                if k > steps:
                    continue
                yield 5.6 if (i, j) == (0, 0) else 0.99
                sent[i, j].wait_recv()
                here = rb.at[slot(i, j, k)]
                if k < steps:
                    dest = planes[i] * 8 + self.y_at((steps - k) * way)
                    fold(here, here[...].astype(F32) + term[dest].astype(F32))
                    after = rb.at[slot(i, j, k + 1)]
                    sent[i, j] = self.send(here, after, self.dev_y(self.y_at(way)))
                elif k == 4 and i == 0:
                    fold(zs, self.received(term, rb, 0, self.zp))
                    last = self.send(zs, zb, self.dev_pair)
        yield 30.06
        last.wait_recv()

    def received(self, term, rb, i, plane):
        return (
            term[plane * 8 + self.y].astype(F32)
            + rb[7 * i + 3].astype(F32)
            + rb[7 * i + 6].astype(F32)
        )

    def weight_sum(self, piece, wg, tx, px, mx, sx, tz, pz, mz, res, done):
        zh, x, e = self.zh, self.x, self.e
        xp, xm, zm = self.x_at(e), self.x_at(-e), self.z_at(-e)
        ahead, back = self.dev_x(xp), self.dev_x(xm)
        z_ahead, z_back = self.dev_z(self.z_at(e)), self.dev_z(zm)
        q = (self.z_at(2), self.z_at(e), zm, zh)
        far, plain, near = [], [], []

        def here(i):
            return wg[q[i], x].astype(F32) + px[i].astype(F32) + mx[i].astype(F32)

        for i in range(4):
            piece(q[i])
            far.append(self.send(wg.at[q[i], self.x_at(2)], tx.at[i], ahead))
            plain.append(self.send(wg.at[q[i], xm], px.at[i], back))
            if i < 3:
                yield 0.73
        for i in range(4):
            yield 1.97
            far[i].wait_recv()
            tx[i] = (tx[i].astype(F32) + wg[q[i], xp].astype(F32)).astype(BF)
            near.append(self.send(tx.at[i], mx.at[i], ahead))
        yield 1.86
        plain[0].wait_recv()
        near[0].wait_recv()
        sx[0] = here(0).astype(BF)
        z_far = self.send(sx.at[0], tz, z_ahead)
        for i in (1, 2):
            yield 1.82
            plain[i].wait_recv()
            near[i].wait_recv()
        sx[1] = here(2).astype(BF)
        z_plain = self.send(sx.at[1], pz, z_back)
        yield 1.67
        z_far.wait_recv()
        tz[...] = (tz[...].astype(F32) + here(1)).astype(BF)
        z_near = self.send(tz, mz, z_ahead)
        yield 2.93
        plain[3].wait_recv()
        near[3].wait_recv()
        yield 3.8
        z_plain.wait_recv()
        z_near.wait_recv()
        total = (here(3) + pz[...].astype(F32) + mz[...].astype(F32)).astype(BF)
        res[zh, x] = total

        def pass_on(at, column, device):
            return self.send(res.at[at, column], res.at[at, column], device)

        up, down = pass_on(zh, x, z_ahead), pass_on(zh, x, z_back)
        first, second, third = [pass_on(zh, x, ahead)], [pass_on(zh, x, back)], []
        yield 8.72
        up.wait_recv()
        up = pass_on(zm, x, z_ahead)
        first.append(pass_on(zm, x, ahead))
        second.append(pass_on(zm, x, back))
        yield 0.23
        down.wait_recv()
        first.append(pass_on(q[1], x, ahead))
        second.append(pass_on(q[1], x, back))
        yield 8.0
        first[0].wait_recv()
        third.append(pass_on(zh, xm, ahead))
        yield 61.54
        up.wait_recv()
        first.append(pass_on(q[0], x, ahead))
        second.append(pass_on(q[0], x, back))
        for i, at in ((1, zm), (2, q[1]), (3, q[0])):
            yield 3.2
            first[i].wait_recv()
            third.append(pass_on(at, xm, ahead))
        for copy in second + third:
            yield 47.18
            copy.wait_recv()
        done()

    def out_sum(self, wo, tx, px, mx, sx, tz, pz, mz, done):
        zh, x, e = self.zh, self.x, self.e
        xp, xm, zm = self.x_at(e), self.x_at(-e), self.z_at(-e)
        ahead, back = self.dev_x(xp), self.dev_x(xm)
        z_ahead, z_back = self.dev_z(self.z_at(e)), self.dev_z(zm)
        far = self.send(wo.at[:, self.x_at(2)], tx, ahead)
        plain = self.send(wo.at[:, xm], px, back)
        yield 20.24
        far.wait_recv()
        tx[...] = (tx[...].astype(F32) + wo[:, xp].astype(F32)).astype(BF)
        near = self.send(tx, mx, ahead)
        yield 23.11
        plain.wait_recv()
        near.wait_recv()
        sx[...] = (wo[:, x].astype(F32) + px[...].astype(F32) + mx[...].astype(F32)).astype(BF)
        z_far = self.send(sx.at[self.z_at(2)], tz, z_ahead)
        z_plain = self.send(sx.at[zm], pz, z_back)
        yield 70.29
        z_far.wait_recv()
        tz[...] = (tz[...].astype(F32) + sx[self.z_at(e)].astype(F32)).astype(BF)
        z_near = self.send(tz, mz, z_ahead)
        yield 3.93
        z_plain.wait_recv()
        z_near.wait_recv()
        total = wo[zh, x].astype(F32) + px[zh].astype(F32) + mx[zh].astype(F32)
        done((total + pz[...].astype(F32) + mz[...].astype(F32)).astype(BF))


def flat(block):
    return block.reshape(256, HEAD)


def fold(ref, total):
    ref[pl.ds(0, 256)] = total[:256].astype(BF)
    if total.shape[0] == ROWS:
        inner = total[256:272] + total[272:288]
        high = inner.astype(BF)
        ref[pl.ds(256, 16)] = high
        ref[pl.ds(272, 16)] = (inner - high.astype(F32)).astype(BF)


def kernel(
    x_hbm, gain_hbm, wqkv_hbm, wout_hbm, g_hbm,
    lo_out, ig_out, dwqkv_out, dwo_out,
    both, mid, gain_ref, xb, gb, wqkv, wout, gain, inv, norm, norm_t, qkv, att, att_t,
    probs, probs_t, gheads, dqkv, term1, rb1, zs1, zb1, term2, rb2, zs2, zb2,
    wv, txv, pxv, mxv, sxv, tzv, pzv, mzv, resv,
    wg, tx, px, mx, sx, tz, pz, mz, wo, txo, pxo, mxo, sxo, tzo, pzo, mzo, res, dwo, done_both, back_both,
    ssem, rsem, lsem,
):
    loads = [
        pltpu.make_async_copy(src, dst, lsem.at[at])
        for at, (src, dst) in enumerate(
            [
                (x_hbm, both.at[:, :, 0]),
                (g_hbm, both.at[:, :, 1]),
                (gain_hbm, gain_ref),
                (wqkv_hbm, wqkv),
                (wout_hbm, wout),
            ]
        )
    ]
    for load in loads:
        load.start()
    stores = []

    def store(src, dst):
        stores.append(pltpu.make_async_copy(src, dst, lsem.at[len(loads) + len(stores)]))
        stores[-1].start()

    net = Net(ssem, rsem)
    mp = net.mp

    for load in loads[:3]:
        load.wait()
    bring = net.start(net.frames_to_patches(both, mid, xb, gb))
    gain[...] = gain_ref[...].astype(F32)
    net.finish(bring)
    gather_x = net.start(net.gather(xb))
    net.until(gather_x, 2)
    gather_g = net.start(net.gather(gb))
    net.finish(gather_x)

    def square(m, total):
        block = flat(xb[m]).astype(F32)
        return total + block * block

    squares = lax.fori_loop(0, 16, square, jnp.zeros((256, HEAD), F32))
    mean = jnp.sum(squares, axis=-1, keepdims=True) * (1.0 / 2048)
    inv[...] = jnp.broadcast_to(lax.rsqrt(mean + EPS), (256, HEAD))

    def normalise(m, carry):
        block = flat(xb[m]).astype(F32) * inv[...] * gain[pl.ds(m, 1), :]
        norm[:, pl.ds(pl.multiple_of(m * 128, 128), 128)] = block.astype(BF)
        return carry

    lax.fori_loop(0, 16, normalise, 0, unroll=2)
    net.passed(0.25)
    for load in loads[3:]:
        load.wait()
    qkv[...] = mm(norm[...], wqkv[...]).astype(BF)
    net.passed(0.46)

    scale = HEAD ** (-0.5)
    rows = lax.broadcasted_iota(jnp.int32, (256, 256), 0)
    cols = lax.broadcasted_iota(jnp.int32, (256, 256), 1)
    keep = (((rows - cols) & 15) == 0) & (cols <= rows)
    queries, keys, values = (qkv[:, pl.ds(i * 128, 128)] for i in range(3))
    scores = jnp.where(keep, mm_nt(queries, keys) * scale, -1e30)
    expo = jnp.exp(scores - jnp.max(scores, axis=-1, keepdims=True))
    soft = expo / jnp.sum(expo, axis=-1, keepdims=True)
    probs[...] = soft
    attended = mm(soft.astype(BF), values)
    att[...] = attended.astype(BF)
    net.passed(0.19)

    def out_term(i, carry):
        wide = mm(att[...], wout[:, pl.ds(pl.multiple_of(i * 256, 256), 256)]).astype(BF)
        term1[2 * i] = wide[:, :128]
        term1[2 * i + 1] = wide[:, 128:]
        return carry

    lax.fori_loop(0, 8, out_term, 0, unroll=4)
    net.passed(0.05)

    att_t[...] = jnp.transpose(attended).astype(BF)
    probs_t[...] = jnp.transpose(soft).astype(BF)

    def turn(m, carry):
        at = pl.multiple_of(m * 128, 128)
        block = norm[:, pl.ds(at, 128)].astype(F32)
        norm_t[pl.ds(at, 128), :] = jnp.transpose(block).astype(BF)
        return carry

    lax.fori_loop(0, 16, turn, 0, unroll=2)
    net.finish(gather_g)

    def pair_of(i):
        return jnp.concatenate([flat(gb[2 * i]), flat(gb[2 * i + 1])], axis=1)

    sum_1 = net.start(net.scatter_sum(term1, rb1, zs1, zb1))
    for i in range(8):
        wide = mm(att_t[...], pair_of(i)).astype(BF)
        wo[i // 2, 2 * (i % 2)] = wide[:, :128]
        wo[i // 2, 2 * (i % 2) + 1] = wide[:, 128:]

    def out_stored(total):
        dwo[...] = total
        store(dwo, dwo_out)

    net.start(net.out_sum(wo, txo, pxo, mxo, sxo, tzo, pzo, mzo, out_stored))
    total = jnp.zeros((256, HEAD), F32)
    for i in range(8):
        total += mm_nt(pair_of(i), wout[:, pl.ds(i * 256, 256)])
    gheads[...] = total.astype(BF)
    net.passed(2.87)

    def pieces(wg, first, count):
        def piece(q):
            for half in range(2):
                at = q * 4 + half * 2
                rows = norm_t[pl.ds(pl.multiple_of(at * 128, 256), 256), :]
                tall = mm(rows, dqkv[:, pl.ds(first * 128, count * 128)]).astype(BF)
                for k in range(2):
                    for c in range(count):
                        wg[q, 2 * half + k, c] = tall[k * 128 : k * 128 + 128, c * 128 : c * 128 + 128]

        return piece

    def stored(res, first, count):
        def store_all():
            for c in range(count):
                store(res.at[:, :, c], dwqkv_out.at[:, :, :, pl.ds((first + c) * 128, 128)])

        return store_all

    dqkv[:, pl.ds(256, 128)] = mm(probs_t[...], gheads[...]).astype(BF)
    net.start(
        net.weight_sum(pieces(wv, 2, 1), wv, txv, pxv, mxv, sxv, tzv, pzv, mzv, resv, stored(resv, 2, 1))
    )
    net.passed(0.26)
    dprobs = mm_nt(gheads[...], qkv[:, pl.ds(256, 128)]).astype(BF).astype(F32)
    soft = probs[...]
    delta = jnp.sum(soft * dprobs, axis=-1, keepdims=True)
    dscores = soft * (dprobs - delta) * scale
    high = dscores.astype(BF)
    low = (dscores - high.astype(F32)).astype(BF)
    keys = qkv[:, pl.ds(128, 128)]
    dqkv[:, pl.ds(0, 128)] = (mm(high, keys) + mm(low, keys)).astype(BF)
    turned = jnp.transpose(dscores)
    high = turned.astype(BF)
    low = (turned - high.astype(F32)).astype(BF)
    queries = qkv[:, pl.ds(0, 128)]
    dqkv[:, pl.ds(128, 128)] = (mm(high, queries) + mm(low, queries)).astype(BF)

    net.start(net.weight_sum(pieces(wg, 0, 2), wg, tx, px, mx, sx, tz, pz, mz, res, stored(res, 0, 2)))
    net.passed(1.18)

    def norm_term(i, total):
        tall = wqkv[pl.ds(pl.multiple_of(i * 256, 256), 256), :]
        wide = mm_nt(dqkv[...], tall).astype(BF)
        for half in (0, 1):
            part = wide[:, half * 128 : half * 128 + 128]
            term2[2 * i + half, pl.ds(0, 256)] = part
            total += gain[pl.ds(2 * i + half, 1), :] * part.astype(F32) * flat(
                xb[2 * i + half]
            ).astype(F32)
        return total

    inner = lax.fori_loop(0, 8, norm_term, jnp.zeros((256, HEAD), F32), unroll=2)
    inner = jnp.sum(jnp.transpose(inner), axis=0, keepdims=True)
    at_row = lax.broadcasted_iota(jnp.int32, (16, HEAD), 0)
    inner = jnp.where(at_row == 0, inner[:, :128], jnp.where(at_row == 1, inner[:, 128:], 0.0))
    high = inner.astype(BF)
    low = (inner - high.astype(F32)).astype(BF)
    for m in range(16):
        term2[m, pl.ds(256, 16)] = high
        term2[m, pl.ds(272, 16)] = low

    def token_flow():
        yield from net.scatter_sum(term2, rb2, zs2, zb2)
        total = net.received(term2, rb2, 1, net.zl) + zb2[...].astype(F32)
        while any(item[1] is sum_1 for item in net.flows):
            yield 217.08
        summed = net.received(term1, rb1, 1, net.zl) + zb1[...].astype(F32)
        local = flat(xb[mp]).astype(F32)
        done_both[:, :, 0] = (local + summed).astype(BF).reshape(4, 4, 16, HEAD)
        rows = total[256:272] + total[272:288]
        rows = jnp.concatenate(
            [jnp.transpose(jnp.broadcast_to(rows[k : k + 1], (HEAD, HEAD))) for k in (0, 1)], axis=0
        )
        scale_own = inv[...]
        grad = (
            flat(gb[mp]).astype(F32)
            + scale_own * gain[pl.ds(mp, 1), :] * total[:256]
            - local * (scale_own * scale_own * scale_own) * rows * (1.0 / 2048)
        )
        done_both[:, :, 1] = grad.astype(BF).reshape(4, 4, 16, HEAD)
        yield 0.82
        yield from net.patches_to_frames(done_both, back_both)
        store(back_both.at[:, :, 0], lo_out)
        store(back_both.at[:, :, 1], ig_out)

    net.start(token_flow())
    net.finish()
    net.close()
    for copy in stores:
        copy.wait()


def bf(*shape):
    return pltpu.VMEM(shape, BF)


def f32(*shape):
    return pltpu.VMEM(shape, F32)


def shards(frames_in, norm_gain, w_qkv, w_out, cotangent):
    hbm = pl.BlockSpec(memory_space=pltpu.HBM)
    block = (4, 4, 16, HEAD)
    scratch = [
        bf(4, 4, 2, 16, HEAD), bf(4, 4, 2, 16, HEAD), bf(16, HEAD),
        bf(16, *block), bf(16, *block),
        bf(2048, 384), bf(HEAD, 2048),
        f32(16, HEAD), f32(256, HEAD),
        bf(256, 2048), bf(2048, 256),
        bf(256, 384), bf(256, HEAD), bf(HEAD, 256),
        f32(256, 256), bf(256, 256),
        bf(256, HEAD), bf(256, 384),
        bf(16, 256, HEAD), bf(14, 256, HEAD), bf(256, HEAD), bf(256, HEAD),
        bf(16, ROWS, HEAD), bf(14, ROWS, HEAD), bf(ROWS, HEAD), bf(ROWS, HEAD),
        bf(4, 4, 1, HEAD, HEAD),
        bf(4, 1, HEAD, HEAD), bf(4, 1, HEAD, HEAD), bf(4, 1, HEAD, HEAD),
        bf(2, 1, HEAD, HEAD),
        bf(1, HEAD, HEAD), bf(1, HEAD, HEAD), bf(1, HEAD, HEAD),
        bf(4, 4, 1, HEAD, HEAD),
        bf(4, 4, 2, HEAD, HEAD),
        bf(4, 2, HEAD, HEAD), bf(4, 2, HEAD, HEAD), bf(4, 2, HEAD, HEAD),
        bf(2, 2, HEAD, HEAD),
        bf(2, HEAD, HEAD), bf(2, HEAD, HEAD), bf(2, HEAD, HEAD),
        bf(4, 4, HEAD, HEAD), bf(4, HEAD, HEAD), bf(4, HEAD, HEAD),
        bf(4, HEAD, HEAD), bf(4, HEAD, HEAD),
        bf(HEAD, HEAD), bf(HEAD, HEAD), bf(HEAD, HEAD),
        bf(4, 4, 2, HEAD, HEAD), bf(HEAD, HEAD),
        bf(4, 4, 2, 16, HEAD), bf(4, 4, 2, 16, HEAD),
        pltpu.SemaphoreType.DMA((COPIES,)),
        pltpu.SemaphoreType.DMA((COPIES,)),
        pltpu.SemaphoreType.DMA((11,)),
    ]
    layer_out, input_grad, qkv_weight_grad, out_weight_grad = pl.pallas_call(
        kernel,
        out_shape=(
            jax.ShapeDtypeStruct(block, BF),
            jax.ShapeDtypeStruct(block, BF),
            jax.ShapeDtypeStruct((4, 4, HEAD, 384), BF),
            jax.ShapeDtypeStruct((HEAD, HEAD), BF),
        ),
        in_specs=[hbm] * 5,
        out_specs=(hbm,) * 4,
        scratch_shapes=scratch,
        compiler_params=pltpu.CompilerParams(
            collective_id=0, has_side_effects=True, vmem_limit_bytes=55040 * 1024
        ),
        name="sublayer",
    )(frames_in.reshape(block), norm_gain.reshape(16, HEAD), w_qkv, w_out, cotangent.reshape(block))
    return (
        layer_out.reshape(1, 256, HEAD),
        input_grad.reshape(1, 256, HEAD),
        qkv_weight_grad.reshape(2048, 384),
        out_weight_grad,
    )


def solution(mesh):
    return jax.shard_map(
        shards,
        mesh=mesh,
        in_specs=(
            P(("clip", "seq"), None, "mp"),
            P(),
            P(None, "mp"),
            P("mp", None),
            P(("clip", "seq"), None, "mp"),
        ),
        out_specs=(
            P(("clip", "seq"), None, "mp"),
            P(("clip", "seq"), None, "mp"),
            P("clip", "mp"),
            P(("clip", "mp"), "seq"),
        ),
        check_vma=False,
    )
```

```python
import jax
import jax.numpy as jnp
from jax import lax
from jax.experimental import pallas as pl
from jax.experimental.pallas import tpu as pltpu
from jax.sharding import PartitionSpec as P

HEAD = 128
EPS = 1e-05
BF = jnp.bfloat16
F32 = jnp.float32
MESH = pl.DeviceIdType.MESH
COPIES = 159
ROWS = 288
SCALE = HEAD ** (-0.5)
NT = (((1,), (1,)), ((), ()))


def mm(a, b):
    return jnp.dot(a, b, preferred_element_type=F32)


def mm_nt(a, b):
    return lax.dot_general(a, b, NT, preferred_element_type=F32)


def mm_tn(a, b):
    return lax.dot_general(a, b, (((0,), (0,)), ((), ())), preferred_element_type=F32)


class Net:
    def __init__(self, ssem, rsem):
        self.ssem, self.rsem, self.started, self.flows, self.clock, self.steps = ssem, rsem, [], [], 0.0, {}
        self.drained = 0
        clip, seq, mp = lax.axis_index("clip"), lax.axis_index("seq"), lax.axis_index("mp")
        self.clip, self.seq, self.mp = clip, seq, mp
        self.zh, self.x = seq // 4, seq & 3
        self.zl, self.y = mp // 8, mp & 7
        self.e = 1 - 2 * clip
        self.zp = 1 - self.zl
        self.dev_pair = (clip, seq, self.zp * 8 + self.y)
        barrier = pltpu.get_barrier_semaphore()
        peers = [(clip, (seq + s) & 15, mp) for s in range(1, 16)]
        peers += [self.dev_y(self.y_at(s)) for s in (1, -1, 2, -2)] + [self.dev_pair]
        for peer in peers:
            pl.semaphore_signal(barrier, inc=1, device_id=peer, device_id_type=MESH)
        pl.semaphore_wait(barrier, len(peers))

    def x_at(self, step):
        return (self.x + step) & 3

    def z_at(self, step):
        return (self.zh + step) & 3

    def y_at(self, step):
        return (self.y + step) & 7

    def dev_x(self, to):
        return (self.clip, self.zh * 4 + to, self.mp)

    def dev_z(self, to):
        return (self.clip, to * 4 + self.x, self.mp)

    def dev_y(self, to):
        return (self.clip, self.seq, self.zl * 8 + to)

    def send(self, src, dst, device):
        at = len(self.started)
        copy = pltpu.make_async_remote_copy(
            src_ref=src,
            dst_ref=dst,
            send_sem=self.ssem.at[at],
            recv_sem=self.rsem.at[at],
            device_id=device,
            device_id_type=MESH,
        )
        copy.start()
        self.started.append(copy)
        return copy

    def start(self, flow):
        self.flows.append([self.clock + next(flow), flow])
        return flow

    def step(self, item=None):
        item = item or min(self.flows, key=lambda entry: entry[0])
        for _ in range(2):
            if self.drained < len(self.started) - 24:
                self.started[self.drained].wait_send()
                self.drained += 1
        self.clock = max(self.clock, item[0])
        wait = next(item[1], None)
        self.steps[id(item[1])] = self.steps.get(id(item[1]), 0) + 1
        if wait is None:
            self.flows.remove(item)
        else:
            item[0] = self.clock + wait

    def until(self, flow, steps):
        while self.steps.get(id(flow), 0) < steps:
            self.step(next(entry for entry in self.flows if entry[1] is flow))

    def finish(self, flow=None):
        while any(flow is None or item[1] is flow for item in self.flows):
            self.step()

    def passed(self, time):
        target = self.clock + time
        while self.flows and min(item[0] for item in self.flows) <= target:
            self.step()
        self.clock = target

    def close(self):
        for copy in self.started[self.drained :]:
            copy.wait_send()

    def frames_to_patches(self, src, mid, xb, gb):
        zh, x, mp = self.zh, self.x, self.mp
        sent = []
        for s in range(1, 16):
            to = (self.seq + s) & 15
            there = (self.clip, to, mp)
            sent.append(self.send(src.at[to // 4, to & 3], mid.at[zh, x], there))
        mid[zh, x] = src[zh, x]
        yield 17.64
        for copy in sent:
            copy.wait_recv()
        xb[mp] = mid[:, :, 0]
        gb[mp] = mid[:, :, 1]

    def patches_to_frames(self, src, dst):
        sent = []
        for s in range(1, 16):
            to = (self.seq + s) & 15
            there = self.dev_far(to)
            sent.append(self.send(src.at[to // 4, to & 3], dst.at[self.zh, self.x], there))
        dst[self.zh, self.x] = src[self.zh, self.x]
        yield 252.77
        for copy in sent:
            copy.wait_recv()

    def dev_far(self, seq):
        return (self.clip, seq, self.mp)

    def gather(self, buf):
        def pass_on(block, device):
            return self.send(buf.at[block], buf.at[block], device)

        ahead, back = self.dev_y(self.y_at(self.e)), self.dev_y(self.y_at(-self.e))

        def own(step):
            return self.zl * 8 + self.y_at(step)

        def other(step):
            return self.zp * 8 + self.y_at(step)

        a = pass_on(self.mp, ahead)
        b = pass_on(self.mp, back)
        pair = [pass_on(self.mp, self.dev_pair)]
        yield 3.61
        a.wait_recv()
        a = pass_on(own(-self.e), ahead)
        yield 2.72
        b.wait_recv()
        b = pass_on(own(self.e), back)
        yield 1.5
        pair[0].wait_recv()
        c = pass_on(other(0), ahead)
        d = pass_on(other(0), back)
        yield 1.22
        a.wait_recv()
        a = pass_on(own(-2 * self.e), ahead)
        yield 1.94
        b.wait_recv()
        b = pass_on(own(2 * self.e), back)
        pair.append(pass_on(own(2 * self.e), self.dev_pair))
        yield 0.58
        c.wait_recv()
        c = pass_on(other(-self.e), ahead)
        yield 1.11
        d.wait_recv()
        yield 0.74
        a.wait_recv()
        a = pass_on(own(-3 * self.e), ahead)
        pair.append(pass_on(own(-3 * self.e), self.dev_pair))
        yield 1.18
        b.wait_recv()
        pair.append(pass_on(own(3 * self.e), self.dev_pair))
        yield 1.54
        c.wait_recv()
        yield 0.05
        a.wait_recv()
        pair.append(pass_on(own(-4 * self.e), self.dev_pair))
        for copy in pair[1:]:
            yield 1.54
            copy.wait_recv()

    def scatter_sum(self, term, rb, zs, zb):
        planes = (self.zp, self.zl)
        ways = ((self.e, 4), (-self.e, 3))
        order = [(i, j) for i in (0, 1) for j in (0, 1)]

        def slot(i, j, k):
            return i * 7 + j * 4 + k - 1

        sent = {}
        for i, j in order:
            way, steps = ways[j]
            dest = planes[i] * 8 + self.y_at(steps * way)
            sent[i, j] = self.send(term.at[dest], rb.at[slot(i, j, 1)], self.dev_y(self.y_at(way)))
        last = None
        for k in (1, 2, 3, 4):
            for i, j in order:
                way, steps = ways[j]
                if k > steps:
                    continue
                yield 5.6 if (i, j) == (0, 0) else 0.99
                sent[i, j].wait_recv()
                here = rb.at[slot(i, j, k)]
                if k < steps:
                    dest = planes[i] * 8 + self.y_at((steps - k) * way)
                    fold(here, here[...].astype(F32) + term[dest].astype(F32))
                    after = rb.at[slot(i, j, k + 1)]
                    sent[i, j] = self.send(here, after, self.dev_y(self.y_at(way)))
                elif k == 4 and i == 0:
                    fold(zs, self.received(term, rb, 0, self.zp))
                    last = self.send(zs, zb, self.dev_pair)
        yield 25.36
        last.wait_recv()

    def received(self, term, rb, i, plane):
        return (
            term[plane * 8 + self.y].astype(F32)
            + rb[7 * i + 3].astype(F32)
            + rb[7 * i + 6].astype(F32)
        )

    def weight_sum(self, piece, wg, tx, px, mx, sx, tz, pz, mz, res, done):
        zh, x, e = self.zh, self.x, self.e
        xp, xm, zm = self.x_at(e), self.x_at(-e), self.z_at(-e)
        ahead, back = self.dev_x(xp), self.dev_x(xm)
        z_ahead, z_back = self.dev_z(self.z_at(e)), self.dev_z(zm)
        q = (self.z_at(2), self.z_at(e), zm, zh)
        far, plain, near = [], [], []

        def here(i):
            return wg[q[i], x].astype(F32) + px[i].astype(F32) + mx[i].astype(F32)

        for i in range(4):
            piece(q[i])
            far.append(self.send(wg.at[q[i], self.x_at(2)], tx.at[i], ahead))
            plain.append(self.send(wg.at[q[i], xm], px.at[i], back))
            if i < 3:
                yield 0.73
        for i in range(4):
            yield 1.97
            far[i].wait_recv()
            tx[i] = (tx[i].astype(F32) + wg[q[i], xp].astype(F32)).astype(BF)
            near.append(self.send(tx.at[i], mx.at[i], ahead))
        yield 1.86
        plain[0].wait_recv()
        near[0].wait_recv()
        sx[0] = here(0).astype(BF)
        z_far = self.send(sx.at[0], tz, z_ahead)
        for i in (1, 2):
            yield 1.82
            plain[i].wait_recv()
            near[i].wait_recv()
        sx[1] = here(2).astype(BF)
        z_plain = self.send(sx.at[1], pz, z_back)
        yield 1.67
        z_far.wait_recv()
        tz[...] = (tz[...].astype(F32) + here(1)).astype(BF)
        z_near = self.send(tz, mz, z_ahead)
        yield 2.93
        plain[3].wait_recv()
        near[3].wait_recv()
        yield 3.8
        z_plain.wait_recv()
        z_near.wait_recv()
        total = (here(3) + pz[...].astype(F32) + mz[...].astype(F32)).astype(BF)
        res[zh, x] = total

        def pass_on(at, column, device):
            return self.send(res.at[at, column], res.at[at, column], device)

        up, down = pass_on(zh, x, z_ahead), pass_on(zh, x, z_back)
        first, second, third = [pass_on(zh, x, ahead)], [pass_on(zh, x, back)], []
        yield 8.72
        up.wait_recv()
        up = pass_on(zm, x, z_ahead)
        first.append(pass_on(zm, x, ahead))
        second.append(pass_on(zm, x, back))
        yield 0.05
        down.wait_recv()
        first.append(pass_on(q[1], x, ahead))
        second.append(pass_on(q[1], x, back))
        yield 8.0
        first[0].wait_recv()
        third.append(pass_on(zh, xm, ahead))
        yield 61.54
        up.wait_recv()
        first.append(pass_on(q[0], x, ahead))
        second.append(pass_on(q[0], x, back))
        for i, at in ((1, zm), (2, q[1]), (3, q[0])):
            yield 3.2
            first[i].wait_recv()
            third.append(pass_on(at, xm, ahead))
        for copy in second + third:
            yield 46.94
            copy.wait_recv()
        done()

    def out_sum(self, wo, tx, px, mx, sx, tz, pz, mz, done):
        zh, x, e = self.zh, self.x, self.e
        xp, xm, zm = self.x_at(e), self.x_at(-e), self.z_at(-e)
        ahead, back = self.dev_x(xp), self.dev_x(xm)
        z_ahead, z_back = self.dev_z(self.z_at(e)), self.dev_z(zm)
        far = self.send(wo.at[:, self.x_at(2)], tx, ahead)
        plain = self.send(wo.at[:, xm], px, back)
        yield 20.24
        far.wait_recv()
        tx[...] = (tx[...].astype(F32) + wo[:, xp].astype(F32)).astype(BF)
        near = self.send(tx, mx, ahead)
        yield 23.11
        plain.wait_recv()
        near.wait_recv()
        sx[...] = (wo[:, x].astype(F32) + px[...].astype(F32) + mx[...].astype(F32)).astype(BF)
        z_far = self.send(sx.at[self.z_at(2)], tz, z_ahead)
        z_plain = self.send(sx.at[zm], pz, z_back)
        yield 70.29
        z_far.wait_recv()
        tz[...] = (tz[...].astype(F32) + sx[self.z_at(e)].astype(F32)).astype(BF)
        z_near = self.send(tz, mz, z_ahead)
        yield 3.59
        z_plain.wait_recv()
        z_near.wait_recv()
        total = wo[zh, x].astype(F32) + px[zh].astype(F32) + mx[zh].astype(F32)
        done((total + pz[...].astype(F32) + mz[...].astype(F32)).astype(BF))


def flat(block):
    return block.reshape(256, HEAD)


def fold(ref, total):
    ref[pl.ds(0, 256)] = total[:256].astype(BF)
    if total.shape[0] == ROWS:
        inner = total[256:272] + total[272:288]
        high = inner.astype(BF)
        ref[pl.ds(256, 16)] = high
        ref[pl.ds(272, 16)] = (inner - high.astype(F32)).astype(BF)


def kernel(
    x_hbm, gain_hbm, wqkv_hbm, wout_hbm, g_hbm,
    lo_out, ig_out, dwqkv_out, dwo_out,
    both, mid, gain_ref, xb, gb, wqkv, wout, gain, inv, norm, norm_t, qkv, att, att_t,
    probs, probs_t, gheads, dqkv, term1, rb1, zs1, zb1, term2, rb2, zs2, zb2,
    wv, txv, pxv, mxv, sxv, tzv, pzv, mzv, resv,
    wg, tx, px, mx, sx, tz, pz, mz, wo, txo, pxo, mxo, sxo, tzo, pzo, mzo, res, dwo, done_both, back_both,
    ssem, rsem, lsem,
):
    loads = [
        pltpu.make_async_copy(src, dst, lsem.at[at])
        for at, (src, dst) in enumerate(
            [
                (x_hbm, both.at[:, :, 0]),
                (g_hbm, both.at[:, :, 1]),
                (gain_hbm, gain_ref),
                (wqkv_hbm, wqkv),
                (wout_hbm, wout),
            ]
        )
    ]
    for load in loads:
        load.start()
    stores = []

    def store(src, dst):
        stores.append(pltpu.make_async_copy(src, dst, lsem.at[len(loads) + len(stores)]))
        stores[-1].start()

    net = Net(ssem, rsem)
    mp = net.mp

    for load in loads[:3]:
        load.wait()
    bring = net.start(net.frames_to_patches(both, mid, xb, gb))
    gain[...] = gain_ref[...].astype(F32)
    net.finish(bring)
    gather_x = net.start(net.gather(xb))
    net.until(gather_x, 2)
    gather_g = net.start(net.gather(gb))
    net.finish(gather_x)

    def square(m, total):
        block = flat(xb[m]).astype(F32)
        return total + block * block

    squares = lax.fori_loop(0, 16, square, jnp.zeros((256, HEAD), F32))
    mean = jnp.sum(squares, axis=-1, keepdims=True) * (1.0 / 2048)
    inv[...] = jnp.broadcast_to(lax.rsqrt(mean + EPS), (256, HEAD))

    def normalise(m, carry):
        block = flat(xb[m]).astype(F32) * inv[...] * gain[pl.ds(m, 1), :]
        norm[:, pl.ds(pl.multiple_of(m * 128, 128), 128)] = block.astype(BF)
        return carry

    lax.fori_loop(0, 16, normalise, 0, unroll=2)
    net.passed(1.02)
    for load in loads[3:]:
        load.wait()
    qkv[...] = mm(norm[...], wqkv[...]).astype(BF)
    net.passed(0.71)

    scale = HEAD ** (-0.5)
    rows = lax.broadcasted_iota(jnp.int32, (256, 256), 0)
    cols = lax.broadcasted_iota(jnp.int32, (256, 256), 1)
    keep = (((rows - cols) & 15) == 0) & (cols <= rows)
    queries, keys, values = (qkv[:, pl.ds(i * 128, 128)] for i in range(3))
    scores = jnp.where(keep, mm_nt(queries, keys) * scale, -1e30)
    expo = jnp.exp(scores - jnp.max(scores, axis=-1, keepdims=True))
    soft = expo / jnp.sum(expo, axis=-1, keepdims=True)
    probs[...] = soft
    attended = mm(soft.astype(BF), values)
    att[...] = attended.astype(BF)
    net.passed(1.4)

    def out_term(i, carry):
        wide = mm(att[...], wout[:, pl.ds(pl.multiple_of(i * 256, 256), 256)]).astype(BF)
        term1[2 * i] = wide[:, :128]
        term1[2 * i + 1] = wide[:, 128:]
        return carry

    lax.fori_loop(0, 8, out_term, 0, unroll=4)
    net.passed(0.57)

    att_t[...] = jnp.transpose(attended).astype(BF)
    probs_t[...] = jnp.transpose(soft).astype(BF)

    def turn(m, carry):
        at = pl.multiple_of(m * 128, 128)
        block = norm[:, pl.ds(at, 128)].astype(F32)
        norm_t[pl.ds(at, 128), :] = jnp.transpose(block).astype(BF)
        return carry

    lax.fori_loop(0, 16, turn, 0, unroll=2)
    net.finish(gather_g)

    def pair_of(i):
        return jnp.concatenate([flat(gb[2 * i]), flat(gb[2 * i + 1])], axis=1)

    sum_1 = net.start(net.scatter_sum(term1, rb1, zs1, zb1))
    for i in range(8):
        wide = mm(att_t[...], pair_of(i)).astype(BF)
        wo[i // 2, 2 * (i % 2)] = wide[:, :128]
        wo[i // 2, 2 * (i % 2) + 1] = wide[:, 128:]

    def out_stored(total):
        dwo[...] = total
        store(dwo, dwo_out)

    net.start(net.out_sum(wo, txo, pxo, mxo, sxo, tzo, pzo, mzo, out_stored))
    total = jnp.zeros((256, HEAD), F32)
    for i in range(8):
        total += mm_nt(pair_of(i), wout[:, pl.ds(i * 256, 256)])
    gheads[...] = total.astype(BF)
    net.passed(2.87)

    def pieces(wg, first, count):
        def piece(q):
            for half in range(2):
                at = q * 4 + half * 2
                rows = norm_t[pl.ds(pl.multiple_of(at * 128, 256), 256), :]
                tall = mm(rows, dqkv[:, pl.ds(first * 128, count * 128)]).astype(BF)
                for k in range(2):
                    for c in range(count):
                        wg[q, 2 * half + k, c] = tall[k * 128 : k * 128 + 128, c * 128 : c * 128 + 128]

        return piece

    def stored(res, first, count):
        def store_all():
            for c in range(count):
                store(res.at[:, :, c], dwqkv_out.at[:, :, :, pl.ds((first + c) * 128, 128)])

        return store_all

    dqkv[:, pl.ds(256, 128)] = mm(probs_t[...], gheads[...]).astype(BF)
    net.start(
        net.weight_sum(pieces(wv, 2, 1), wv, txv, pxv, mxv, sxv, tzv, pzv, mzv, resv, stored(resv, 2, 1))
    )
    net.passed(0.26)
    dprobs = mm_nt(gheads[...], qkv[:, pl.ds(256, 128)]).astype(BF).astype(F32)
    soft = probs[...]
    delta = jnp.sum(soft * dprobs, axis=-1, keepdims=True)
    dscores = soft * (dprobs - delta) * scale
    high = dscores.astype(BF)
    low = (dscores - high.astype(F32)).astype(BF)
    keys = qkv[:, pl.ds(128, 128)]
    dqkv[:, pl.ds(0, 128)] = (mm(high, keys) + mm(low, keys)).astype(BF)
    turned = jnp.transpose(dscores)
    high = turned.astype(BF)
    low = (turned - high.astype(F32)).astype(BF)
    queries = qkv[:, pl.ds(0, 128)]
    dqkv[:, pl.ds(128, 128)] = (mm(high, queries) + mm(low, queries)).astype(BF)

    net.start(net.weight_sum(pieces(wg, 0, 2), wg, tx, px, mx, sx, tz, pz, mz, res, stored(res, 0, 2)))
    net.passed(1.18)

    def norm_term(i, total):
        tall = wqkv[pl.ds(pl.multiple_of(i * 256, 256), 256), :]
        wide = mm_nt(dqkv[...], tall).astype(BF)
        for half in (0, 1):
            part = wide[:, half * 128 : half * 128 + 128]
            term2[2 * i + half, pl.ds(0, 256)] = part
            total += gain[pl.ds(2 * i + half, 1), :] * part.astype(F32) * flat(
                xb[2 * i + half]
            ).astype(F32)
        return total

    inner = lax.fori_loop(0, 8, norm_term, jnp.zeros((256, HEAD), F32), unroll=2)
    inner = jnp.sum(jnp.transpose(inner), axis=0, keepdims=True)
    at_row = lax.broadcasted_iota(jnp.int32, (16, HEAD), 0)
    inner = jnp.where(at_row == 0, inner[:, :128], jnp.where(at_row == 1, inner[:, 128:], 0.0))
    high = inner.astype(BF)
    low = (inner - high.astype(F32)).astype(BF)
    for m in range(16):
        term2[m, pl.ds(256, 16)] = high
        term2[m, pl.ds(272, 16)] = low

    def token_flow():
        yield from net.scatter_sum(term2, rb2, zs2, zb2)
        total = net.received(term2, rb2, 1, net.zl) + zb2[...].astype(F32)
        while any(item[1] is sum_1 for item in net.flows):
            yield 6.77
        summed = net.received(term1, rb1, 1, net.zl) + zb1[...].astype(F32)
        local = flat(xb[mp]).astype(F32)
        done_both[:, :, 0] = (local + summed).astype(BF).reshape(4, 4, 16, HEAD)
        rows = total[256:272] + total[272:288]
        rows = jnp.concatenate(
            [jnp.transpose(jnp.broadcast_to(rows[k : k + 1], (HEAD, HEAD))) for k in (0, 1)], axis=0
        )
        scale_own = inv[...]
        grad = (
            flat(gb[mp]).astype(F32)
            + scale_own * gain[pl.ds(mp, 1), :] * total[:256]
            - local * (scale_own * scale_own * scale_own) * rows * (1.0 / 2048)
        )
        done_both[:, :, 1] = grad.astype(BF).reshape(4, 4, 16, HEAD)
        yield 20.22
        yield from net.patches_to_frames(done_both, back_both)
        store(back_both.at[:, :, 0], lo_out)
        store(back_both.at[:, :, 1], ig_out)

    net.start(token_flow())
    net.finish()
    net.close()
    for copy in stores:
        copy.wait()


def bf(*shape):
    return pltpu.VMEM(shape, BF)


def f32(*shape):
    return pltpu.VMEM(shape, F32)


def shards(frames_in, norm_gain, w_qkv, w_out, cotangent):
    hbm = pl.BlockSpec(memory_space=pltpu.HBM)
    block = (4, 4, 16, HEAD)
    scratch = [
        bf(4, 4, 2, 16, HEAD), bf(4, 4, 2, 16, HEAD), bf(16, HEAD),
        bf(16, *block), bf(16, *block),
        bf(2048, 384), bf(HEAD, 2048),
        f32(16, HEAD), f32(256, HEAD),
        bf(256, 2048), bf(2048, 256),
        bf(256, 384), bf(256, HEAD), bf(HEAD, 256),
        f32(256, 256), bf(256, 256),
        bf(256, HEAD), bf(256, 384),
        bf(16, 256, HEAD), bf(14, 256, HEAD), bf(256, HEAD), bf(256, HEAD),
        bf(16, ROWS, HEAD), bf(14, ROWS, HEAD), bf(ROWS, HEAD), bf(ROWS, HEAD),
        bf(4, 4, 1, HEAD, HEAD),
        bf(4, 1, HEAD, HEAD), bf(4, 1, HEAD, HEAD), bf(4, 1, HEAD, HEAD),
        bf(2, 1, HEAD, HEAD),
        bf(1, HEAD, HEAD), bf(1, HEAD, HEAD), bf(1, HEAD, HEAD),
        bf(4, 4, 1, HEAD, HEAD),
        bf(4, 4, 2, HEAD, HEAD),
        bf(4, 2, HEAD, HEAD), bf(4, 2, HEAD, HEAD), bf(4, 2, HEAD, HEAD),
        bf(2, 2, HEAD, HEAD),
        bf(2, HEAD, HEAD), bf(2, HEAD, HEAD), bf(2, HEAD, HEAD),
        bf(4, 4, HEAD, HEAD), bf(4, HEAD, HEAD), bf(4, HEAD, HEAD),
        bf(4, HEAD, HEAD), bf(4, HEAD, HEAD),
        bf(HEAD, HEAD), bf(HEAD, HEAD), bf(HEAD, HEAD),
        bf(4, 4, 2, HEAD, HEAD), bf(HEAD, HEAD),
        bf(4, 4, 2, 16, HEAD), bf(4, 4, 2, 16, HEAD),
        pltpu.SemaphoreType.DMA((COPIES,)),
        pltpu.SemaphoreType.DMA((COPIES,)),
        pltpu.SemaphoreType.DMA((11,)),
    ]
    layer_out, input_grad, qkv_weight_grad, out_weight_grad = pl.pallas_call(
        kernel,
        out_shape=(
            jax.ShapeDtypeStruct(block, BF),
            jax.ShapeDtypeStruct(block, BF),
            jax.ShapeDtypeStruct((4, 4, HEAD, 384), BF),
            jax.ShapeDtypeStruct((HEAD, HEAD), BF),
        ),
        in_specs=[hbm] * 5,
        out_specs=(hbm,) * 4,
        scratch_shapes=scratch,
        compiler_params=pltpu.CompilerParams(
            collective_id=0, has_side_effects=True, vmem_limit_bytes=55040 * 1024
        ),
        name="sublayer",
    )(frames_in.reshape(block), norm_gain.reshape(16, HEAD), w_qkv, w_out, cotangent.reshape(block))
    return (
        layer_out.reshape(1, 256, HEAD),
        input_grad.reshape(1, 256, HEAD),
        qkv_weight_grad.reshape(2048, 384),
        out_weight_grad,
    )


def solution(mesh):
    return jax.shard_map(
        shards,
        mesh=mesh,
        in_specs=(
            P(("clip", "seq"), None, "mp"),
            P(),
            P(None, "mp"),
            P("mp", None),
            P(("clip", "seq"), None, "mp"),
        ),
        out_specs=(
            P(("clip", "seq"), None, "mp"),
            P(("clip", "seq"), None, "mp"),
            P("clip", "mp"),
            P(("clip", "mp"), "seq"),
        ),
        check_vma=False,
    )
```
